32 devices in a mesh: pack: 4 (over y, x), blk: 4 (over z), head: 2 (over core).
Axes of the slice: x: 2, y: 2, z: 4, core: 2. Of those that a mesh axis runs over, the one named last changes fastest.
Arguments:
- tokens_full: bfloat16 [4, 3072, 1152], P('pack', 'blk'), may hold values from -6 to 6
- condition: bfloat16 [4, 9, 1152], P('pack'), may hold values from -6 to 6
- kept_index: int32 [4, 1536], P('pack', 'blk'), may hold values from 0 to 3071, as said below
- segment_ids: int32 [4, 1536], P('pack'), may hold values from 0 to 8, as said below
- cotangent: bfloat16 [4, 3072, 1152], P('pack', 'blk'), may hold values from -6 to 6
- qkv_weight: bfloat16 [1152, 3, 1152], P(None, None, 'head'), may hold values from -0.1875 to 0.1875
- query_value_bias: bfloat16 [2, 1152], P(None, 'head'), may hold values from -3 to 3
- output_weight: bfloat16 [1152, 1152], P('head'), may hold values from -2 to 2
- output_bias: bfloat16 [1152], replicated, may hold values from -2 to 2
- hidden_weight: bfloat16 [1152, 4608], P(None, 'head'), may hold values from -0.1875 to 0.1875
- hidden_bias: bfloat16 [4608], P('head'), may hold values from -2 to 2
- down_weight: bfloat16 [4608, 1152], P('head'), may hold values from -0.09375 to 0.09375
- down_bias: bfloat16 [1152], replicated, may hold values from -2 to 2
- modulation_weight: bfloat16 [1152, 6, 1152], P(None, None, 'head'), may hold values from -0.1875 to 0.1875
- modulation_bias: bfloat16 [6, 1152], P(None, 'head'), may hold values from -2 to 2
Outputs:
- block_output: bfloat16 [4, 3072, 1152], P('pack', 'blk')
- tokens_grad: bfloat16 [4, 3072, 1152], P('pack', 'blk')
- condition_grad: float32 [4, 9, 1152], P('pack')
- qkv_weight_grad: float32 [1152, 3, 1152], P('blk', None, 'head')
- query_value_bias_grad: float32 [2, 1152], P(None, 'head')
- output_weight_grad: float32 [1152, 1152], P('head', 'blk')
- output_bias_grad: float32 [1152], replicated
- hidden_weight_grad: float32 [1152, 4608], P('blk', 'head')
- hidden_bias_grad: float32 [4608], P('head')
- down_weight_grad: float32 [4608, 1152], P('head', 'blk')
- down_bias_grad: float32 [1152], replicated
- modulation_weight_grad: float32 [1152, 6, 1152], P('blk', None, 'head')
- modulation_bias_grad: float32 [6, 1152], P(None, 'head')
The draws below stay inside these ranges and needn't reach their ends.
Inputs may be any that keep to these rules, and one draw needn't show every extreme that they name: `kept_index`: within a pack, the kept tokens j * 384 to (j + 1) * 384 - 1 hold distinct positions from 2 * j * 384 to 2 * (j + 1) * 384 - 1; the first block keeps position 0 and the last keeps the pack's last position. `segment_ids`: each pack is 1 latents of 512 kept tokens and the others of 128, in an order drawn per pack; the ids never fall along a pack, and each id from 0 to 8 names one latent.
All inputs are finite; a program needn't handle non-finite values.
Results may differ from the reference program's by a relative error of at most 0.015.
The reference program's roundings to bfloat16 on the way count: a program that leaves them out, or rounds other values in their place, can miss the bound.
Values may be sent and summed in bfloat16 or wider, within the bound.
No kernel may reach another device: no remote copies, remote signals or barrier semaphores. Data moves between devices by JAX's collectives and lax.ppermute only.
A program may use at most 320 MiB of HBM per device.

```python
import math
import jax
import jax.numpy as jnp
from jax import lax

HEADS = 16
HEAD_DIM = 72
D = 1152
FF = 4608
LONG_LEN = 512
SHORT_LEN = 128
TOK_DEV = 384
SEQ = 1536
LONGS = 1
SEGS = 9
FULL = 3072
PACKS = 4
N_BLK = 4


def draw_kept_index(key, part):
    key = jax.random.fold_in(key, 11)
    total_blocks = PACKS * N_BLK
    keys_all = jax.random.split(key, total_blocks)
    places = jnp.arange(total_blocks, dtype=jnp.int32) % N_BLK

    def choose(one_key, block_place):
        key_drawn, key_rest = jax.random.split(one_key)
        drawn_pick = jax.random.permutation(key_drawn, 2 * TOK_DEV)[:TOK_DEV].astype(jnp.int32)
        rest_pick = jax.random.permutation(key_rest, 2 * TOK_DEV - 1)[:TOK_DEV - 1].astype(jnp.int32)
        last_pick = jnp.concatenate([rest_pick, jnp.full((1,), 2 * TOK_DEV - 1, jnp.int32)])
        first_pick = jnp.concatenate([jnp.zeros((1,), jnp.int32), rest_pick + 1])
        picked = jnp.where(block_place == 0, first_pick, jnp.where(block_place == N_BLK - 1, last_pick, drawn_pick))
        return picked + block_place * (2 * TOK_DEV)
    chosen = jax.vmap(choose)(keys_all, places)
    return chosen.reshape(PACKS, SEQ).astype(jnp.int32)


def draw_segment_ids(key, part):
    key = jax.random.fold_in(key, 23)
    pack_keys = jax.random.split(key, PACKS)

    def one_pack(pack_key):
        order = jax.random.permutation(pack_key, SEGS).astype(jnp.int32)
        lengths = jnp.where(order < LONGS, LONG_LEN, SHORT_LEN).astype(jnp.int32)
        ends = jnp.cumsum(lengths).astype(jnp.int32)
        position = jnp.arange(SEQ, dtype=jnp.int32)
        return jnp.sum((position[:, None] >= ends[None, :]).astype(jnp.int32), axis=1).astype(jnp.int32)
    return jax.vmap(one_pack)(pack_keys).astype(jnp.int32)


def block_levels(key, dims, cuts, least, largest):
    loudness = 1.0
    for dim, parts in cuts:
        draws = jax.random.uniform(jax.random.fold_in(jax.random.fold_in(key, 6), dim), (parts,), jnp.float32, least / len(cuts), largest / len(cuts))
        loudness = loudness * jnp.repeat(jnp.exp(draws), dims[dim] // parts).reshape((-1,) + (1,) * (len(dims) - 1 - dim))
    return loudness


def normal_values(stream_key, dims, scale, limit, cuts=(), kind=jnp.bfloat16):
    gain = block_levels(stream_key, dims, cuts, -0.22, 0.18) if cuts else 1.0
    array = jax.random.normal(stream_key, dims, jnp.float32) * scale * gain
    return jnp.minimum(jnp.maximum(array, -limit), limit).astype(kind)


def setup_inputs(seed: int = 0) -> dict:
    keys = jax.random.split(jax.random.key(seed), 16)
    return {
        "tokens_full": normal_values(keys[0], (PACKS, FULL, D), 1.0, 6.0, ((0, 4), (1, 4))),
        "condition": normal_values(keys[1], (PACKS, SEGS, D), 1.0, 6.0, ((0, 4),)),
        "kept_index": draw_kept_index(jax.random.fold_in(keys[15], 71), 0),
        "segment_ids": draw_segment_ids(jax.random.fold_in(keys[15], 71), 0),
        "cotangent": normal_values(keys[4], (PACKS, FULL, D), 1.0, 6.0, ((0, 4), (1, 4))),
        "qkv_weight": normal_values(keys[5], (D, 3, D), D ** -0.5, 0.1875, ((2, 2),)),
        "query_value_bias": normal_values(keys[6], (2, D), 0.5, 3.0, ((1, 2),)),
        "output_weight": normal_values(keys[7], (D, D), (max(D * 4 // LONG_LEN, 1)) ** -0.5, 2.0, ((0, 2),)),
        "output_bias": normal_values(keys[8], (D,), 0.3, 2.0),
        "hidden_weight": normal_values(keys[9], (D, FF), D ** -0.5, 0.1875, ((1, 2),)),
        "hidden_bias": normal_values(keys[10], (FF,), 0.3, 2.0, ((0, 2),)),
        "down_weight": normal_values(keys[11], (FF, D), FF ** -0.5, 0.09375, ((0, 2),)),
        "down_bias": normal_values(keys[12], (D,), 0.3, 2.0),
        "modulation_weight": normal_values(keys[13], (D, 6, D), D ** -0.5, 0.1875, ((2, 2),)),
        "modulation_bias": normal_values(keys[14], (6, D), 0.3, 2.0, ((1, 2),)),
    }


EPSILON = 1e-06
MASKED = -1e+30
HIGHEST = lax.Precision.HIGHEST

@jax.custom_vjp
def low(v):
    return lax.optimization_barrier(v.astype(jnp.bfloat16)).astype(jnp.float32)

@jax.custom_vjp
def low_back(v):
    return v

def low_keep(v):
    return (low(v), None)

def low_pass(kept, grad):
    return (grad,)

def back_keep(v):
    return (v, None)

def back_low(kept, grad):
    return (low(grad),)
low.defvjp(low_keep, low_pass)
low_back.defvjp(back_keep, back_low)

def product(operand_a, operand_b):
    return jnp.dot(operand_a, operand_b, precision=HIGHEST)

def layer_norm(values):
    center = values - lax.optimization_barrier(jnp.mean(values, axis=-1, keepdims=True))
    spread = lax.optimization_barrier(jnp.mean(center * center, axis=-1, keepdims=True))
    return center * lax.rsqrt(spread + EPSILON)

def attend(queries, key_rows, value_rows, segments):
    length = queries.shape[0]
    block_rows = math.gcd(length, 512)
    factor = 1.0 / math.sqrt(HEAD_DIM)

    def one_block(start):
        query_block = lax.dynamic_slice_in_dim(queries, start, block_rows, 0)
        seg_block = lax.dynamic_slice_in_dim(segments, start, block_rows, 0)
        scores = jnp.einsum('qhd,khd->hqk', query_block, key_rows, precision=HIGHEST) * factor
        scores = low_back(scores)
        same_doc = seg_block[:, None] == segments[None, :]
        scores = jnp.where(same_doc[None], scores, MASKED)
        weights = jax.nn.softmax(scores, axis=-1)
        return jnp.einsum('hqk,khd->qhd', low(weights), value_rows, precision=HIGHEST)
    starts = jnp.arange(length // block_rows, dtype=jnp.int32) * block_rows
    stacked = lax.map(jax.checkpoint(one_block), starts)
    return stacked.reshape(length, HEADS * HEAD_DIM)

def block_forward(kept_rows, condition, params, segments):
    qkv_weight, query_value_bias, output_weight, output_bias, hidden_weight, hidden_bias, down_weight, down_bias, modulation_weight, modulation_bias = params
    model_width = kept_rows.shape[1]
    active = low(jax.nn.silu(condition))
    modulation = product(active, modulation_weight.reshape(model_width, 6 * model_width)) + modulation_bias.reshape(6 * model_width)
    per_token = modulation[segments]
    pieces = [per_token[:, number * model_width:(number + 1) * model_width] for number in range(6)]
    shift_one, scale_one, gate_one, shift_two, scale_two, gate_two = pieces
    normed_one = layer_norm(kept_rows)
    hidden_one = low(normed_one * (1.0 + scale_one) + shift_one)
    queries = low(low_back(product(hidden_one, qkv_weight[:, 0]) + query_value_bias[0]))
    key_rows = low(low_back(product(hidden_one, qkv_weight[:, 1])))
    value_rows = low(low_back(product(hidden_one, qkv_weight[:, 2]) + query_value_bias[1]))
    head_shape = (kept_rows.shape[0], HEADS, HEAD_DIM)
    attended = attend(queries.reshape(head_shape), key_rows.reshape(head_shape), value_rows.reshape(head_shape), segments)
    attended = low(low_back(attended))
    branch_one = low_back(product(attended, output_weight) + output_bias)
    middle = kept_rows + gate_one * branch_one
    normed_two = layer_norm(middle)
    hidden_two = low(normed_two * (1.0 + scale_two) + shift_two)
    pre_act = low_back(product(hidden_two, hidden_weight) + hidden_bias)
    gelu_out = low(jax.nn.gelu(pre_act, approximate=True))
    branch_two = low_back(product(gelu_out, down_weight) + down_bias)
    return middle + gate_two * branch_two

def reference(tokens_full, condition, kept_index, segment_ids, cotangent, qkv_weight, query_value_bias, output_weight, output_bias, hidden_weight, hidden_bias, down_weight, down_bias, modulation_weight, modulation_bias):
    params = tuple((weight.astype(jnp.float32) for weight in (qkv_weight, query_value_bias, output_weight, output_bias, hidden_weight, hidden_bias, down_weight, down_bias, modulation_weight, modulation_bias)))

    def one_pack(totals, inputs):
        full_rows, cond_rows, kept_pos, segments, cot_rows = inputs
        kept_rows = full_rows.astype(jnp.float32)[kept_pos]

        def forward(kept_vals, cond_vals, weights):
            return block_forward(kept_vals, cond_vals, weights, segments)
        result_rows, pullback = jax.vjp(forward, kept_rows, cond_rows.astype(jnp.float32), params)
        kept_grad, cond_grad, param_grads = pullback(cot_rows.astype(jnp.float32)[kept_pos])
        out_rows = full_rows.at[kept_pos].set(result_rows.astype(jnp.bfloat16))
        grad_rows = cot_rows.at[kept_pos].set(kept_grad.astype(jnp.bfloat16))
        totals = jax.tree.map(jnp.add, totals, param_grads)
        return (totals, (out_rows, grad_rows, cond_grad))
    initial = jax.tree.map(jnp.zeros_like, params)
    totals, (block_output, tokens_grad, condition_grad) = lax.scan(one_pack, initial, (tokens_full, condition, kept_index, segment_ids, cotangent))
    return (block_output, tokens_grad, condition_grad, totals[0], totals[1], totals[2], totals[3], totals[4], totals[5], totals[6], totals[7], totals[8], totals[9])
```

```python
import math

import jax
import jax.numpy as jnp
from jax import lax
from jax.sharding import PartitionSpec as P

HEAD_DIM = 72
SHORT = 128
LANES = 128
EPSILON = 1e-06
MASKED = -1e30


def bf_dot(operand_a, operand_b):
    return jnp.dot(operand_a, operand_b, preferred_element_type=jnp.float32)


def exact_rows(picker, rows):
    high = rows.astype(jnp.bfloat16)
    low = (rows - high.astype(jnp.float32)).astype(jnp.bfloat16)
    return bf_dot(picker, high) + bf_dot(picker, low)


def layer_norm(values):
    center = values - jnp.mean(values, axis=-1, keepdims=True)
    spread = jnp.mean(center * center, axis=-1, keepdims=True)
    inverse = lax.rsqrt(spread + EPSILON)
    return (center * inverse, inverse)


def norm_back(upstream, normed, inverse):
    mean_grad = jnp.mean(upstream, axis=-1, keepdims=True)
    mean_cross = jnp.mean(upstream * normed, axis=-1, keepdims=True)
    return inverse * (upstream - mean_grad - normed * mean_cross)


def xor_permute(block, axis, bits):
    return lax.ppermute(block, axis, [(i, i ^ bits) for i in range(lax.axis_size(axis))])


def swap(block):
    return xor_permute(block, "head", 1)


def head_sum(block):
    return block.astype(jnp.float32) + swap(block).astype(jnp.float32)


def move(block, step):
    count = lax.axis_size("blk")
    pairs = [(i, i + step) for i in range(count) if 0 <= i + step < count]
    return lax.ppermute(block, "blk", pairs)


def axis_bits(axis, turned):
    bits = [1 << b for b in range((lax.axis_size(axis) - 1).bit_length())]
    return bits[::-1] if turned else bits


def gather_xor(block, axis, turned=False):
    held = {0: block}
    for bits in axis_bits(axis, turned):
        for entry in list(held):
            held[entry ^ bits] = xor_permute(held[entry], axis, bits)
    return [held[entry] for entry in range(lax.axis_size(axis))]


def in_order(entries, axis):
    order = jnp.arange(len(entries), dtype=jnp.int32) ^ lax.axis_index(axis)
    return jnp.take(jnp.stack(entries), order, axis=0)


def windows(width, parts):
    tiles = width // LANES
    size = -(-tiles // parts)
    return [LANES * (q * (tiles - size) // (parts - 1)) for q in range(parts)], size * LANES


def trade_columns(block, axis):
    count = lax.axis_size(axis)
    starts, size = windows(block.shape[1], count)
    table = jnp.asarray(starts, jnp.int32)
    me = lax.axis_index(axis)
    out = []
    for entry in range(count):
        piece = lax.dynamic_slice_in_dim(block, table[me ^ entry], size, 1)
        out.append(xor_permute(piece, axis, entry) if entry else piece)
    return out


def trade_pieces(pieces, axis):
    me = lax.axis_index(axis)
    out = []
    for entry in range(lax.axis_size(axis)):
        piece = lax.dynamic_index_in_dim(pieces, me ^ entry, 0, keepdims=False)
        out.append(xor_permute(piece, axis, entry) if entry else piece)
    return out


def gather_rows(block, turned):
    width = block.shape[1]
    half = -(-width // (2 * LANES)) * LANES
    core = lax.axis_index("head")
    own = jnp.where(core == 0, block[:, :half], block[:, width - half :])
    own = jnp.concatenate(gather_xor(own, "pack", turned), axis=0)
    other = swap(own)
    low = jnp.where(core == 0, own, other)
    high = jnp.where(core == 0, other, own)
    return jnp.concatenate([low, high[:, 2 * half - width :]], axis=1)


def sum_blk(term):
    count = lax.axis_size("blk")
    me = lax.axis_index("blk")
    rows = term.shape[0] // count
    total = lax.dynamic_slice_in_dim(term, me * rows, rows, 0)
    for step in range(1, count):
        target = lax.rem(me + step, count)
        piece = lax.dynamic_slice_in_dim(term, target * rows, rows, 0).astype(jnp.bfloat16)
        pairs = [(i, (i + step) % count) for i in range(count)]
        total = total + lax.ppermute(piece, "blk", pairs).astype(jnp.float32)
    return total


def weight_grad(rows, columns, turned):
    term = lax.dot_general(
        rows,
        jnp.concatenate(columns, axis=0),
        (((0,), (0,)), ((), ())),
        preferred_element_type=jnp.float32,
    )
    share = sum_blk(term).astype(jnp.bfloat16)
    return in_order(gather_xor(share, "pack", turned), "pack")


def join_windows(stacked, width):
    starts, size = windows(width, stacked.shape[0])
    parts = []
    for q, start in enumerate(starts):
        end = starts[q + 1] if q + 1 < len(starts) else width
        parts.append(stacked[q, :, : end - start])
    return jnp.concatenate(parts, axis=1).astype(jnp.float32)


def split_heads(matrix):
    return matrix.reshape(matrix.shape[0], -1, HEAD_DIM).transpose(1, 0, 2)


def join_heads(stacked):
    return stacked.transpose(1, 0, 2).reshape(stacked.shape[1], -1)


def local(
    tokens_full,
    condition,
    kept_index,
    segment_ids,
    cotangent,
    qkv_weight,
    query_value_bias,
    output_weight,
    output_bias,
    hidden_weight,
    hidden_bias,
    down_weight,
    down_bias,
    modulation_weight,
    modulation_bias,
):
    width = tokens_full.shape[2]
    own_width = qkv_weight.shape[2]
    hidden = hidden_weight.shape[1]
    count = kept_index.shape[1]
    seg_count = condition.shape[1]
    places = count // SHORT
    longs = (segment_ids.shape[1] - SHORT * seg_count) // (3 * SHORT)
    packs = lax.axis_size("pack")
    blocks = lax.axis_size("blk")
    factor = 1.0 / math.sqrt(HEAD_DIM)
    blk = lax.axis_index("blk")
    core = lax.axis_index("head")

    local_index = kept_index[0] - blk * (2 * count)
    full_rows = tokens_full[0]
    cot_rows = cotangent[0]
    picker = (
        local_index[:, None] == jnp.arange(full_rows.shape[0], dtype=jnp.int32)[None, :]
    ).astype(jnp.bfloat16)
    kept_low = bf_dot(picker, full_rows).astype(jnp.bfloat16)
    kept_rows = kept_low.astype(jnp.float32)
    upstream = bf_dot(picker, cot_rows)

    segments = segment_ids[0]
    outside = jnp.full((count,), -1, jnp.int32)
    padded = jnp.concatenate([outside, segments, outside])
    near = lax.dynamic_slice_in_dim(padded, blk * count, 3 * count, 0)
    own_segments = near[count : 2 * count]
    reaches_low = near[count - 1] == near[count]

    def beside(block):
        low, high = move(block, 1), move(block, -1)
        if longs == 1:
            return jnp.where(reaches_low, low, high)
        return jnp.concatenate([low, high], axis=0)

    if longs == 1:
        beside_segments = jnp.where(reaches_low, near[:count], near[2 * count :])
    else:
        beside_segments = jnp.concatenate([near[:count], near[2 * count :]])
    all_segments = jnp.concatenate([own_segments, beside_segments])
    half = count // 2
    own_half = lax.dynamic_slice_in_dim(kept_low, core * half, half, 0)
    near_half = beside(own_half)
    other_half = swap(near_half)
    first = jnp.where(core == 0, near_half, other_half).reshape(-1, half, width)
    second = jnp.where(core == 0, other_half, near_half).reshape(-1, half, width)
    near_rows = jnp.concatenate([first, second], axis=1).reshape(-1, width).astype(jnp.float32)

    cond_rows = condition[0].astype(jnp.float32)
    active = jax.nn.silu(cond_rows).astype(jnp.bfloat16)
    mod_own = (
        jnp.einsum("sd,dgf->sgf", active, modulation_weight, preferred_element_type=jnp.float32)
        + modulation_bias.astype(jnp.float32)[None]
    )
    mod_other = swap(mod_own)
    mod_all = jnp.concatenate(
        [jnp.where(core == 0, mod_own, mod_other), jnp.where(core == 0, mod_other, mod_own)],
        axis=2,
    )
    place_segments = jnp.maximum(all_segments[::SHORT], 0)
    mod_places = jnp.take(mod_all, place_segments, axis=0)

    def per_token(number, first, last):
        picked = mod_places[first:last, number]
        return jnp.broadcast_to(picked[:, None], (last - first, SHORT, width)).reshape(-1, width)

    shift_one, scale_one, gate_one, shift_two, scale_two, gate_two = [
        per_token(number, 0, places) for number in range(6)
    ]
    down_in = (gate_two * upstream).astype(jnp.bfloat16)
    down_in_all = gather_rows(down_in, False)

    normed_one, inverse_one = layer_norm(kept_rows)
    hidden_one = (normed_one * (1.0 + scale_one) + shift_one).astype(jnp.bfloat16)
    hidden_one_all = gather_rows(hidden_one, True)
    near_hidden = (
        layer_norm(near_rows)[0] * (1.0 + per_token(1, places, mod_places.shape[0]))
        + per_token(0, places, mod_places.shape[0])
    ).astype(jnp.bfloat16)

    flat_qkv = qkv_weight.reshape(width, 3 * own_width)
    bias_rows = query_value_bias.astype(jnp.float32)
    projected = bf_dot(jnp.concatenate([hidden_one, near_hidden], axis=0), flat_qkv)
    queries = (projected[:, :own_width] + bias_rows[0]).astype(jnp.bfloat16)
    key_rows = projected[:, own_width : 2 * own_width].astype(jnp.bfloat16)
    value_rows = (projected[:, 2 * own_width :] + bias_rows[1]).astype(jnp.bfloat16)
    head_rows = (split_heads(queries), split_heads(key_rows), split_heads(value_rows))
    same_doc = all_segments[:, None] == all_segments[None, :]

    def probs_of(query_head, key_head, mask):
        scores = jnp.where(mask, bf_dot(query_head, key_head.T) * factor, MASKED)
        exponent = jnp.exp(scores - jnp.max(scores, axis=1, keepdims=True))
        return exponent / jnp.sum(exponent, axis=1, keepdims=True)

    def head_forward(operands):
        query_head, key_head, value_head = operands
        probs = probs_of(query_head[:count], key_head, same_doc[:count])
        return bf_dot(probs.astype(jnp.bfloat16), value_head)

    attended = join_heads(lax.map(head_forward, head_rows)).astype(jnp.bfloat16)
    packs_width = own_width // packs
    attended_split = attended.reshape(count, packs, packs_width).transpose(1, 0, 2)
    attended_all = trade_pieces(attended_split, "pack")

    branch_one = head_sum(bf_dot(attended, output_weight)) + output_bias.astype(jnp.float32)
    middle = kept_rows + gate_one * branch_one
    normed_two, inverse_two = layer_norm(middle)
    hidden_two = (normed_two * (1.0 + scale_two) + shift_two).astype(jnp.bfloat16)
    hidden_two_all = gather_rows(hidden_two, False)
    pre_act = bf_dot(hidden_two, hidden_weight) + hidden_bias.astype(jnp.float32)
    gelu_out, gelu_back = jax.vjp(lambda v: jax.nn.gelu(v, approximate=True), pre_act)
    gelu_out = gelu_out.astype(jnp.bfloat16)
    gelu_all = trade_columns(gelu_out, "pack")
    gelu_grad = bf_dot(down_in, down_weight.T)
    pre_grad = gelu_back(gelu_grad)[0].astype(jnp.bfloat16)
    pre_all = trade_columns(pre_grad, "pack")
    hidden_two_grad = head_sum(bf_dot(pre_grad, hidden_weight.T))
    branch_two = head_sum(bf_dot(gelu_out, down_weight).astype(jnp.bfloat16))
    branch_two = branch_two + down_bias.astype(jnp.float32)
    result_rows = middle + gate_two * branch_two

    def put_rows(base, rows):
        spread = lax.dot_general(
            picker, rows, (((0,), (0,)), ((), ())), preferred_element_type=jnp.float32
        )
        kept = jnp.max(picker, axis=0)[:, None] > 0
        return jnp.where(kept, spread.astype(jnp.bfloat16), base)[None]

    block_output = put_rows(full_rows, result_rows.astype(jnp.bfloat16))

    middle_grad = upstream + norm_back(hidden_two_grad * (1.0 + scale_two), normed_two, inverse_two)
    branch_grad = (gate_one * middle_grad).astype(jnp.bfloat16)
    attended_grad = bf_dot(branch_grad, output_weight.T).astype(jnp.bfloat16)
    near_grad = beside(attended_grad)
    branch_grad_all = gather_rows(branch_grad, True)

    def head_backward(operands):
        query_head, key_head, value_head, grad_head = operands
        probs = probs_of(query_head, key_head, same_doc)
        weight_grad_ = bf_dot(grad_head, value_head.T)
        row_dot = jnp.sum(probs * weight_grad_, axis=1, keepdims=True)
        score_grad = (probs * (weight_grad_ - row_dot)).astype(jnp.bfloat16)
        query_grad = bf_dot(score_grad[:count], key_head) * factor
        key_grad = bf_dot(score_grad[:, :count].T, query_head) * factor
        value_grad = bf_dot(probs[:, :count].astype(jnp.bfloat16).T, grad_head)
        return (query_grad, key_grad, value_grad)

    grads = lax.map(
        head_backward,
        (*head_rows, split_heads(jnp.concatenate([attended_grad, near_grad], axis=0))),
    )
    grads = [join_heads(grad).astype(jnp.bfloat16) for grad in grads]
    qkv_grad = jnp.concatenate(grads, axis=1)
    qkv_split = (
        jnp.stack(grads, axis=1)
        .reshape(count, 3, packs, packs_width)
        .transpose(2, 0, 1, 3)
        .reshape(packs, count, 3 * packs_width)
    )
    qkv_all = trade_pieces(qkv_split, "pack")
    hidden_one_grad = head_sum(bf_dot(qkv_grad, flat_qkv.T).astype(jnp.bfloat16))
    input_grad = middle_grad + norm_back(
        hidden_one_grad * (1.0 + scale_one), normed_one, inverse_one
    )
    tokens_grad = put_rows(cot_rows, input_grad.astype(jnp.bfloat16))

    down_stack = weight_grad(down_in_all, gelu_all, False)
    down_weight_grad = join_windows(down_stack, hidden).T
    hidden_stack = weight_grad(hidden_two_all, pre_all, True)
    hidden_weight_grad = join_windows(hidden_stack, hidden)
    output_stack = weight_grad(branch_grad_all, attended_all, False)
    output_weight_grad = (
        output_stack.transpose(0, 2, 1).reshape(own_width, -1).astype(jnp.float32)
    )
    qkv_stack = weight_grad(hidden_one_all, qkv_all, True)
    qkv_weight_grad = (
        qkv_stack.reshape(packs, -1, 3, packs_width)
        .transpose(1, 2, 0, 3)
        .reshape(-1, 3, own_width)
        .astype(jnp.float32)
    )

    terms = jnp.stack(
        [
            hidden_one_grad,
            hidden_one_grad * normed_one,
            middle_grad * branch_one,
            hidden_two_grad,
            hidden_two_grad * normed_two,
            upstream * branch_two,
        ],
        axis=1,
    )
    place_sums = jnp.sum(terms.reshape(places, SHORT, 6, width), axis=1)
    own_sums = lax.dynamic_slice_in_dim(place_sums, core * own_width, own_width, 2)
    grad_sums = jnp.sum(qkv_grad.astype(jnp.float32), axis=0)
    bias_terms = (
        grad_sums[:own_width],
        grad_sums[2 * own_width :],
        jnp.sum(branch_grad.astype(jnp.float32), axis=0),
        jnp.sum(pre_grad.astype(jnp.float32), axis=0),
        jnp.sum(down_in.astype(jnp.float32), axis=0),
    )
    place_active = jnp.take(active, place_segments[:places], axis=0).astype(jnp.float32)
    sent = jnp.concatenate([own_sums.reshape(-1), place_active.reshape(-1), *bias_terms])
    sent = sent.reshape(-1, LANES)
    by_blk = in_order(gather_xor(sent, "blk"), "blk")
    by_pack = in_order(gather_xor(by_blk, "pack"), "pack")
    received = by_pack.reshape(packs * blocks, -1)
    cut = places * 6 * own_width
    sums_all = received[:, :cut].reshape(-1, 6 * own_width)
    active_all = received[:, cut : cut + places * width].reshape(-1, width)
    biases = jnp.sum(received[:, cut + places * width :], axis=0)
    modulation_bias_grad = jnp.sum(sums_all, axis=0).reshape(6, own_width)
    rows = width // blocks
    active_share = lax.dynamic_slice_in_dim(active_all, blk * rows, rows, 1)
    sums_high = sums_all.astype(jnp.bfloat16)
    sums_low = (sums_all - sums_high.astype(jnp.float32)).astype(jnp.bfloat16)
    active_share = active_share.astype(jnp.bfloat16).T
    modulation_weight_grad = (
        bf_dot(active_share, sums_high) + bf_dot(active_share, sums_low)
    ).reshape(rows, 6, own_width)

    pack_sums = lax.dynamic_index_in_dim(
        sums_all.reshape(packs, -1, 6 * own_width), lax.axis_index("pack"), 0, keepdims=False
    )
    of_segment = (
        jnp.arange(seg_count, dtype=jnp.int32)[:, None] == segments[None, ::SHORT]
    ).astype(jnp.bfloat16)
    mod_grad = exact_rows(of_segment, pack_sums)
    mod_high = mod_grad.astype(jnp.bfloat16)
    mod_low = (mod_grad - mod_high.astype(jnp.float32)).astype(jnp.bfloat16)
    cond_terms = jnp.einsum(
        "sgf,dgf->sd",
        jnp.concatenate([mod_high, mod_low], axis=0).reshape(-1, 6, own_width),
        modulation_weight,
        preferred_element_type=jnp.float32,
    )
    cond_total = head_sum(cond_terms[:seg_count] + cond_terms[seg_count:])
    squashed = jax.nn.sigmoid(cond_rows)
    condition_grad = (cond_total * squashed * (1.0 + cond_rows * (1.0 - squashed)))[None]

    ends = [own_width, 2 * own_width, 2 * own_width + width, 2 * own_width + width + hidden]
    value_bias = jnp.stack([biases[: ends[0]], biases[ends[0] : ends[1]]])
    return (
        block_output,
        tokens_grad,
        condition_grad,
        qkv_weight_grad,
        value_bias,
        output_weight_grad,
        biases[ends[1] : ends[2]],
        hidden_weight_grad,
        biases[ends[2] : ends[3]],
        down_weight_grad,
        biases[ends[3] :],
        modulation_weight_grad,
        modulation_bias_grad,
    )


def solution(mesh):
    in_specs = (
        P("pack", "blk", None),
        P("pack", None, None),
        P("pack", "blk"),
        P("pack", None),
        P("pack", "blk", None),
        P(None, None, "head"),
        P(None, "head"),
        P("head", None),
        P(),
        P(None, "head"),
        P("head"),
        P("head", None),
        P(),
        P(None, None, "head"),
        P(None, "head"),
    )
    out_specs = (
        P("pack", "blk", None),
        P("pack", "blk", None),
        P("pack", None, None),
        P("blk", None, "head"),
        P(None, "head"),
        P("head", "blk"),
        P(),
        P("blk", "head"),
        P("head"),
        P("head", "blk"),
        P(),
        P("blk", None, "head"),
        P(None, "head"),
    )
    return jax.shard_map(local, mesh=mesh, in_specs=in_specs, out_specs=out_specs, check_vma=False)
```

```python
import math

import jax
import jax.numpy as jnp
from jax import lax
from jax.experimental import pallas as pl
from jax.experimental.pallas import tpu as pltpu
from jax.sharding import PartitionSpec as P

HEAD_DIM = 72
SHORT = 128
LONG = 4 * SHORT
LANES = 128
EPSILON = 1e-06
FACTOR = 1.0 / math.sqrt(HEAD_DIM)
FACTOR_LOG2 = FACTOR * math.log2(math.e)
GELU_SLOPE = math.sqrt(2.0 / math.pi)
GELU_CUBE = 0.044715
F32 = jnp.float32
BF16 = jnp.bfloat16
ROWS_BY_ROWS = (((1,), (1,)), ((), ()))
COLUMNS_BY_COLUMNS = (((0,), (0,)), ((), ()))
VMEM = pl.BlockSpec(memory_space=pltpu.VMEM)
SMEM = pl.BlockSpec(memory_space=pltpu.SMEM)


def bf_dot(operand_a, operand_b):
    return jnp.dot(operand_a, operand_b, preferred_element_type=F32)


def dot_by(dims, operand_a, operand_b):
    return lax.dot_general(operand_a, operand_b, dims, preferred_element_type=F32)


def array(shape, kind):
    return jax.ShapeDtypeStruct(shape, kind)


def kernel_call(body, name, outs, args, flops, grid=(), in_specs=None, out_specs=None, scratch=()):
    moved = sum(math.prod(a.shape) * a.dtype.itemsize for a in (*args, *outs))
    return pl.pallas_call(
        body,
        name=name,
        out_shape=tuple(outs),
        grid=grid,
        in_specs=in_specs or [VMEM] * len(args),
        out_specs=out_specs or (VMEM,) * len(outs),
        scratch_shapes=scratch,
        compiler_params=pltpu.CompilerParams(vmem_limit_bytes=48 << 20),
        cost_estimate=pl.CostEstimate(
            flops=int(flops), bytes_accessed=int(moved), transcendentals=0
        ),
    )(*args)


def aligned(index, to=LANES):
    return pl.multiple_of(index, to)


def layer_norm(values):
    center = values - jnp.mean(values, axis=-1, keepdims=True)
    spread = jnp.mean(center * center, axis=-1, keepdims=True)
    inverse = lax.rsqrt(spread + EPSILON)
    return (center * inverse, inverse)


def norm_back(upstream, normed, inverse):
    mean_grad = jnp.mean(upstream, axis=-1, keepdims=True)
    mean_cross = jnp.mean(upstream * normed, axis=-1, keepdims=True)
    return inverse * (upstream - mean_grad - normed * mean_cross)


def gelu_pair(value):
    square = value * value
    bent = jnp.tanh(GELU_SLOPE * (value + GELU_CUBE * (value * square)))
    half = 0.5 * (1.0 + bent)
    slope = GELU_SLOPE * (1.0 + (3.0 * GELU_CUBE) * square)
    return value * half, half + 0.5 * value * (1.0 - bent * bent) * slope


def qkv_body(rows_ref, mod_ref, weight_ref, bias_ref, hidden_ref, out_ref):
    step = pl.program_id(0)

    @pl.when(step == 0)
    def _():
        for place in range(rows_ref.shape[0] // SHORT):
            rows = pl.ds(place * SHORT, SHORT)
            normed, _ = layer_norm(rows_ref[rows].astype(F32))
            shift, scale = mod_ref[place, 0:1], mod_ref[place, 1:2]
            hidden_ref[rows] = (normed * (1.0 + scale) + shift).astype(BF16)

    out_ref[0] = (bf_dot(hidden_ref[...], weight_ref[0]) + bias_ref[0]).astype(BF16)


def project(rows, mod_places, weight, bias):
    count, width = rows.shape
    own_width = weight.shape[2]
    return kernel_call(
        qkv_body,
        "norm_qkv",
        [array((count, width), BF16), array((3, count, own_width), BF16)],
        [rows, mod_places, weight, bias],
        6 * count * width * own_width,
        grid=(3,),
        in_specs=[
            pl.BlockSpec(rows.shape, lambda i: (0, 0)),
            pl.BlockSpec(mod_places.shape, lambda i: (0, 0, 0)),
            pl.BlockSpec((1, width, own_width), lambda i: (i, 0, 0)),
            pl.BlockSpec((1, 1, own_width), lambda i: (i, 0, 0)),
        ],
        out_specs=(
            pl.BlockSpec((count, width), lambda i: (0, 0)),
            pl.BlockSpec((1, count, own_width), lambda i: (i, 0, 0)),
        ),
    )


def lay_beside(buffer, own, beside, table):
    count = own.shape[0]
    buffer[count : 2 * count] = own
    if beside.shape[0] == count:
        buffer[pl.ds(aligned(table[0], SHORT), count)] = beside
    else:
        buffer[:count] = beside[:count]
        buffer[2 * count :] = beside[count:]


def attend_body(table, own_ref, near_ref, weight_ref, attended_ref, branch_ref, *rest):
    pieces, (keys, values, turned, split) = rest[:-4], rest[-4:]
    count, own_width = own_ref.shape[1:]
    places = count // SHORT
    lay_beside(keys, own_ref[1], near_ref[1], table)
    lay_beside(values, own_ref[2], near_ref[2], table)

    def attend(place, size):
        near = pl.ds(aligned(table[3 + place] * SHORT, SHORT), size)
        rows = pl.ds(place * SHORT, SHORT)
        for head in range(own_width // HEAD_DIM):
            columns = pl.ds(head * HEAD_DIM, HEAD_DIM)
            scores = dot_by(ROWS_BY_ROWS, keys[near, columns], own_ref[0, rows, columns])
            peak = jnp.max(scores, axis=0, keepdims=True)
            exponent = jnp.exp2((scores - peak) * FACTOR_LOG2)
            total = jnp.sum(exponent, axis=0, keepdims=True)
            probs = (exponent * (1.0 / total)).astype(BF16)
            turned[columns, rows] = dot_by(COLUMNS_BY_COLUMNS, values[near, columns], probs)

    for place in range(places):
        pl.when(table[3 + places + place] == 1)(lambda: attend(place, LONG))
        pl.when(table[3 + places + place] == 0)(lambda: attend(place, SHORT))
    attended = turned[...].T.astype(BF16)
    attended_ref[...] = attended
    branch_ref[...] = bf_dot(attended, weight_ref[...])
    share = own_width // len(pieces)
    for number in range(len(pieces)):
        split[number] = attended[:, number * share : (number + 1) * share]
    for entry, piece in enumerate(pieces):
        piece[...] = split[table[3 + 2 * places + entry]]


def attend(table, own, near, weight, packs):
    _, count, own_width = own.shape
    width = weight.shape[1]
    share = own_width // packs
    outs = kernel_call(
        attend_body,
        "attend",
        [array((count, own_width), BF16), array((count, width), F32)]
        + [array((count, share), BF16)] * packs,
        [table, own, near, weight],
        2 * count * own_width * (width + 2 * LONG),
        in_specs=[SMEM, VMEM, VMEM, VMEM],
        scratch=[
            pltpu.VMEM((3 * count, own_width), BF16),
            pltpu.VMEM((3 * count, own_width), BF16),
            pltpu.VMEM((own_width, count), F32),
            pltpu.VMEM((packs, count, share), BF16),
        ],
    )
    return outs[0], outs[1], list(outs[2:])


def attend_back_body(table, own_ref, near_ref, grad_ref, near_grad_ref, weight_ref, *rest):
    hidden_grad_ref, bias_ref, pieces = rest[0], rest[1], rest[2:-3]
    held, grads, split = rest[-3:]
    count, own_width = own_ref.shape[1:]
    places = count // SHORT
    for number in range(3):
        lay_beside(held.at[number], own_ref[number], near_ref[number], table)
    lay_beside(held.at[3], grad_ref[...], near_grad_ref[...], table)

    def attend_back(first, size):
        rows = pl.ds(aligned(first * SHORT, SHORT), size)
        for head in range(own_width // HEAD_DIM):
            columns = pl.ds(head * HEAD_DIM, HEAD_DIM)
            query, key, value, grad = (held[number, rows, columns] for number in range(4))
            scores = dot_by(ROWS_BY_ROWS, key, query)
            peak = jnp.max(scores, axis=0, keepdims=True)
            exponent = jnp.exp2((scores - peak) * FACTOR_LOG2)
            probs = exponent * (1.0 / jnp.sum(exponent, axis=0, keepdims=True))
            probs_grad = dot_by(ROWS_BY_ROWS, value, grad)
            row_dot = jnp.sum(probs * probs_grad, axis=0, keepdims=True)
            score_grad = (probs * (probs_grad - row_dot)).astype(BF16)
            query_grad = dot_by(COLUMNS_BY_COLUMNS, score_grad, key) * FACTOR
            grads[0, rows, columns] = query_grad.astype(BF16)
            grads[1, rows, columns] = (bf_dot(score_grad, query) * FACTOR).astype(BF16)
            grads[2, rows, columns] = bf_dot(probs.astype(BF16), grad).astype(BF16)

    for place in range(places):
        pl.when(table[3 + places + place] == 0)(lambda: attend_back(places + place, SHORT))

    def long_latent(number, carry):
        pl.when(table[1 + number] >= 0)(lambda: attend_back(table[1 + number], LONG))
        return carry

    lax.fori_loop(0, 2, long_latent, 0)
    own_grads = [grads[number, count : 2 * count] for number in range(3)]
    total = dot_by(ROWS_BY_ROWS, own_grads[0], weight_ref[0])
    for number in range(1, 3):
        total = total + dot_by(ROWS_BY_ROWS, own_grads[number], weight_ref[number])
    hidden_grad_ref[...] = total.astype(BF16)
    for number, grad in enumerate((own_grads[0], own_grads[2])):
        bias_ref[number : number + 1] = jnp.sum(grad.astype(F32), axis=0, keepdims=True)
    share = own_width // len(pieces)
    for number in range(len(pieces)):
        for part in range(3):
            split[number, :, part * share : (part + 1) * share] = own_grads[part][
                :, number * share : (number + 1) * share
            ]
    for entry, piece in enumerate(pieces):
        piece[...] = split[table[3 + 2 * places + entry]]


def attend_back(table, own, near, grad, near_grad, weight, packs):
    _, count, own_width = own.shape
    width = weight.shape[1]
    share = 3 * own_width // packs
    outs = kernel_call(
        attend_back_body,
        "attend_back",
        [array((count, width), BF16), array((2, own_width), F32)]
        + [array((count, share), BF16)] * packs,
        [table, own, near, grad, near_grad, weight],
        6 * count * own_width * width + 10 * own_width * LONG * LONG,
        in_specs=[SMEM] + [VMEM] * 5,
        scratch=[
            pltpu.VMEM((4, 3 * count, own_width), BF16),
            pltpu.VMEM((3, 3 * count, own_width), BF16),
            pltpu.VMEM((packs, count, share), BF16),
        ],
    )
    return outs[0], outs[1], list(outs[2:])


def feed_body(packs, scalars, kept_ref, term_ref, other_ref, bias_ref, mod_ref, *rest):
    (down_in_ref, weight_ref, hidden_bias_ref, down_ref) = rest[:4]
    branch_ref, hidden_ref, share_ref, two_ref, back_ref, sums_ref = rest[4:10]
    gelu_pieces, pre_pieces = rest[10 : 10 + packs], rest[10 + packs : 10 + 2 * packs]
    gelu_rows, pre_rows, total = rest[10 + 2 * packs :]
    step = pl.program_id(0)
    size = weight_ref.shape[1]

    @pl.when(step == 0)
    def _():
        for place in range(kept_ref.shape[0] // SHORT):
            rows = pl.ds(place * SHORT, SHORT)
            branch = (term_ref[rows] + other_ref[rows]) + bias_ref[...]
            branch_ref[rows] = branch
            middle = kept_ref[rows].astype(F32) + mod_ref[place, 2:3] * branch
            normed, _ = layer_norm(middle)
            shift, scale = mod_ref[place, 3:4], mod_ref[place, 4:5]
            hidden_ref[rows] = (normed * (1.0 + scale) + shift).astype(BF16)
        total[...] = jnp.zeros_like(total)
        back_ref[...] = jnp.zeros_like(back_ref)

    weight, down = weight_ref[...], down_ref[...]
    gelu, slope = gelu_pair(bf_dot(hidden_ref[...], weight) + hidden_bias_ref[...])
    gelu = gelu.astype(BF16)
    pre_grad = (dot_by(ROWS_BY_ROWS, down_in_ref[...], down) * slope).astype(BF16)
    columns = pl.ds(aligned(step * size), size)
    gelu_rows[:, columns] = gelu
    pre_rows[:, columns] = pre_grad
    sums_ref[...] = jnp.sum(pre_grad.astype(F32), axis=0, keepdims=True)
    total[...] += bf_dot(gelu, down)
    back_ref[...] += dot_by(ROWS_BY_ROWS, pre_grad, weight)

    @pl.when(step == pl.num_programs(0) - 1)
    def _():
        two_ref[...] = total[...].astype(BF16)
        start = aligned(scalars[0] * (hidden_ref.shape[1] - share_ref.shape[1]))
        share_ref[...] = hidden_ref[:, pl.ds(start, share_ref.shape[1])]
        for entry in range(packs):
            window = pl.ds(aligned(scalars[2 + entry]), gelu_pieces[entry].shape[1])
            gelu_pieces[entry][...] = gelu_rows[:, window]
            pre_pieces[entry][...] = pre_rows[:, window]


def feed(scalars, kept, term, other, bias, mod_places, down_in, weight, hidden_bias, down, packs):
    count, width = kept.shape
    hidden = weight.shape[1]
    size = 3 * LANES
    window = windows(hidden, packs)[1]
    share = half_width(width)

    def whole(shape):
        return pl.BlockSpec(shape, lambda i: (0,) * len(shape))

    outs = [
        array((count, width), F32),
        array((count, width), BF16),
        array((count, share), BF16),
        array((count, width), BF16),
        array((count, width), F32),
        array((1, hidden), F32),
    ] + [array((count, window), BF16)] * (2 * packs)
    out_specs = [whole(out.shape) for out in outs]
    out_specs[5] = pl.BlockSpec((1, size), lambda i: (0, i))
    result = kernel_call(
        lambda *refs: feed_body(packs, *refs),
        "feed",
        outs,
        [scalars, kept, term, other, bias, mod_places, down_in, weight, hidden_bias, down],
        8 * count * width * hidden,
        grid=(hidden // size,),
        in_specs=[
            SMEM,
            *[whole(a.shape) for a in (kept, term, other, bias, mod_places, down_in)],
            pl.BlockSpec((width, size), lambda i: (0, i)),
            pl.BlockSpec((1, size), lambda i: (0, i)),
            pl.BlockSpec((size, width), lambda i: (i, 0)),
        ],
        out_specs=tuple(out_specs),
        scratch=[
            pltpu.VMEM((count, hidden), BF16),
            pltpu.VMEM((count, hidden), BF16),
            pltpu.VMEM((count, width), F32),
        ],
    )
    return *result[:6], list(result[6 : 6 + packs]), list(result[6 + packs :])


def middle_back_body(scalars, term_ref, other_ref, branch_ref, kept_ref, up_ref, mod_ref, *rest):
    weight_ref, middle_grad_ref, branch_grad_ref, share_ref, attended_ref, sums_ref, bias_ref = rest
    hidden_grad = term_ref[...] + other_ref[...]
    branch = branch_ref[...]
    gate = mod_ref[0, 2:3]
    normed, inverse = layer_norm(kept_ref[...].astype(F32) + gate * branch)
    middle_grad = up_ref[...].astype(F32) + norm_back(
        hidden_grad * (1.0 + mod_ref[0, 4:5]), normed, inverse
    )
    middle_grad_ref[...] = middle_grad
    branch_grad = (gate * middle_grad).astype(BF16)
    branch_grad_ref[...] = branch_grad
    start = aligned(scalars[0] * (branch_grad_ref.shape[1] - share_ref.shape[1]))
    share_ref[...] = branch_grad_ref[:, pl.ds(start, share_ref.shape[1])]
    attended_ref[...] = dot_by(ROWS_BY_ROWS, branch_grad, weight_ref[...]).astype(BF16)
    bias_ref[0] = jnp.sum(branch_grad.astype(F32), axis=0, keepdims=True)
    sums_ref[0, 0:1] = jnp.sum(middle_grad * branch, axis=0, keepdims=True)
    sums_ref[0, 1:2] = jnp.sum(hidden_grad, axis=0, keepdims=True)
    sums_ref[0, 2:3] = jnp.sum(hidden_grad * normed, axis=0, keepdims=True)


def by_place(body, name, outs, args, flops, scalars=None):
    places = args[0].shape[0] // SHORT

    def spec(a):
        if a.shape[0] == places * SHORT and len(a.shape) == 2:
            return pl.BlockSpec((SHORT, a.shape[1]), lambda i: (i, 0))
        if a.shape[0] == places and len(a.shape) == 3:
            return pl.BlockSpec((1, *a.shape[1:]), lambda i: (i, 0, 0))
        return pl.BlockSpec(a.shape, lambda i: (0,) * len(a.shape))

    front = [] if scalars is None else [scalars]
    return kernel_call(
        body,
        name,
        outs,
        front + args,
        flops,
        grid=(places,),
        in_specs=[SMEM] * len(front) + [spec(a) for a in args],
        out_specs=tuple(spec(a) for a in outs),
    )


def middle_back(scalars, term, other, branch, kept, upstream, mod_places, weight):
    count, width = kept.shape
    places = count // SHORT
    return by_place(
        middle_back_body,
        "middle_back",
        [
            array((count, width), F32),
            array((count, width), BF16),
            array((count, half_width(width)), BF16),
            array((count, weight.shape[0]), BF16),
            array((places, 3, width), F32),
            array((places, 1, width), F32),
        ],
        [term, other, branch, kept, upstream, mod_places, weight],
        2 * count * width * weight.shape[0],
        scalars,
    )


def input_back_body(term_ref, other_ref, middle_grad_ref, kept_ref, mod_ref, grad_ref, sums_ref):
    hidden_grad = term_ref[...].astype(F32) + other_ref[...].astype(F32)
    normed, inverse = layer_norm(kept_ref[...].astype(F32))
    grad = middle_grad_ref[...] + norm_back(hidden_grad * (1.0 + mod_ref[0, 1:2]), normed, inverse)
    grad_ref[...] = grad.astype(BF16)
    sums_ref[0, 0:1] = jnp.sum(hidden_grad, axis=0, keepdims=True)
    sums_ref[0, 1:2] = jnp.sum(hidden_grad * normed, axis=0, keepdims=True)


def input_back(term, other, middle_grad, kept, mod_places):
    count, width = kept.shape
    return by_place(
        input_back_body,
        "input_back",
        [array((count, width), BF16), array((count // SHORT, 2, width), F32)],
        [term, other, middle_grad, kept, mod_places],
        0,
    )


def result_body(term_ref, other_ref, bias_ref, branch_ref, kept_ref, up_ref, mod_ref, *rest):
    result_ref, sums_ref, bias_grad_ref = rest
    branch_two = term_ref[...].astype(F32) + other_ref[...].astype(F32) + bias_ref[...]
    middle = kept_ref[...].astype(F32) + mod_ref[0, 2:3] * branch_ref[...]
    gate = mod_ref[0, 5:6]
    upstream = up_ref[...].astype(F32)
    result_ref[...] = (middle + gate * branch_two).astype(BF16)
    sums_ref[0, 0:1] = jnp.sum(upstream * branch_two, axis=0, keepdims=True)
    down_in = (gate * upstream).astype(BF16).astype(F32)
    bias_grad_ref[0] = jnp.sum(down_in, axis=0, keepdims=True)


def result(term, other, bias, branch, kept, upstream, mod_places):
    count, width = kept.shape
    places = count // SHORT
    return by_place(
        result_body,
        "result",
        [
            array((count, width), BF16),
            array((places, 1, width), F32),
            array((places, 1, width), F32),
        ],
        [term, other, bias, branch, kept, upstream, mod_places],
        0,
    )


def weight_grad_body(packs, blocks, scalars, *refs):
    own_ref, shares, others = refs[0], refs[1:packs], refs[packs : 2 * packs - 1]
    columns, outs = refs[2 * packs - 1 : 3 * packs - 1], refs[3 * packs - 1 : -3]
    rows_all, columns_all, total = refs[-3:]
    count, width = own_ref.shape
    half = shares[0].shape[1]
    core = scalars[0]
    rows_all[:count] = own_ref[...]
    columns_all[:count] = columns[0][...]
    for entry in range(1, packs):
        rows = pl.ds(entry * count, count)
        rows_all[rows, pl.ds(aligned(core * (width - half)), half)] = shares[entry - 1][...]
        rows_all[rows, pl.ds(aligned((1 - core) * (width - half)), half)] = others[entry - 1][...]
        columns_all[rows] = columns[entry][...]
    total[...] = dot_by(COLUMNS_BY_COLUMNS, rows_all[...], columns_all[...])
    size = width // blocks
    for step in range(blocks):
        target = lax.rem(scalars[1] + step, blocks)
        piece = total[pl.ds(aligned(target * size, 8), size)]
        outs[step][...] = piece.astype(outs[step].dtype)


def weight_grad(scalars, own, shares, others, columns, packs, blocks):
    count, width = own.shape
    wide = columns[0].shape[1]
    size = width // blocks
    return kernel_call(
        lambda *refs: weight_grad_body(packs, blocks, *refs),
        "weight_grad",
        [array((size, wide), F32)] + [array((size, wide), BF16)] * (blocks - 1),
        [scalars, own, *shares, *others, *columns],
        2 * packs * count * width * wide,
        in_specs=[SMEM] + [VMEM] * (3 * packs - 1),
        scratch=[
            pltpu.VMEM((packs * count, width), BF16),
            pltpu.VMEM((packs * count, wide), BF16),
            pltpu.VMEM((width, wide), F32),
        ],
    )


def join_body(kind, starts, scalars, *refs):
    entries, out_ref, held = refs[:-2], refs[-2], refs[-1]
    packs = len(entries)
    for entry in range(packs):
        held[entry] = entries[entry][...]
    for number in range(packs):
        piece = held[jnp.bitwise_xor(scalars[2 + packs], number)].astype(F32)
        if kind == "qkv":
            share = piece.shape[1] // 3
            for part in range(3):
                out_ref[:, part, number * share : (number + 1) * share] = piece[
                    :, part * share : (part + 1) * share
                ]
        elif kind == "output":
            share = piece.shape[1]
            out_ref[number * share : (number + 1) * share] = piece.T
        else:
            ends = [*starts[1:], out_ref.shape[0 if kind == "down" else 1]]
            keep = ends[number] - starts[number]
            if kind == "down":
                out_ref[starts[number] : ends[number]] = piece[:, :keep].T
            else:
                out_ref[:, starts[number] : ends[number]] = piece[:, :keep]


def join(kind, scalars, entries, shape, starts=()):
    return kernel_call(
        lambda *refs: join_body(kind, starts, *refs),
        "join_" + kind,
        [array(shape, F32)],
        [scalars, *entries],
        0,
        in_specs=[SMEM] + [VMEM] * len(entries),
        scratch=[pltpu.VMEM((len(entries), *entries[0].shape), BF16)],
    )[0]


def modulation_body(active_ref, sums_ref, out_ref):
    active = active_ref[...]
    for number in range(sums_ref.shape[0]):
        out_ref[:, number] = dot_by(COLUMNS_BY_COLUMNS, active, sums_ref[number])


def modulation_grad(active, sums):
    rows = active.shape[1]
    return kernel_call(
        modulation_body,
        "modulation_grad",
        [array((rows, sums.shape[0], sums.shape[2]), F32)],
        [active, sums],
        2 * rows * math.prod(sums.shape),
    )[0]


def xor_permute(block, axis, bits):
    return lax.ppermute(block, axis, [(i, i ^ bits) for i in range(lax.axis_size(axis))])


def swap(block):
    return xor_permute(block, "head", 1)


def move(block, step):
    count = lax.axis_size("blk")
    pairs = [(i, i + step) for i in range(count) if 0 <= i + step < count]
    return lax.ppermute(block, "blk", pairs)


def gather_xor(block, axis, turned=False):
    bits = [1 << b for b in range((lax.axis_size(axis) - 1).bit_length())]
    held = {0: block}
    for bit in bits[::-1] if turned else bits:
        for entry in list(held):
            held[entry ^ bit] = xor_permute(held[entry], axis, bit)
    return [held[entry] for entry in range(lax.axis_size(axis))]


def in_order(entries, axis):
    order = jnp.arange(len(entries), dtype=jnp.int32) ^ lax.axis_index(axis)
    return jnp.take(jnp.stack(entries), order, axis=0)


def trade(pieces, axis):
    return [xor_permute(piece, axis, r) if r else piece for r, piece in enumerate(pieces)]


def windows(width, parts):
    tiles = width // LANES
    size = -(-tiles // parts)
    return [LANES * (q * (tiles - size) // (parts - 1)) for q in range(parts)], size * LANES


def half_width(width):
    return -(-width // (2 * LANES)) * LANES


def share_of(block):
    half = half_width(block.shape[1])
    first, last = block[:, :half], block[:, block.shape[1] - half :]
    return jnp.where(lax.axis_index("head") == 0, first, last)


def gather_shares(share, turned):
    shares = gather_xor(share, "pack", turned)[1:]
    return shares, [swap(entry) for entry in shares]


def sum_blk(pieces):
    count = len(pieces)
    total = pieces[0]
    for step in range(1, count):
        pairs = [(i, (i + step) % count) for i in range(count)]
        total = total + lax.ppermute(pieces[step], "blk", pairs).astype(F32)
    return total.astype(BF16)


def local(
    tokens_full,
    condition,
    kept_index,
    segment_ids,
    cotangent,
    qkv_weight,
    query_value_bias,
    output_weight,
    output_bias,
    hidden_weight,
    hidden_bias,
    down_weight,
    down_bias,
    modulation_weight,
    modulation_bias,
):
    width = tokens_full.shape[2]
    own_width = qkv_weight.shape[2]
    hidden = hidden_weight.shape[1]
    count = kept_index.shape[1]
    seg_count = condition.shape[1]
    places = count // SHORT
    longs = (segment_ids.shape[1] - SHORT * seg_count) // (LONG - SHORT)
    packs = lax.axis_size("pack")
    blocks = lax.axis_size("blk")
    blk = lax.axis_index("blk")
    core = lax.axis_index("head")
    pack = lax.axis_index("pack")

    local_index = kept_index[0] - blk * (2 * count)
    full_rows = tokens_full[0]
    cot_rows = cotangent[0]
    picker = (
        local_index[:, None] == jnp.arange(full_rows.shape[0], dtype=jnp.int32)[None, :]
    ).astype(BF16)
    kept_rows = bf_dot(picker, full_rows).astype(BF16)
    upstream = bf_dot(picker, cot_rows).astype(BF16)

    segments = segment_ids[0, ::SHORT]
    outside = jnp.full((places,), -1, jnp.int32)
    near_places = lax.dynamic_slice_in_dim(
        jnp.concatenate([outside, segments, outside]), blk * places, 3 * places, 0
    )
    own_places = near_places[places : 2 * places]
    same = own_places[:, None] == near_places[None, :]
    first_place = jnp.argmax(same, axis=1).astype(jnp.int32)
    is_long = (jnp.sum(same.astype(jnp.int32), axis=1) > 1).astype(jnp.int32)
    reaches_low = near_places[places - 1] == near_places[places]
    reaches_high = near_places[2 * places - 1] == near_places[2 * places]
    order = jnp.arange(packs, dtype=jnp.int32) ^ pack
    table = jnp.concatenate(
        [
            jnp.stack(
                [
                    jnp.where(reaches_low, 0, 2 * count),
                    jnp.where(reaches_low, first_place[0], -1),
                    jnp.where(reaches_high, first_place[-1], -1),
                ]
            ),
            first_place,
            is_long,
            order,
        ]
    ).astype(jnp.int32)
    starts, window = windows(hidden, packs)
    scalars = jnp.concatenate(
        [jnp.stack([core, blk]), jnp.take(jnp.asarray(starts, jnp.int32), order), pack[None]]
    ).astype(jnp.int32)

    def beside(block):
        low, high = move(block, 1), move(block, -1)
        if longs == 1:
            return jnp.where(reaches_low, low, high)
        return jnp.concatenate([low, high], axis=0)

    if longs == 1:
        beside_places = jnp.where(reaches_low, near_places[:places], near_places[2 * places :])
    else:
        beside_places = jnp.concatenate([near_places[:places], near_places[2 * places :]])
    half = count // 2
    near_half = beside(lax.dynamic_slice_in_dim(kept_rows, core * half, half, 0))
    other_half = swap(near_half)
    first = jnp.where(core == 0, near_half, other_half).reshape(-1, half, width)
    second = jnp.where(core == 0, other_half, near_half).reshape(-1, half, width)
    near_rows = jnp.concatenate([first, second], axis=1).reshape(-1, width)

    cond_rows = condition[0].astype(F32)
    active = jax.nn.silu(cond_rows).astype(BF16)
    mod_own = (
        jnp.einsum("sd,dgf->sgf", active, modulation_weight, preferred_element_type=F32)
        + modulation_bias.astype(F32)[None]
    )
    mod_other = swap(mod_own)
    mod_all = jnp.concatenate(
        [jnp.where(core == 0, mod_own, mod_other), jnp.where(core == 0, mod_other, mod_own)],
        axis=2,
    )
    mod_places = jnp.take(mod_all, own_places, axis=0)
    mod_beside = jnp.take(mod_all, jnp.maximum(beside_places, 0), axis=0)

    gate_two = jnp.broadcast_to(mod_places[:, 5:6], (places, SHORT, width)).reshape(count, width)
    down_in = (gate_two * upstream.astype(F32)).astype(BF16)
    down_shares = gather_shares(share_of(down_in), False)

    qkv_parts = jnp.swapaxes(qkv_weight, 0, 1)
    wide_bias = query_value_bias.astype(F32)
    qkv_bias = jnp.stack([wide_bias[0], jnp.zeros_like(wide_bias[0]), wide_bias[1]])[:, None]
    hidden_one, qkv_own = project(kept_rows, mod_places, qkv_parts, qkv_bias)
    hidden_one_shares = gather_shares(share_of(hidden_one), True)
    _, qkv_near = project(near_rows, mod_beside, qkv_parts, qkv_bias)

    attended, branch_term, attended_pieces = attend(table, qkv_own, qkv_near, output_weight, packs)
    branch_other = swap(branch_term)
    attended_all = trade(attended_pieces, "pack")
    branch_one, hidden_two, hidden_two_share, two_term, back_term, hidden_sums, gelu, pre = feed(
        scalars,
        kept_rows,
        branch_term,
        branch_other,
        output_bias.astype(F32)[None],
        mod_places,
        down_in,
        hidden_weight,
        hidden_bias.astype(F32)[None],
        down_weight,
        packs,
    )
    back_other = swap(back_term)
    gelu_all = trade(gelu, "pack")
    hidden_two_shares = gather_shares(hidden_two_share, False)
    pre_all = trade(pre, "pack")
    two_other = swap(two_term)

    middle_grad, branch_grad, branch_grad_share, attended_grad, middle_sums, output_sums = (
        middle_back(
            scalars,
            back_term,
            back_other,
            branch_one,
            kept_rows,
            upstream,
            mod_places,
            output_weight,
        )
    )
    near_grad = beside(attended_grad)
    branch_grad_shares = gather_shares(branch_grad_share, True)
    result_rows, two_sums, down_sums = result(
        two_term,
        two_other,
        down_bias.astype(F32)[None],
        branch_one,
        kept_rows,
        upstream,
        mod_places,
    )

    def put_rows(base, rows):
        spread = dot_by(COLUMNS_BY_COLUMNS, picker, rows)
        kept = jnp.max(picker, axis=0)[:, None] > 0
        return jnp.where(kept, spread.astype(BF16), base)[None]

    block_output = put_rows(full_rows, result_rows)

    hidden_term, qkv_sums, qkv_pieces = attend_back(
        table, qkv_own, qkv_near, attended_grad, near_grad, qkv_parts, packs
    )
    hidden_other = swap(hidden_term)
    qkv_all = trade(qkv_pieces, "pack")
    input_grad, input_sums = input_back(
        hidden_term, hidden_other, middle_grad, kept_rows, mod_places
    )
    tokens_grad = put_rows(cot_rows, input_grad)

    def total_grad(kind, own, shares, columns, turned, shape):
        terms = weight_grad(scalars, own, *shares, columns, packs, blocks)
        entries = gather_xor(sum_blk(terms), "pack", turned)
        return join(kind, scalars, entries, shape, starts)

    rows = width // blocks
    down_weight_grad = total_grad("down", down_in, down_shares, gelu_all, False, (hidden, rows))
    hidden_weight_grad = total_grad(
        "hidden", hidden_two, hidden_two_shares, pre_all, True, (rows, hidden)
    )
    output_weight_grad = total_grad(
        "output", branch_grad, branch_grad_shares, attended_all, False, (own_width, rows)
    )
    qkv_weight_grad = total_grad(
        "qkv", hidden_one, hidden_one_shares, qkv_all, True, (rows, 3, own_width)
    )

    place_sums = jnp.concatenate([input_sums, middle_sums, two_sums], axis=1)
    own_sums = lax.dynamic_slice_in_dim(place_sums, core * own_width, own_width, 2)
    place_active = jnp.take(active, own_places, axis=0).astype(F32)
    sent = jnp.concatenate(
        [
            own_sums.reshape(-1),
            place_active.reshape(-1),
            qkv_sums.reshape(-1),
            jnp.sum(output_sums, axis=(0, 1)),
            hidden_sums.reshape(-1),
            jnp.sum(down_sums, axis=(0, 1)),
        ]
    ).reshape(-1, LANES)
    by_blk = in_order(gather_xor(sent, "blk"), "blk")
    by_pack = in_order(gather_xor(by_blk, "pack"), "pack")
    received = by_pack.reshape(packs * blocks, -1)
    cut = places * 6 * own_width
    sums_all = received[:, :cut].reshape(-1, 6, own_width)
    active_all = received[:, cut : cut + places * width].reshape(-1, width)
    biases = jnp.sum(received[:, cut + places * width :], axis=0)
    modulation_bias_grad = jnp.sum(sums_all, axis=0)

    def two_terms(values):
        high = values.astype(BF16)
        return high, (values - high.astype(F32)).astype(BF16)

    active_share = lax.dynamic_slice_in_dim(active_all, blk * rows, rows, 1).astype(BF16)
    modulation_weight_grad = modulation_grad(
        jnp.concatenate([active_share, active_share], axis=0),
        jnp.swapaxes(jnp.concatenate(two_terms(sums_all), axis=0), 0, 1),
    )

    pack_sums = lax.dynamic_index_in_dim(
        sums_all.reshape(packs, -1, 6 * own_width), pack, 0, keepdims=False
    )
    of_segment = (jnp.arange(seg_count, dtype=jnp.int32)[:, None] == segments[None]).astype(BF16)
    mod_grad = sum(bf_dot(of_segment, term) for term in two_terms(pack_sums))
    cond_terms = jnp.einsum(
        "sgf,dgf->sd",
        jnp.concatenate(two_terms(mod_grad), axis=0).reshape(-1, 6, own_width),
        modulation_weight,
        preferred_element_type=F32,
    )
    cond_term = cond_terms[:seg_count] + cond_terms[seg_count:]
    cond_total = cond_term + swap(cond_term)
    squashed = jax.nn.sigmoid(cond_rows)
    condition_grad = (cond_total * squashed * (1.0 + cond_rows * (1.0 - squashed)))[None]

    ends = [own_width, 2 * own_width, 2 * own_width + width, 2 * own_width + width + hidden]
    value_bias = jnp.stack([biases[: ends[0]], biases[ends[0] : ends[1]]])
    return (
        block_output,
        tokens_grad,
        condition_grad,
        qkv_weight_grad,
        value_bias,
        output_weight_grad,
        biases[ends[1] : ends[2]],
        hidden_weight_grad,
        biases[ends[2] : ends[3]],
        down_weight_grad,
        biases[ends[3] :],
        modulation_weight_grad,
        modulation_bias_grad,
    )


def solution(mesh):
    in_specs = (
        P("pack", "blk", None),
        P("pack", None, None),
        P("pack", "blk"),
        P("pack", None),
        P("pack", "blk", None),
        P(None, None, "head"),
        P(None, "head"),
        P("head", None),
        P(),
        P(None, "head"),
        P("head"),
        P("head", None),
        P(),
        P(None, None, "head"),
        P(None, "head"),
    )
    out_specs = (
        P("pack", "blk", None),
        P("pack", "blk", None),
        P("pack", None, None),
        P("blk", None, "head"),
        P(None, "head"),
        P("head", "blk"),
        P(),
        P("blk", "head"),
        P("head"),
        P("head", "blk"),
        P(),
        P("blk", None, "head"),
        P(None, "head"),
    )
    return jax.shard_map(local, mesh=mesh, in_specs=in_specs, out_specs=out_specs, check_vma=False)
```

```python
import math

import jax
import jax.numpy as jnp
from jax import lax
from jax.experimental import pallas as pl
from jax.experimental.pallas import tpu as pltpu
from jax.sharding import PartitionSpec as P

HEAD_DIM = 72
SHORT = 128
LONG = 4 * SHORT
LANES = 128
EPSILON = 1e-06
FACTOR = 1.0 / math.sqrt(HEAD_DIM)
FACTOR_LOG2 = FACTOR * math.log2(math.e)
GELU_SLOPE = math.sqrt(2.0 / math.pi)
GELU_CUBE = 0.044715
F32 = jnp.float32
BF16 = jnp.bfloat16
ROWS_BY_ROWS = (((1,), (1,)), ((), ()))
COLUMNS_BY_COLUMNS = (((0,), (0,)), ((), ()))
VMEM = pl.BlockSpec(memory_space=pltpu.VMEM)
SMEM = pl.BlockSpec(memory_space=pltpu.SMEM)


def bf_dot(operand_a, operand_b):
    return jnp.dot(operand_a, operand_b, preferred_element_type=F32)


def dot_by(dims, operand_a, operand_b):
    return lax.dot_general(operand_a, operand_b, dims, preferred_element_type=F32)


def array(shape, kind):
    return jax.ShapeDtypeStruct(shape, kind)


SLOW = 1000


def kernel_call(
    body, name, outs, args, flops, grid=(), in_specs=None, out_specs=None, scratch=(), vmem=56
):
    moved = sum(math.prod(a.shape) * a.dtype.itemsize for a in (*args, *outs))
    return pl.pallas_call(
        body,
        name=name,
        out_shape=tuple(outs),
        grid=grid,
        in_specs=in_specs or [VMEM] * len(args),
        out_specs=out_specs or (VMEM,) * len(outs),
        scratch_shapes=scratch,
        compiler_params=pltpu.CompilerParams(vmem_limit_bytes=vmem << 20),
        cost_estimate=pl.CostEstimate(
            flops=int(flops) // SLOW, bytes_accessed=int(moved) // SLOW, transcendentals=0
        ),
    )(*args)


def aligned(index, to=LANES):
    return pl.multiple_of(index, to)


def layer_norm(values):
    center = values - jnp.mean(values, axis=-1, keepdims=True)
    spread = jnp.mean(center * center, axis=-1, keepdims=True)
    inverse = lax.rsqrt(spread + EPSILON)
    return (center * inverse, inverse)


def norm_back(upstream, normed, inverse):
    mean_grad = jnp.mean(upstream, axis=-1, keepdims=True)
    mean_cross = jnp.mean(upstream * normed, axis=-1, keepdims=True)
    return inverse * (upstream - mean_grad - normed * mean_cross)


def gelu_pair(value):
    square = value * value
    bent = jnp.tanh(GELU_SLOPE * (value + GELU_CUBE * (value * square)))
    half = 0.5 * (1.0 + bent)
    slope = GELU_SLOPE * (1.0 + (3.0 * GELU_CUBE) * square)
    return value * half, half + 0.5 * value * (1.0 - bent * bent) * slope


def plan_body(longs, packs, starts, place_ref, segments, out_ref):
    core, blk, pack, blocks = (place_ref[number] for number in range(4))
    places = 3
    out_ref[0] = core
    out_ref[1] = blk
    for entry in range(packs):
        window = jnp.bitwise_xor(pack, entry)
        start = jnp.int32(0)
        for number in range(packs):
            start = jnp.where(window == number, starts[number], start)
        out_ref[2 + entry] = start
    out_ref[2 + packs] = pack
    near = []
    for number in range(3 * places):
        index = (blk - 1) * places + number
        inside = jnp.logical_and(index >= 0, index < blocks * places)
        found = segments[jnp.clip(index, 0, blocks * places - 1) * SHORT]
        near.append(jnp.where(inside, found, -1))
    reaches_low = near[places - 1] == near[places]
    reaches_high = near[2 * places - 1] == near[2 * places]
    base = 3 + packs
    firsts, lengths = [], []
    for place in range(places):
        own = near[places + place]
        first = jnp.int32(0)
        length = jnp.int32(0)
        for number in reversed(range(3 * places)):
            same = near[number] == own
            first = jnp.where(same, number, first)
            length = length + same.astype(jnp.int32)
        firsts.append(first)
        lengths.append((length > 1).astype(jnp.int32))
    out_ref[base] = jnp.where(reaches_low, 0, 2 * places * SHORT)
    out_ref[base + 1] = jnp.where(reaches_low, firsts[0], -1)
    out_ref[base + 2] = jnp.where(reaches_high, firsts[-1], -1)
    for place in range(places):
        out_ref[base + 3 + place] = firsts[place]
        out_ref[base + 3 + places + place] = lengths[place]
        out_ref[base + 3 + 2 * places + place] = near[places + place]
    beside = near[:places] + near[2 * places :]
    if longs == 1:
        beside = [
            jnp.where(reaches_low, low, high)
            for low, high in zip(near[:places], near[2 * places :])
        ]
    for number, segment in enumerate(beside):
        out_ref[base + 3 + 3 * places + number] = jnp.maximum(segment, 0)
    out_ref[base + 3 + 3 * places + len(beside)] = reaches_low.astype(jnp.int32)


def plan(longs, packs, starts, place, segments):
    beside = 3 if longs == 1 else 6
    size = 3 + packs + 3 + 9 + beside + 1
    return kernel_call(
        lambda *refs: plan_body(longs, packs, starts, *refs),
        "plan",
        [array((size,), jnp.int32)],
        [place, segments],
        0,
        in_specs=[SMEM, SMEM],
        out_specs=(SMEM,),
    )[0]


def pick_body(first, scalars, own_ref, other_ref, out_ref):
    half = own_ref.shape[2]
    core = scalars[0]
    for place in range(out_ref.shape[0]):
        segment = scalars[first + place]

        def write(low, high):
            out_ref[place, :, :half] = low[segment]
            out_ref[place, :, half:] = high[segment]

        pl.when(core == 0)(lambda: write(own_ref, other_ref))
        pl.when(core == 1)(lambda: write(other_ref, own_ref))


def pick(scalars, first, own, other, count):
    shape = (count, own.shape[1], 2 * own.shape[2])
    return kernel_call(
        lambda *refs: pick_body(first, *refs),
        "pick",
        [array(shape, F32)],
        [scalars, own, other],
        0,
        in_specs=[SMEM, VMEM, VMEM],
    )[0]


def norm_body(scalars, own_ref, near_ref, up_ref, mod_ref, hidden_ref, down_in_ref, shares_ref):
    step = pl.program_id(0)
    places = 3
    half = shares_ref.shape[1] // 2
    shift, scale = mod_ref[0, 0:1], mod_ref[0, 1:2]

    def write(rows):
        normed, _ = layer_norm(rows.astype(F32))
        hidden_ref[...] = (normed * (1.0 + scale) + shift).astype(BF16)

    @pl.when(step < places)
    def _():
        write(own_ref[...])
        down_in_ref[...] = (mod_ref[0, 5:6] * up_ref[...].astype(F32)).astype(BF16)
        start = aligned(scalars[0] * (hidden_ref.shape[1] - half))
        shares_ref[:, :half] = down_in_ref[:, pl.ds(start, half)]
        shares_ref[:, half:] = hidden_ref[:, pl.ds(start, half)]

    pl.when(step >= places)(lambda: write(near_ref[...]))


def norm(scalars, own, near, upstream, mod_places):
    count, width = own.shape
    places = count // SHORT
    total = count + near.shape[0]
    share = 2 * half_width(width)

    def own_place(i):
        return (jnp.minimum(i, places - 1), 0)

    return kernel_call(
        norm_body,
        "norm",
        [array((total, width), BF16), array((count, width), BF16), array((count, share), BF16)],
        [scalars, own, near, upstream, mod_places],
        0,
        grid=(total // SHORT,),
        in_specs=[
            SMEM,
            pl.BlockSpec((SHORT, width), own_place),
            pl.BlockSpec((SHORT, width), lambda i: (jnp.maximum(i - places, 0), 0)),
            pl.BlockSpec((SHORT, width), own_place),
            pl.BlockSpec((1, *mod_places.shape[1:]), lambda i: (i, 0, 0)),
        ],
        out_specs=(
            pl.BlockSpec((SHORT, width), lambda i: (i, 0)),
            pl.BlockSpec((SHORT, width), own_place),
            pl.BlockSpec((SHORT, share), own_place),
        ),
    )


def lay_beside(buffer, own, beside, table):
    count = own.shape[0]
    buffer[count : 2 * count] = own
    if beside.shape[0] == count:
        buffer[pl.ds(aligned(table[0], SHORT), count)] = beside
    else:
        buffer[:count] = beside[:count]
        buffer[2 * count :] = beside[count:]


def attend_body(base, scalars, rows_ref, weight_ref, attended_ref, branch_ref, keys, values, turned):
    count, own_width = attended_ref.shape
    places = count // SHORT
    table = [scalars[base + number] for number in range(3)]
    lay_beside(keys, rows_ref[1, :count], rows_ref[1, count:], table)
    lay_beside(values, rows_ref[2, :count], rows_ref[2, count:], table)

    def attend(place, size):
        near = pl.ds(aligned(scalars[base + 3 + place] * SHORT, SHORT), size)
        rows = pl.ds(aligned(place * SHORT, SHORT), SHORT)
        for head in range(own_width // HEAD_DIM):
            columns = pl.ds(head * HEAD_DIM, HEAD_DIM)
            scores = dot_by(ROWS_BY_ROWS, keys[near, columns], rows_ref[0, rows, columns])
            peak = jnp.max(scores, axis=0, keepdims=True)
            exponent = jnp.exp2((scores - peak) * FACTOR_LOG2)
            total = jnp.sum(exponent, axis=0, keepdims=True)
            probs = (exponent * (1.0 / total)).astype(BF16)
            turned[columns] = dot_by(COLUMNS_BY_COLUMNS, values[near, columns], probs)
        attended_ref[rows] = turned[...].T.astype(BF16)

    def one_place(place, carry):
        is_long = scalars[base + 3 + places + place]
        pl.when(is_long == 1)(lambda: attend(place, LONG))
        pl.when(is_long == 0)(lambda: attend(place, SHORT))
        return carry

    lax.fori_loop(0, places, one_place, 0)
    branch_ref[...] = bf_dot(attended_ref[...], weight_ref[...])


def attend(base, scalars, rows, weight, count):
    own_width, width = weight.shape
    return kernel_call(
        lambda *refs: attend_body(base, *refs),
        "attend",
        [array((count, own_width), BF16), array((count, width), F32)],
        [scalars, rows, weight],
        2 * count * own_width * (width + 2 * LONG),
        in_specs=[SMEM, VMEM, VMEM],
        scratch=[
            pltpu.VMEM((3 * count, own_width), BF16),
            pltpu.VMEM((3 * count, own_width), BF16),
            pltpu.VMEM((own_width, SHORT), F32),
        ],
    )


def attend_back_body(base, scalars, rows_ref, grad_ref, near_grad_ref, weight_ref, *rest):
    hidden_grad_ref, bias_ref, pieces = rest[0], rest[1], rest[2:-3]
    held, grads, split = rest[-3:]
    count, own_width = grad_ref.shape
    places = count // SHORT
    table = [scalars[base + number] for number in range(3)]
    for number in range(3):
        lay_beside(held.at[number], rows_ref[number, :count], rows_ref[number, count:], table)
    lay_beside(held.at[3], grad_ref[...], near_grad_ref[...], table)

    def attend_back(first, size):
        rows = pl.ds(aligned(first * SHORT, SHORT), size)
        for head in range(own_width // HEAD_DIM):
            columns = pl.ds(head * HEAD_DIM, HEAD_DIM)
            query, key, value, grad = (held[number, rows, columns] for number in range(4))
            scores = dot_by(ROWS_BY_ROWS, key, query)
            peak = jnp.max(scores, axis=0, keepdims=True)
            exponent = jnp.exp2((scores - peak) * FACTOR_LOG2)
            probs = exponent * (1.0 / jnp.sum(exponent, axis=0, keepdims=True))
            probs_grad = dot_by(ROWS_BY_ROWS, value, grad)
            row_dot = jnp.sum(probs * probs_grad, axis=0, keepdims=True)
            score_grad = (probs * (probs_grad - row_dot)).astype(BF16)
            query_grad = dot_by(COLUMNS_BY_COLUMNS, score_grad, key) * FACTOR
            grads[0, rows, columns] = query_grad.astype(BF16)
            grads[1, rows, columns] = (bf_dot(score_grad, query) * FACTOR).astype(BF16)
            grads[2, rows, columns] = bf_dot(probs.astype(BF16), grad).astype(BF16)

    def short_latent(place, carry):
        is_long = scalars[base + 3 + places + place]
        pl.when(is_long == 0)(lambda: attend_back(places + place, SHORT))
        return carry

    lax.fori_loop(0, places, short_latent, 0)

    def long_latent(number, carry):
        first = scalars[base + 1 + number]
        pl.when(first >= 0)(lambda: attend_back(first, LONG))
        return carry

    lax.fori_loop(0, 2, long_latent, 0)
    own_grads = [grads[number, count : 2 * count] for number in range(3)]
    total = bf_dot(own_grads[0], weight_ref[0])
    for number in range(1, 3):
        total = total + bf_dot(own_grads[number], weight_ref[number])
    hidden_grad_ref[...] = total.astype(BF16)
    for number, grad in enumerate((own_grads[0], own_grads[2])):
        bias_ref[number : number + 1] = jnp.sum(grad.astype(F32), axis=0, keepdims=True)
    share = own_width // len(pieces)
    for number in range(len(pieces)):
        for part in range(3):
            split[number, :, part * share : (part + 1) * share] = own_grads[part][
                :, number * share : (number + 1) * share
            ]
    for entry, piece in enumerate(pieces):
        piece[...] = split[jnp.bitwise_xor(scalars[base - 1], entry)]


def attend_back(base, scalars, rows, grad, near_grad, weight, packs):
    count, own_width = grad.shape
    width = weight.shape[2]
    share = 3 * own_width // packs
    outs = kernel_call(
        lambda *refs: attend_back_body(base, *refs),
        "attend_back",
        [array((count, width), BF16), array((2, own_width), F32)]
        + [array((count, share), BF16)] * packs,
        [scalars, rows, grad, near_grad, weight],
        6 * count * own_width * width + 10 * own_width * LONG * LONG,
        in_specs=[SMEM] + [VMEM] * 4,
        scratch=[
            pltpu.VMEM((4, 3 * count, own_width), BF16),
            pltpu.VMEM((3, 3 * count, own_width), BF16),
            pltpu.VMEM((packs, count, share), BF16),
        ],
    )
    return outs[0], outs[1], list(outs[2:])


def whole(shape):
    return pl.BlockSpec(shape, lambda i: (0,) * len(shape))


def feed_up_body(scalars, kept_ref, term_ref, other_ref, bias_ref, mod_ref, *rest):
    weight_ref, hidden_bias_ref, branch_ref, hidden_ref, share_ref, slope_ref = rest[:6]
    gelu_ref, pieces = rest[6], rest[7:]
    step = pl.program_id(0)
    size = weight_ref.shape[1]

    @pl.when(step == 0)
    def _():
        def place(number, carry):
            rows = pl.ds(aligned(number * SHORT, SHORT), SHORT)
            branch = (term_ref[rows] + other_ref[rows]) + bias_ref[...]
            branch_ref[rows] = branch
            middle = kept_ref[rows].astype(F32) + mod_ref[number, 2:3] * branch
            normed, _ = layer_norm(middle)
            shift, scale = mod_ref[number, 3:4], mod_ref[number, 4:5]
            hidden_ref[rows] = (normed * (1.0 + scale) + shift).astype(BF16)
            return carry

        lax.fori_loop(0, kept_ref.shape[0] // SHORT, place, 0)
        start = aligned(scalars[0] * (hidden_ref.shape[1] - share_ref.shape[1]))
        share_ref[...] = hidden_ref[:, pl.ds(start, share_ref.shape[1])]

    gelu, slope = gelu_pair(bf_dot(hidden_ref[...], weight_ref[...]) + hidden_bias_ref[...])
    slope_ref[...] = slope
    gelu_ref[:, pl.ds(aligned(step * size), size)] = gelu.astype(BF16)

    @pl.when(step == pl.num_programs(0) - 1)
    def _():
        for entry, piece in enumerate(pieces):
            piece[...] = gelu_ref[:, pl.ds(aligned(scalars[2 + entry]), piece.shape[1])]


def feed_up(scalars, kept, term, other, bias, mod_places, weight, hidden_bias, packs):
    count, width = kept.shape
    hidden = weight.shape[1]
    size = hidden // 3
    window = windows(hidden, packs)[1]
    outs = [
        array((count, width), F32),
        array((count, width), BF16),
        array((count, half_width(width)), BF16),
        array((count, hidden), F32),
        array((count, hidden), BF16),
    ] + [array((count, window), BF16)] * packs
    out_specs = [whole(out.shape) for out in outs]
    out_specs[3] = pl.BlockSpec((count, size), lambda i: (0, i))
    result = kernel_call(
        feed_up_body,
        "feed_up",
        outs,
        [scalars, kept, term, other, bias, mod_places, weight, hidden_bias],
        2 * count * width * hidden,
        grid=(hidden // size,),
        in_specs=[
            SMEM,
            *[whole(a.shape) for a in (kept, term, other, bias, mod_places)],
            pl.BlockSpec((width, size), lambda i: (0, i)),
            pl.BlockSpec((1, size), lambda i: (0, i)),
        ],
        out_specs=tuple(out_specs),
    )
    return *result[:5], list(result[5:])


def feed_back_body(scalars, down_in_ref, down_ref, slope_ref, weight_ref, *rest):
    back_ref, sums_ref, pieces, pre_rows = rest[0], rest[1], rest[2:-1], rest[-1]
    step = pl.program_id(0)
    size = weight_ref.shape[1]
    pre_grad = dot_by(ROWS_BY_ROWS, down_in_ref[...], down_ref[...]) * slope_ref[...]
    pre_grad = pre_grad.astype(BF16)
    pre_rows[:, pl.ds(aligned(step * size), size)] = pre_grad
    sums_ref[...] = jnp.sum(pre_grad.astype(F32), axis=0, keepdims=True)
    back = dot_by(ROWS_BY_ROWS, pre_grad, weight_ref[...])

    @pl.when(step == 0)
    def _():
        back_ref[...] = back

    @pl.when(step > 0)
    def _():
        back_ref[...] += back

    @pl.when(step == pl.num_programs(0) - 1)
    def _():
        for entry, piece in enumerate(pieces):
            piece[...] = pre_rows[:, pl.ds(aligned(scalars[2 + entry]), piece.shape[1])]


def feed_back(scalars, down_in, down, slope, weight, packs):
    count, width = down_in.shape
    hidden = weight.shape[1]
    size = hidden // 3
    window = windows(hidden, packs)[1]
    outs = [array((count, width), F32), array((1, hidden), F32)]
    outs += [array((count, window), BF16)] * packs
    out_specs = [whole(out.shape) for out in outs]
    out_specs[1] = pl.BlockSpec((1, size), lambda i: (0, i))
    result = kernel_call(
        feed_back_body,
        "feed_back",
        outs,
        [scalars, down_in, down, slope, weight],
        4 * count * width * hidden,
        grid=(hidden // size,),
        in_specs=[
            SMEM,
            whole(down_in.shape),
            pl.BlockSpec((size, width), lambda i: (i, 0)),
            pl.BlockSpec((count, size), lambda i: (0, i)),
            pl.BlockSpec((width, size), lambda i: (0, i)),
        ],
        out_specs=tuple(out_specs),
        scratch=[pltpu.VMEM((count, hidden), BF16)],
    )
    return result[0], result[1], list(result[2:])


def middle_back_body(term_ref, other_ref, branch_ref, kept_ref, up_ref, mod_ref, *rest):
    weight_ref, middle_grad_ref, branch_grad_ref, attended_ref, sums_ref, bias_ref = rest
    hidden_grad = term_ref[...] + other_ref[...]
    branch = branch_ref[...]
    gate = mod_ref[0, 2:3]
    normed, inverse = layer_norm(kept_ref[...].astype(F32) + gate * branch)
    middle_grad = up_ref[...].astype(F32) + norm_back(
        hidden_grad * (1.0 + mod_ref[0, 4:5]), normed, inverse
    )
    middle_grad_ref[...] = middle_grad
    branch_grad = (gate * middle_grad).astype(BF16)
    branch_grad_ref[...] = branch_grad
    attended_ref[...] = dot_by(ROWS_BY_ROWS, branch_grad, weight_ref[...]).astype(BF16)
    bias_ref[0] = jnp.sum(branch_grad.astype(F32), axis=0, keepdims=True)
    sums_ref[0, 0:1] = jnp.sum(middle_grad * branch, axis=0, keepdims=True)
    sums_ref[0, 1:2] = jnp.sum(hidden_grad, axis=0, keepdims=True)
    sums_ref[0, 2:3] = jnp.sum(hidden_grad * normed, axis=0, keepdims=True)


def by_place(body, name, outs, args, flops):
    places = args[0].shape[0] // SHORT

    def spec(a):
        if a.shape[0] == places * SHORT and len(a.shape) == 2:
            return pl.BlockSpec((SHORT, a.shape[1]), lambda i: (i, 0))
        if a.shape[0] == places and len(a.shape) == 3:
            return pl.BlockSpec((1, *a.shape[1:]), lambda i: (i, 0, 0))
        return pl.BlockSpec(a.shape, lambda i: (0,) * len(a.shape))

    return kernel_call(
        body,
        name,
        outs,
        args,
        flops,
        grid=(places,),
        in_specs=[spec(a) for a in args],
        out_specs=tuple(spec(a) for a in outs),
    )


def middle_back(term, other, branch, kept, upstream, mod_places, weight):
    count, width = kept.shape
    places = count // SHORT
    return by_place(
        middle_back_body,
        "middle_back",
        [
            array((count, width), F32),
            array((count, width), BF16),
            array((count, weight.shape[0]), BF16),
            array((places, 3, width), F32),
            array((places, 1, width), F32),
        ],
        [term, other, branch, kept, upstream, mod_places, weight],
        2 * count * width * weight.shape[0],
    )


def input_back_body(term_ref, other_ref, middle_grad_ref, kept_ref, mod_ref, grad_ref, sums_ref):
    hidden_grad = term_ref[...].astype(F32) + other_ref[...].astype(F32)
    normed, inverse = layer_norm(kept_ref[...].astype(F32))
    grad = middle_grad_ref[...] + norm_back(hidden_grad * (1.0 + mod_ref[0, 1:2]), normed, inverse)
    grad_ref[...] = grad.astype(BF16)
    sums_ref[0, 0:1] = jnp.sum(hidden_grad, axis=0, keepdims=True)
    sums_ref[0, 1:2] = jnp.sum(hidden_grad * normed, axis=0, keepdims=True)


def input_back(term, other, middle_grad, kept, mod_places):
    count, width = kept.shape
    return by_place(
        input_back_body,
        "input_back",
        [array((count, width), BF16), array((count // SHORT, 2, width), F32)],
        [term, other, middle_grad, kept, mod_places],
        0,
    )


def result_body(term_ref, other_ref, bias_ref, branch_ref, kept_ref, up_ref, mod_ref, *rest):
    result_ref, sums_ref, bias_grad_ref = rest
    branch_two = term_ref[...].astype(F32) + other_ref[...].astype(F32) + bias_ref[...]
    middle = kept_ref[...].astype(F32) + mod_ref[0, 2:3] * branch_ref[...]
    gate = mod_ref[0, 5:6]
    upstream = up_ref[...].astype(F32)
    result_ref[...] = (middle + gate * branch_two).astype(BF16)
    sums_ref[0, 0:1] = jnp.sum(upstream * branch_two, axis=0, keepdims=True)
    down_in = (gate * upstream).astype(BF16).astype(F32)
    bias_grad_ref[0] = jnp.sum(down_in, axis=0, keepdims=True)


def result(term, other, bias, branch, kept, upstream, mod_places):
    count, width = kept.shape
    places = count // SHORT
    return by_place(
        result_body,
        "result",
        [
            array((count, width), BF16),
            array((places, 1, width), F32),
            array((places, 1, width), F32),
        ],
        [term, other, bias, branch, kept, upstream, mod_places],
        0,
    )


def weight_grad_body(packs, offset, count_shares, scalars, *refs):
    shares, refs = refs[:count_shares], refs[count_shares:]
    columns, refs = refs[:packs], refs[packs:]
    outs, (rows_all, columns_all, total) = refs[:-3], refs[-3:]
    count, wide = columns[0].shape
    width = rows_all.shape[1]
    half = half_width(width)
    for entry in range(packs):
        rows = pl.ds(entry * count, count)
        columns_all[rows] = columns[entry][...]
        if count_shares == 1:
            source = jnp.bitwise_xor(scalars[2 + packs], entry) * (2 * count)
            low = pl.ds(aligned(source, SHORT), count)
            high = pl.ds(aligned(source + count, SHORT), count)
            rows_all[rows, :half] = shares[0][low, offset : offset + half]
            rows_all[rows, half:] = shares[0][high, offset + 2 * half - width : offset + half]
        elif entry == 0:
            rows_all[rows] = shares[0][...]
        else:
            skip = width - half
            place = pl.ds(aligned(scalars[0] * skip), half)
            rows_all[rows, place] = shares[1][(entry - 1) * count : entry * count]
            place = pl.ds(aligned((1 - scalars[0]) * skip), half)
            rows_all[rows, place] = shares[2][(entry - 1) * count : entry * count]
    if len(outs) == 1:
        outs[0][...] = dot_by(COLUMNS_BY_COLUMNS, rows_all[...], columns_all[...]).astype(BF16)
        return
    total[...] = dot_by(COLUMNS_BY_COLUMNS, rows_all[...], columns_all[...])
    cut_by_blk(scalars, total, outs)


def cut_by_blk(scalars, total, outs):
    blocks = len(outs)
    size = total.shape[0] // blocks
    for step in range(blocks):
        target = lax.rem(scalars[1] + step, blocks)
        piece = total[pl.ds(aligned(target * size, 8), size)]
        outs[step][...] = piece.astype(outs[step].dtype)


def cut_shapes(width, wide, blocks):
    size = width // blocks
    return [array((size, wide), F32)] + [array((size, wide), BF16)] * (blocks - 1)


def weight_grad(scalars, width, offset, shares, columns, blocks=1):
    packs = len(columns)
    count, wide = columns[0].shape
    outs = [array((width, wide), BF16)]
    if blocks > 1:
        outs = cut_shapes(width, wide, blocks)
    return kernel_call(
        lambda *refs: weight_grad_body(packs, offset, len(shares), *refs),
        "weight_grad",
        outs,
        [scalars, *shares, *columns],
        2 * packs * count * width * wide,
        in_specs=[SMEM] + [VMEM] * (packs + len(shares)),
        scratch=[
            pltpu.VMEM((packs * count, width), BF16),
            pltpu.VMEM((packs * count, wide), BF16),
            pltpu.VMEM((width, wide), F32),
        ],
    )


def own_weight_grad_body(rows_ref, columns_ref, out_ref):
    out_ref[...] = dot_by(COLUMNS_BY_COLUMNS, rows_ref[...], columns_ref[...]).astype(BF16)


def own_weight_grad(rows, columns):
    shape = (rows.shape[1], columns.shape[1])
    return kernel_call(
        own_weight_grad_body,
        "own_weight_grad",
        [array(shape, BF16)],
        [rows, columns],
        2 * rows.shape[0] * math.prod(shape),
    )[0]


def join_body(kind, starts, packs, scalars, *refs):
    entries, outs, held = refs[:-2], refs[-2:-1], refs[-1]
    size = entries[0].shape[0] // (packs if len(entries) == 1 else 1)
    if len(entries) > 1:
        for entry in range(packs):
            held[entry] = entries[entry][...]
    if kind == "output":
        total = held[scalars[2 + packs]].astype(F32)
        for number in range(1, packs):
            total = total + held[jnp.bitwise_xor(scalars[2 + packs], number)].astype(F32)
        outs[0][...] = total
        return
    for number in range(packs):
        if len(entries) > 1:
            piece = held[jnp.bitwise_xor(scalars[2 + packs], number)].astype(F32)
        else:
            piece = entries[0][number * size : (number + 1) * size].astype(F32)
        if kind == "qkv":
            share = piece.shape[1] // 3
            for part in range(3):
                columns = pl.ds(number * share, share)
                outs[0][part, :, columns] = piece[:, part * share : (part + 1) * share]
        else:
            end = [*starts[1:], outs[0].shape[1]][number]
            outs[0][:, starts[number] : end] = piece[:, : end - starts[number]]


def join(kind, scalars, entries, packs, shapes, starts=()):
    held = (len(entries), *entries[0].shape) if len(entries) > 1 else (16, LANES)
    return kernel_call(
        lambda *refs: join_body(kind, starts, packs, *refs),
        "join_" + kind,
        [array(shape, F32) for shape in shapes],
        [scalars, *entries],
        0,
        in_specs=[SMEM] + [VMEM] * len(entries),
        scratch=[pltpu.VMEM(held, BF16)],
    )


def collect_body(first, scalars, input_ref, middle_ref, two_ref, active_ref, *refs):
    qkv_ref, output_ref, hidden_ref, down_ref, out_ref, held = refs
    places, _, width = middle_ref.shape
    half = width // 2
    row = 0

    def put(value):
        nonlocal row
        held[row : row + 1] = value
        row += 1

    def put_twice(value):
        high = value.astype(BF16).astype(F32)
        put(high)
        put(value - high)

    def put_sums(start):
        nonlocal row
        row = 0
        for place in range(places):
            for source in (input_ref, middle_ref, two_ref):
                for number in range(source.shape[1]):
                    put(source[place, number : number + 1, start : start + half])

    held[...] = jnp.zeros_like(held)
    pl.when(scalars[0] == 0)(lambda: put_sums(0))
    pl.when(scalars[0] == 1)(lambda: put_sums(half))
    for place in range(places):
        active = active_ref[pl.ds(scalars[first + place], 1)]
        put(active[:, :half])
        put(active[:, half:])
    put_twice(qkv_ref[0:1])
    put_twice(qkv_ref[1:2])
    for number in range(hidden_ref.shape[1] // half):
        put_twice(hidden_ref[:, number * half : (number + 1) * half])
    for source in (output_ref, down_ref):
        total = jnp.sum(source[...], axis=0)
        put_twice(total[:, :half])
        put_twice(total[:, half:])
    out_ref[...] = held[...].astype(BF16)


def collect(first, scalars, *args):
    places, _, width = args[0].shape
    hidden = args[6].shape[1]
    used = places * 8 + 2 * (2 + 2 * hidden // width + 4)
    size = -(-used // 16) * 16
    return kernel_call(
        lambda *refs: collect_body(first, *refs),
        "collect",
        [array((size, width // 2), BF16)],
        [scalars, *args],
        0,
        in_specs=[SMEM] + [VMEM] * len(args),
        scratch=[pltpu.VMEM((size, width // 2), F32)],
    )[0]


def spread_body(packs, blocks, places, size, scalars, segments, *refs):
    entries = refs[:packs]
    weight_ref, bias_ref, biases_ref, grad_ref, held, rows_all, active, sums = refs[packs:]
    half = weight_ref.shape[2]
    rows = weight_ref.shape[1]
    pack = scalars[2 + packs]
    for entry in range(packs):
        held[entry] = entries[entry][...].reshape(blocks, size, half)
    for number in range(packs):
        for block in range(blocks):
            source = held[
                jnp.bitwise_xor(pack, number), jnp.bitwise_xor(scalars[1], block)
            ]
            rows_all[number * blocks + block] = source.astype(F32)
    cut = 6 * places
    devices = packs * blocks

    def take_active(block):
        start = block * rows
        for device in range(devices):
            for place in range(places):
                row = cut + 2 * place
                whole_row = jnp.concatenate(
                    [rows_all[device, row : row + 1], rows_all[device, row + 1 : row + 2]], axis=1
                )
                number = device * places + place
                active[number : number + 1] = whole_row[:, start : start + rows]

    for block in range(blocks):
        pl.when(scalars[1] == block)(lambda: take_active(block))
    own_active = active[...].astype(BF16)
    for group in range(6):
        for device in range(devices):
            for place in range(places):
                number = device * places + place
                row = place * 6 + group
                sums[number : number + 1] = rows_all[device, row : row + 1]
        values = sums[...]
        bias_ref[group : group + 1] = jnp.sum(values, axis=0, keepdims=True)
        weight_ref[group] = dot_by(COLUMNS_BY_COLUMNS, own_active, values.astype(BF16))
    first = cut + 2 * places
    total = rows_all[0, first:]
    for device in range(1, devices):
        total = total + rows_all[device, first:]
    biases_ref[...] = total
    grad_ref[...] = jnp.zeros_like(grad_ref)
    for block in range(blocks):
        for place in range(places):
            segment = segments[(block * places + place) * SHORT]
            own = rows_all[pack * blocks + block, place * 6 : place * 6 + 6]
            grad_ref[segment] = grad_ref[segment] + own


def spread(scalars, segments, entries, packs, blocks, places, seg_count, width):
    size = entries[0].shape[0] // blocks
    half = entries[0].shape[1]
    devices = packs * blocks
    return kernel_call(
        lambda *refs: spread_body(packs, blocks, places, size, *refs),
        "spread",
        [
            array((6, width // blocks, half), F32),
            array((6, half), F32),
            array((size - 8 * places, half), F32),
            array((seg_count, 6, half), F32),
        ],
        [scalars, segments, *entries],
        0,
        in_specs=[SMEM, SMEM] + [VMEM] * packs,
        scratch=[
            pltpu.VMEM((packs, blocks, size, half), BF16),
            pltpu.VMEM((devices, size, half), F32),
            pltpu.VMEM((devices * places, width // blocks), F32),
            pltpu.VMEM((devices * places, half), F32),
        ],
    )


def xor_permute(block, axis, bits):
    return lax.ppermute(block, axis, [(i, i ^ bits) for i in range(lax.axis_size(axis))])


def swap(block):
    return xor_permute(block, "head", 1)


def move(block, step):
    count = lax.axis_size("blk")
    pairs = [(i, i + step) for i in range(count) if 0 <= i + step < count]
    return lax.ppermute(block, "blk", pairs)


def gather_xor(block, axis, turned=False):
    bits = [1 << b for b in range((lax.axis_size(axis) - 1).bit_length())]
    held = {0: block}
    for bit in bits[::-1] if turned else bits:
        for entry in list(held):
            held[entry ^ bit] = xor_permute(held[entry], axis, bit)
    return [held[entry] for entry in range(lax.axis_size(axis))]


def in_order(entries, axis):
    order = jnp.arange(len(entries), dtype=jnp.int32) ^ lax.axis_index(axis)
    return jnp.take(jnp.stack(entries), order, axis=0)


def trade(pieces, axis, entries):
    return {r: xor_permute(pieces[r], axis, r) for r in entries}


def windows(width, parts):
    tiles = width // LANES
    size = -(-tiles // parts)
    return [LANES * (q * (tiles - size) // (parts - 1)) for q in range(parts)], size * LANES


def half_width(width):
    return -(-width // (2 * LANES)) * LANES


def share_of(block):
    half = half_width(block.shape[1])
    first, last = block[:, :half], block[:, block.shape[1] - half :]
    return jnp.where(lax.axis_index("head") == 0, first, last)


def gather_shares(share):
    return lax.all_gather(share, ("pack", "head"), axis=0, tiled=True)


def hold(values, *after):
    flat, tree = jax.tree.flatten(values)
    held = lax.optimization_barrier((*flat, *after))
    return jax.tree.unflatten(tree, held[: len(flat)])


def sum_blk(pieces):
    count = len(pieces)
    total = pieces[0]
    for step in range(1, count):
        pairs = [(i, (i + step) % count) for i in range(count)]
        total = total + lax.ppermute(pieces[step], "blk", pairs).astype(F32)
    return total.astype(BF16)


def local(
    tokens_full,
    condition,
    kept_index,
    segment_ids,
    cotangent,
    qkv_weight,
    query_value_bias,
    output_weight,
    output_bias,
    hidden_weight,
    hidden_bias,
    down_weight,
    down_bias,
    modulation_weight,
    modulation_bias,
):
    width = tokens_full.shape[2]
    own_width = qkv_weight.shape[2]
    hidden = hidden_weight.shape[1]
    count = kept_index.shape[1]
    seg_count = condition.shape[1]
    places = count // SHORT
    longs = (segment_ids.shape[1] - SHORT * seg_count) // (LONG - SHORT)
    packs = lax.axis_size("pack")
    blocks = lax.axis_size("blk")
    blk = lax.axis_index("blk")
    core = lax.axis_index("head")
    pack = lax.axis_index("pack")

    local_index = kept_index[0] - blk * (2 * count)
    full_rows = tokens_full[0]
    cot_rows = cotangent[0]
    picker = (
        local_index[:, None] == jnp.arange(full_rows.shape[0], dtype=jnp.int32)[None, :]
    ).astype(BF16)
    kept_rows = bf_dot(picker, full_rows).astype(BF16)
    upstream = bf_dot(picker, cot_rows).astype(BF16)

    starts, window = windows(hidden, packs)
    place = jnp.stack([core, blk, pack, jnp.int32(blocks)]).astype(jnp.int32)
    scalars = plan(longs, packs, starts, place, segment_ids[0])
    base = 3 + packs
    reaches_low = scalars[-1] == 1

    def beside(block):
        low, high = move(block, 1), move(block, -1)
        if longs == 1:
            return jnp.where(reaches_low, low, high)
        return jnp.concatenate([low, high], axis=0)

    half = count // 2
    near_half = beside(lax.dynamic_slice_in_dim(kept_rows, core * half, half, 0))
    other_half = swap(near_half)
    first = jnp.where(core == 0, near_half, other_half).reshape(-1, half, width)
    second = jnp.where(core == 0, other_half, near_half).reshape(-1, half, width)
    near_rows = jnp.concatenate([first, second], axis=1).reshape(-1, width)

    cond_rows = condition[0].astype(F32)
    active = jax.nn.silu(cond_rows).astype(BF16)
    mod_own = (
        jnp.einsum("sd,dgf->sgf", active, modulation_weight, preferred_element_type=F32)
        + modulation_bias.astype(F32)[None]
    )
    mod_near = pick(
        scalars,
        base + 3 + 2 * places,
        mod_own,
        swap(mod_own),
        places + near_rows.shape[0] // SHORT,
    )
    mod_places = mod_near[:places]
    wide_bias = query_value_bias.astype(F32)
    qkv_bias = jnp.stack([wide_bias[0], jnp.zeros_like(wide_bias[0]), wide_bias[1]])[:, None]
    hidden_rows, down_in, share = norm(scalars, kept_rows, near_rows, upstream, mod_near)
    early_shares = gather_shares(share)
    qkv_turned = jnp.transpose(qkv_weight, (1, 2, 0))
    projected = jnp.einsum("td,gfd->gtf", hidden_rows, qkv_turned, preferred_element_type=F32)
    qkv_rows = (projected + qkv_bias).astype(BF16)

    attended, branch_term = attend(base, scalars, qkv_rows, output_weight, count)
    branch_one, hidden_two, hidden_two_share, slope, gelu, gelu_pieces = feed_up(
        scalars,
        kept_rows,
        branch_term,
        swap(branch_term),
        output_bias.astype(F32)[None],
        mod_places,
        hidden_weight,
        hidden_bias.astype(F32)[None],
        packs,
    )
    one_step = [r for r in range(1, packs) if r & (r - 1) == 0]
    further = [r for r in range(1, packs) if r & (r - 1)]

    def by_entry(pieces, *parts):
        found = {0: pieces[0]}
        for part in parts:
            found.update(part)
        return [found[r] for r in range(packs)]

    gelu_first = trade(gelu_pieces, "pack", one_step)
    hidden_two_shares = gather_shares(hidden_two_share)
    back_term, hidden_sums, pre_pieces = feed_back(
        scalars, down_in, down_weight, slope, hidden_weight, packs
    )
    back_term, gelu_first, gelu_pieces, pre_pieces = hold(
        (back_term, gelu_first, gelu_pieces, pre_pieces)
    )
    gelu_last = trade(gelu_pieces, "pack", further)
    middle_grad, branch_grad, attended_grad, middle_sums, output_sums = middle_back(
        back_term, swap(back_term), branch_one, kept_rows, upstream, mod_places, output_weight
    )
    attended_grad, gelu_last, early_shares, pre_pieces, gelu = hold(
        (attended_grad, gelu_last, early_shares, pre_pieces, gelu)
    )
    near_grad = beside(attended_grad)

    pre_first = trade(pre_pieces, "pack", range(1, packs))
    gelu_all = by_entry(gelu_pieces, gelu_first, gelu_last)
    down_raw = weight_grad(scalars, width, 0, [early_shares], gelu_all)[0]
    two_term = bf_dot(gelu, down_weight).astype(BF16)
    output_raw = own_weight_grad(branch_grad, attended)
    near_grad, down_raw, output_raw, two_term, pre_first = hold(
        (near_grad, down_raw, output_raw, two_term, pre_first)
    )
    half = half_width(width)
    rows = width // blocks
    down_term = lax.psum_scatter(down_raw, "blk", scatter_dimension=0, tiled=True)
    output_term = lax.psum_scatter(output_raw, "blk", scatter_dimension=0, tiled=True)
    hidden_term, qkv_sums, qkv_pieces = attend_back(
        base, scalars, qkv_rows, attended_grad, near_grad, qkv_turned, packs
    )
    hidden_term, qkv_pieces, two_term = hold((hidden_term, qkv_pieces, two_term))
    qkv_all = by_entry(qkv_pieces, trade(qkv_pieces, "pack", range(1, packs)))

    def put_rows(base, rows):
        spread = dot_by(COLUMNS_BY_COLUMNS, picker, rows)
        kept = jnp.max(picker, axis=0)[:, None] > 0
        return jnp.where(kept, spread.astype(BF16), base)[None]

    input_grad, input_sums = input_back(
        hidden_term, swap(hidden_term), middle_grad, kept_rows, mod_places
    )
    tokens_grad = put_rows(cot_rows, input_grad)
    pre_all = by_entry(pre_pieces, pre_first)
    hidden_raw = weight_grad(scalars, width, 0, [hidden_two_shares], pre_all)[0]
    result_rows, two_sums, down_sums = result(
        two_term,
        swap(two_term),
        down_bias.astype(F32)[None],
        branch_one,
        kept_rows,
        upstream,
        mod_places,
    )
    sent = collect(
        base + 3 + 2 * places,
        scalars,
        input_sums,
        middle_sums,
        two_sums,
        active.astype(F32),
        qkv_sums,
        output_sums,
        hidden_sums,
        down_sums,
    )
    qkv_all, tokens_grad, hidden_raw, result_rows, sent = hold(
        (qkv_all, tokens_grad, hidden_raw, result_rows, sent)
    )
    hidden_term = lax.psum_scatter(hidden_raw, "blk", scatter_dimension=0, tiled=True)
    by_blk = gather_xor(sent, "blk")
    qkv_terms = weight_grad(scalars, width, half, [early_shares], qkv_all, blocks)
    qkv_terms, result_rows, by_blk = hold((qkv_terms, result_rows, by_blk))
    entries = gather_xor(jnp.concatenate(by_blk, axis=0), "pack")
    block_output = put_rows(full_rows, result_rows)
    down_entries = gather_xor(down_term, "pack")
    qkv_share, entries, block_output, down_entries = hold(
        (sum_blk(qkv_terms), entries, block_output, down_entries)
    )
    qkv_entries = gather_xor(qkv_share, "pack")
    modulation_weight_grad, modulation_bias_grad, biases, mod_grad = spread(
        scalars, segment_ids[0], entries, packs, blocks, places, seg_count, width
    )
    down_weight_grad = join("down", scalars, down_entries, packs, [(rows, hidden)], starts)[0].T
    qkv_entries, output_term, hidden_term, modulation_weight_grad = hold(
        (qkv_entries, output_term, hidden_term, modulation_weight_grad)
    )
    hidden_weight_grad = join(
        "hidden", scalars, gather_xor(hidden_term, "pack", True), packs, [(rows, hidden)], starts
    )[0]
    output_weight_grad = join(
        "output", scalars, gather_xor(output_term, "pack"), packs, [(rows, own_width)]
    )[0].T
    qkv_weight_grad = join("qkv", scalars, qkv_entries, packs, [(3, rows, own_width)])[0]
    qkv_weight_grad = jnp.swapaxes(qkv_weight_grad, 0, 1)
    modulation_weight_grad = jnp.swapaxes(modulation_weight_grad, 0, 1)
    mod_high = mod_grad.astype(BF16)
    mod_low = (mod_grad - mod_high.astype(F32)).astype(BF16)
    cond_terms = jnp.einsum(
        "sgf,dgf->sd",
        jnp.concatenate([mod_high, mod_low], axis=0),
        modulation_weight,
        preferred_element_type=F32,
    )
    cond_term = cond_terms[:seg_count] + cond_terms[seg_count:]
    cond_total = cond_term + swap(cond_term)
    squashed = jax.nn.sigmoid(cond_rows)
    condition_grad = (cond_total * squashed * (1.0 + cond_rows * (1.0 - squashed)))[None]

    def bias_rows(first, number):
        pairs = biases[2 * first : 2 * (first + number)].reshape(number, 2, own_width)
        return (pairs[:, 0] + pairs[:, 1]).reshape(-1)

    value_bias = bias_rows(0, 2).reshape(2, own_width)
    hidden_rows_count = hidden // own_width
    return (
        block_output,
        tokens_grad,
        condition_grad,
        qkv_weight_grad,
        value_bias,
        output_weight_grad,
        bias_rows(2 + hidden_rows_count, 2),
        hidden_weight_grad,
        bias_rows(2, hidden_rows_count),
        down_weight_grad,
        bias_rows(4 + hidden_rows_count, 2),
        modulation_weight_grad,
        modulation_bias_grad,
    )


def solution(mesh):
    in_specs = (
        P("pack", "blk", None),
        P("pack", None, None),
        P("pack", "blk"),
        P("pack", None),
        P("pack", "blk", None),
        P(None, None, "head"),
        P(None, "head"),
        P("head", None),
        P(),
        P(None, "head"),
        P("head"),
        P("head", None),
        P(),
        P(None, None, "head"),
        P(None, "head"),
    )
    out_specs = (
        P("pack", "blk", None),
        P("pack", "blk", None),
        P("pack", None, None),
        P("blk", None, "head"),
        P(None, "head"),
        P("head", "blk"),
        P(),
        P("blk", "head"),
        P("head"),
        P("head", "blk"),
        P(),
        P("blk", None, "head"),
        P(None, "head"),
    )
    return jax.shard_map(local, mesh=mesh, in_specs=in_specs, out_specs=out_specs, check_vma=False)
```

```python
import math

import jax
import jax.numpy as jnp
from jax import lax
from jax.experimental import pallas as pl
from jax.experimental.pallas import tpu as pltpu
from jax.sharding import PartitionSpec as P

HEAD_DIM = 72
SHORT = 128
LONG = 4 * SHORT
LANES = 128
EPSILON = 1e-06
FACTOR = 1.0 / math.sqrt(HEAD_DIM)
FACTOR_LOG2 = FACTOR * math.log2(math.e)
GELU_SLOPE = math.sqrt(2.0 / math.pi)
GELU_CUBE = 0.044715
F32 = jnp.float32
BF16 = jnp.bfloat16
ROWS_BY_ROWS = (((1,), (1,)), ((), ()))
COLUMNS_BY_COLUMNS = (((0,), (0,)), ((), ()))
VMEM = pl.BlockSpec(memory_space=pltpu.VMEM)
SMEM = pl.BlockSpec(memory_space=pltpu.SMEM)


def bf_dot(operand_a, operand_b):
    return jnp.dot(operand_a, operand_b, preferred_element_type=F32)


def dot_by(dims, operand_a, operand_b):
    return lax.dot_general(operand_a, operand_b, dims, preferred_element_type=F32)


def array(shape, kind):
    return jax.ShapeDtypeStruct(shape, kind)


SLOW = 1000


def kernel_call(
    body, name, outs, args, flops, grid=(), in_specs=None, out_specs=None, scratch=(), far=(), vmem=48
):
    args = [
        pltpu.with_memory_space_constraint(a, pltpu.HBM) if number in far else a
        for number, a in enumerate(args)
    ]
    moved = sum(math.prod(a.shape) * a.dtype.itemsize for a in (*args, *outs))
    return pl.pallas_call(
        body,
        name=name,
        out_shape=tuple(outs),
        grid=grid,
        in_specs=in_specs or [VMEM] * len(args),
        out_specs=out_specs or (VMEM,) * len(outs),
        scratch_shapes=scratch,
        compiler_params=pltpu.CompilerParams(vmem_limit_bytes=vmem << 20),
        cost_estimate=pl.CostEstimate(
            flops=int(flops) // SLOW, bytes_accessed=int(moved) // SLOW, transcendentals=0
        ),
    )(*args)


def aligned(index, to=LANES):
    return pl.multiple_of(index, to)


def layer_norm(values):
    center = values - jnp.mean(values, axis=-1, keepdims=True)
    spread = jnp.mean(center * center, axis=-1, keepdims=True)
    inverse = lax.rsqrt(spread + EPSILON)
    return (center * inverse, inverse)


def norm_back(upstream, normed, inverse):
    mean_grad = jnp.mean(upstream, axis=-1, keepdims=True)
    mean_cross = jnp.mean(upstream * normed, axis=-1, keepdims=True)
    return inverse * (upstream - mean_grad - normed * mean_cross)


def gelu_pair(value):
    square = value * value
    bent = jnp.tanh(GELU_SLOPE * (value + GELU_CUBE * (value * square)))
    half = 0.5 * (1.0 + bent)
    slope = GELU_SLOPE * (1.0 + (3.0 * GELU_CUBE) * square)
    return value * half, half + 0.5 * value * (1.0 - bent * bent) * slope


def plan_body(longs, packs, starts, place_ref, segments, out_ref):
    core, blk, pack, blocks = (place_ref[number] for number in range(4))
    places = 3
    out_ref[0] = core
    out_ref[1] = blk
    for entry in range(packs):
        window = jnp.bitwise_xor(pack, entry)
        start = jnp.int32(0)
        for number in range(packs):
            start = jnp.where(window == number, starts[number], start)
        out_ref[2 + entry] = start
    out_ref[2 + packs] = pack
    near = []
    for number in range(3 * places):
        index = (blk - 1) * places + number
        inside = jnp.logical_and(index >= 0, index < blocks * places)
        found = segments[jnp.clip(index, 0, blocks * places - 1) * SHORT]
        near.append(jnp.where(inside, found, -1))
    reaches_low = near[places - 1] == near[places]
    reaches_high = near[2 * places - 1] == near[2 * places]
    base = 3 + packs
    firsts, lengths = [], []
    for place in range(places):
        own = near[places + place]
        first = jnp.int32(0)
        length = jnp.int32(0)
        for number in reversed(range(3 * places)):
            same = near[number] == own
            first = jnp.where(same, number, first)
            length = length + same.astype(jnp.int32)
        firsts.append(first)
        lengths.append((length > 1).astype(jnp.int32))
    out_ref[base] = jnp.where(reaches_low, 0, 2 * places * SHORT)
    out_ref[base + 1] = jnp.where(reaches_low, firsts[0], -1)
    out_ref[base + 2] = jnp.where(reaches_high, firsts[-1], -1)
    for place in range(places):
        out_ref[base + 3 + place] = firsts[place]
        out_ref[base + 3 + places + place] = lengths[place]
        out_ref[base + 3 + 2 * places + place] = near[places + place]
    beside = near[:places] + near[2 * places :]
    if longs == 1:
        beside = [
            jnp.where(reaches_low, low, high)
            for low, high in zip(near[:places], near[2 * places :])
        ]
    for number, segment in enumerate(beside):
        out_ref[base + 3 + 3 * places + number] = jnp.maximum(segment, 0)
    out_ref[base + 3 + 3 * places + len(beside)] = reaches_low.astype(jnp.int32)


def plan(longs, packs, starts, place, segments):
    beside = 3 if longs == 1 else 6
    size = 3 + packs + 3 + 9 + beside + 1
    return kernel_call(
        lambda *refs: plan_body(longs, packs, starts, *refs),
        "plan",
        [array((size,), jnp.int32)],
        [place, segments],
        0,
        in_specs=[SMEM, SMEM],
        out_specs=(SMEM,),
    )[0]


def latents_body(first, scalars, condition_ref, own_ref, near_ref):
    wide = condition_ref[...].astype(F32)
    active = (wide / (1.0 + jnp.exp(-wide))).astype(BF16).astype(F32)
    segments = lax.broadcasted_iota(jnp.int32, active.shape, 0)
    number = 0
    for out in (own_ref, near_ref):
        rows = []
        for _ in range(out.shape[0]):
            chosen = jnp.where(segments == scalars[first + number], active, 0.0)
            rows.append(jnp.sum(chosen, axis=0, keepdims=True))
            number += 1
        out[...] = jnp.concatenate(rows, axis=0).astype(BF16)


def latents(scalars, first, condition, own, near):
    width = condition.shape[1]
    return kernel_call(
        lambda *refs: latents_body(first, *refs),
        "latents",
        [array((own, width), BF16), array((near, width), BF16)],
        [scalars, condition],
        0,
        in_specs=[SMEM, VMEM],
    )


def pick_body(scalars, own_ref, other_ref, out_ref):
    half = own_ref.shape[2]

    def write(low, high):
        out_ref[:, :, :half] = low[...]
        out_ref[:, :, half:] = high[...]

    pl.when(scalars[0] == 0)(lambda: write(own_ref, other_ref))
    pl.when(scalars[0] == 1)(lambda: write(other_ref, own_ref))


def pick(scalars, own, other):
    return kernel_call(
        pick_body,
        "pick",
        [array((*own.shape[:2], 2 * own.shape[2]), F32)],
        [scalars, own, other],
        0,
        in_specs=[SMEM, VMEM, VMEM],
    )[0]


def others_body(first, places, scalars, shares_ref, mod_ref, hidden_ref, down_in_ref):
    entry, core = pl.program_id(0), pl.program_id(1)
    half = hidden_ref.shape[0]
    size = SHORT // 2
    for block in range(half // size):
        rows = pl.ds(block * size, size)
        place = first + entry * places + (core * (half // size) + block) // 2
        normed, _ = layer_norm(shares_ref[rows].astype(F32))
        shift, scale, gate = (mod_ref[place, group : group + 1] for group in (0, 1, 5))
        hidden_ref[rows] = (normed * (1.0 + scale) + shift).astype(BF16)
        upstream = shares_ref[pl.ds(half + block * size, size)].astype(F32)
        down_in_ref[rows] = (gate * upstream).astype(BF16)


def others(scalars, shares, mod_all, first, packs, count):
    width = shares.shape[1]
    shape = ((packs - 1) * count, width)

    def source(r, c, scalars_ref):
        return (jnp.bitwise_xor(scalars_ref[2 + packs], r + 1) * 2 + c, 0)

    half_rows = pl.BlockSpec((count // 2, width), lambda r, c, _: (2 * r + c, 0))
    return pl.pallas_call(
        lambda *refs: others_body(first, count // SHORT, *refs),
        name="others",
        out_shape=(array(shape, BF16), array(shape, BF16)),
        grid_spec=pltpu.PrefetchScalarGridSpec(
            num_scalar_prefetch=1,
            grid=(packs - 1, 2),
            in_specs=[
                pl.BlockSpec((count, width), source),
                pl.BlockSpec(mod_all.shape, lambda r, c, _: (0, 0, 0)),
            ],
            out_specs=(half_rows, half_rows),
        ),
        compiler_params=pltpu.CompilerParams(vmem_limit_bytes=56 << 20),
        cost_estimate=pl.CostEstimate(flops=0, bytes_accessed=0, transcendentals=0),
    )(scalars, shares, mod_all)


def norm_body(own_ref, near_ref, up_ref, mod_ref, hidden_ref, down_in_ref):
    step = pl.program_id(0)
    places = 3
    shift, scale = mod_ref[0, 0:1], mod_ref[0, 1:2]

    def write(rows):
        normed, _ = layer_norm(rows.astype(F32))
        hidden_ref[...] = (normed * (1.0 + scale) + shift).astype(BF16)

    @pl.when(step < places)
    def _():
        write(own_ref[...])
        down_in_ref[...] = (mod_ref[0, 5:6] * up_ref[...].astype(F32)).astype(BF16)

    pl.when(step >= places)(lambda: write(near_ref[...]))


def norm(own, near, upstream, mod_places):
    count, width = own.shape
    places = count // SHORT
    total = count + near.shape[0]

    def own_place(i):
        return (jnp.minimum(i, places - 1), 0)

    return kernel_call(
        norm_body,
        "norm",
        [array((total, width), BF16), array((count, width), BF16)],
        [own, near, upstream, mod_places],
        0,
        grid=(total // SHORT,),
        in_specs=[
            pl.BlockSpec((SHORT, width), own_place),
            pl.BlockSpec((SHORT, width), lambda i: (jnp.maximum(i - places, 0), 0)),
            pl.BlockSpec((SHORT, width), own_place),
            pl.BlockSpec((1, *mod_places.shape[1:]), lambda i: (i, 0, 0)),
        ],
        out_specs=(
            pl.BlockSpec((SHORT, width), lambda i: (i, 0)),
            pl.BlockSpec((SHORT, width), own_place),
        ),
    )


def lay_beside(buffer, own, beside, table):
    count = own.shape[0]
    buffer[count : 2 * count] = own
    if beside.shape[0] == count:
        buffer[pl.ds(aligned(table[0], SHORT), count)] = beside
    else:
        buffer[:count] = beside[:count]
        buffer[2 * count :] = beside[count:]


def attend_body(base, scalars, rows_ref, weight_ref, attended_ref, branch_ref, keys, values, turned):
    count, own_width = attended_ref.shape
    places = count // SHORT
    table = [scalars[base + number] for number in range(3)]
    lay_beside(keys, rows_ref[1, :count], rows_ref[1, count:], table)
    lay_beside(values, rows_ref[2, :count], rows_ref[2, count:], table)

    def attend(place, size):
        near = pl.ds(aligned(scalars[base + 3 + place] * SHORT, SHORT), size)
        rows = pl.ds(aligned(place * SHORT, SHORT), SHORT)
        for head in range(own_width // HEAD_DIM):
            columns = pl.ds(head * HEAD_DIM, HEAD_DIM)
            scores = dot_by(ROWS_BY_ROWS, keys[near, columns], rows_ref[0, rows, columns])
            peak = jnp.max(scores, axis=0, keepdims=True)
            exponent = jnp.exp2((scores - peak) * FACTOR_LOG2)
            total = jnp.sum(exponent, axis=0, keepdims=True)
            probs = (exponent * (1.0 / total)).astype(BF16)
            turned[columns] = dot_by(COLUMNS_BY_COLUMNS, values[near, columns], probs)
        attended_ref[rows] = turned[...].T.astype(BF16)

    def one_place(place, carry):
        is_long = scalars[base + 3 + places + place]
        pl.when(is_long == 1)(lambda: attend(place, LONG))
        pl.when(is_long == 0)(lambda: attend(place, SHORT))
        return carry

    lax.fori_loop(0, places, one_place, 0)
    branch_ref[...] = bf_dot(attended_ref[...], weight_ref[...])


def attend(base, scalars, rows, weight, count):
    own_width, width = weight.shape
    return kernel_call(
        lambda *refs: attend_body(base, *refs),
        "attend",
        [array((count, own_width), BF16), array((count, width), F32)],
        [scalars, rows, weight],
        2 * count * own_width * (width + 2 * LONG),
        far=(2,),
        in_specs=[SMEM, VMEM, VMEM],
        scratch=[
            pltpu.VMEM((3 * count, own_width), BF16),
            pltpu.VMEM((3 * count, own_width), BF16),
            pltpu.VMEM((own_width, SHORT), F32),
        ],
    )


def attend_back_body(base, scalars, rows_ref, grad_ref, near_grad_ref, weight_ref, *rest):
    hidden_grad_ref, bias_ref, pieces = rest[0], rest[1], rest[2:-3]
    held, grads, split = rest[-3:]
    count, own_width = grad_ref.shape
    places = count // SHORT
    table = [scalars[base + number] for number in range(3)]
    for number in range(3):
        lay_beside(held.at[number], rows_ref[number, :count], rows_ref[number, count:], table)
    lay_beside(held.at[3], grad_ref[...], near_grad_ref[...], table)

    def attend_back(first, size):
        rows = pl.ds(aligned(first * SHORT, SHORT), size)
        for head in range(own_width // HEAD_DIM):
            columns = pl.ds(head * HEAD_DIM, HEAD_DIM)
            query, key, value, grad = (held[number, rows, columns] for number in range(4))
            scores = dot_by(ROWS_BY_ROWS, key, query)
            peak = jnp.max(scores, axis=0, keepdims=True)
            exponent = jnp.exp2((scores - peak) * FACTOR_LOG2)
            probs = exponent * (1.0 / jnp.sum(exponent, axis=0, keepdims=True))
            probs_grad = dot_by(ROWS_BY_ROWS, value, grad)
            row_dot = jnp.sum(probs * probs_grad, axis=0, keepdims=True)
            score_grad = (probs * (probs_grad - row_dot)).astype(BF16)
            query_grad = dot_by(COLUMNS_BY_COLUMNS, score_grad, key) * FACTOR
            grads[0, rows, columns] = query_grad.astype(BF16)
            grads[1, rows, columns] = (bf_dot(score_grad, query) * FACTOR).astype(BF16)
            grads[2, rows, columns] = bf_dot(probs.astype(BF16), grad).astype(BF16)

    def short_latent(place, carry):
        is_long = scalars[base + 3 + places + place]
        pl.when(is_long == 0)(lambda: attend_back(places + place, SHORT))
        return carry

    lax.fori_loop(0, places, short_latent, 0)

    def long_latent(number, carry):
        first = scalars[base + 1 + number]
        pl.when(first >= 0)(lambda: attend_back(first, LONG))
        return carry

    lax.fori_loop(0, 2, long_latent, 0)
    own_grads = [grads[number, count : 2 * count] for number in range(3)]
    total = bf_dot(own_grads[0], weight_ref[0])
    for number in range(1, 3):
        total = total + bf_dot(own_grads[number], weight_ref[number])
    hidden_grad_ref[...] = total.astype(BF16)
    for number, grad in enumerate((own_grads[0], own_grads[2])):
        bias_ref[number : number + 1] = jnp.sum(grad.astype(F32), axis=0, keepdims=True)
    share = own_width // len(pieces)
    for number in range(len(pieces)):
        for part in range(3):
            split[number, :, part * share : (part + 1) * share] = own_grads[part][
                :, number * share : (number + 1) * share
            ]
    for entry, piece in enumerate(pieces):
        piece[...] = split[jnp.bitwise_xor(scalars[base - 1], entry)]


def attend_back(base, scalars, rows, grad, near_grad, weight, packs):
    count, own_width = grad.shape
    width = weight.shape[2]
    share = 3 * own_width // packs
    outs = kernel_call(
        lambda *refs: attend_back_body(base, *refs),
        "attend_back",
        [array((count, width), BF16), array((2, own_width), F32)]
        + [array((count, share), BF16)] * packs,
        [scalars, rows, grad, near_grad, weight],
        6 * count * own_width * width + 10 * own_width * LONG * LONG,
        far=(4,),
        in_specs=[SMEM] + [VMEM] * 4,
        scratch=[
            pltpu.VMEM((4, 3 * count, own_width), BF16),
            pltpu.VMEM((3, 3 * count, own_width), BF16),
            pltpu.VMEM((packs, count, share), BF16),
        ],
    )
    return outs[0], outs[1], list(outs[2:])


def whole(shape):
    return pl.BlockSpec(shape, lambda i: (0,) * len(shape))


def feed_up_body(scalars, kept_ref, term_ref, other_ref, bias_ref, mod_ref, *rest):
    weight_ref, hidden_bias_ref, branch_ref, hidden_ref, share_ref, slope_ref = rest[:6]
    gelu_ref, pieces = rest[6], rest[7:]
    step = pl.program_id(0)
    size = weight_ref.shape[1]

    @pl.when(step == 0)
    def _():
        def place(number, carry):
            rows = pl.ds(aligned(number * SHORT, SHORT), SHORT)
            branch = (term_ref[rows] + other_ref[rows]) + bias_ref[...]
            branch_ref[rows] = branch
            middle = kept_ref[rows].astype(F32) + mod_ref[number, 2:3] * branch
            normed, _ = layer_norm(middle)
            shift, scale = mod_ref[number, 3:4], mod_ref[number, 4:5]
            hidden_ref[rows] = (normed * (1.0 + scale) + shift).astype(BF16)
            return carry

        lax.fori_loop(0, kept_ref.shape[0] // SHORT, place, 0)
        start = aligned(scalars[0] * (hidden_ref.shape[1] - share_ref.shape[1]))
        share_ref[...] = hidden_ref[:, pl.ds(start, share_ref.shape[1])]

    gelu, slope = gelu_pair(bf_dot(hidden_ref[...], weight_ref[...]) + hidden_bias_ref[...])
    slope_ref[...] = slope
    gelu_ref[:, pl.ds(aligned(step * size), size)] = gelu.astype(BF16)

    @pl.when(step == pl.num_programs(0) - 1)
    def _():
        for entry, piece in enumerate(pieces):
            piece[...] = gelu_ref[:, pl.ds(aligned(scalars[2 + entry]), piece.shape[1])]


def feed_up(scalars, kept, term, other, bias, mod_places, weight, hidden_bias, packs):
    count, width = kept.shape
    hidden = weight.shape[1]
    size = hidden // 3
    window = windows(hidden, packs)[1]
    outs = [
        array((count, width), F32),
        array((count, width), BF16),
        array((count, half_width(width)), BF16),
        array((count, hidden), F32),
        array((count, hidden), BF16),
    ] + [array((count, window), BF16)] * packs
    out_specs = [whole(out.shape) for out in outs]
    out_specs[3] = pl.BlockSpec((count, size), lambda i: (0, i))
    result = kernel_call(
        feed_up_body,
        "feed_up",
        outs,
        [scalars, kept, term, other, bias, mod_places, weight, hidden_bias],
        2 * count * width * hidden,
        far=(6,),
        grid=(hidden // size,),
        in_specs=[
            SMEM,
            *[whole(a.shape) for a in (kept, term, other, bias, mod_places)],
            pl.BlockSpec((width, size), lambda i: (0, i)),
            pl.BlockSpec((1, size), lambda i: (0, i)),
        ],
        out_specs=tuple(out_specs),
    )
    return *result[:5], list(result[5:])


def feed_back_body(scalars, down_in_ref, down_ref, slope_ref, weight_ref, *rest):
    back_ref, sums_ref, pieces, pre_rows = rest[0], rest[1], rest[2:-1], rest[-1]
    step = pl.program_id(0)
    size = weight_ref.shape[1]
    pre_grad = dot_by(ROWS_BY_ROWS, down_in_ref[...], down_ref[...]) * slope_ref[...]
    pre_grad = pre_grad.astype(BF16)
    pre_rows[:, pl.ds(aligned(step * size), size)] = pre_grad
    sums_ref[...] = jnp.sum(pre_grad.astype(F32), axis=0, keepdims=True)
    back = dot_by(ROWS_BY_ROWS, pre_grad, weight_ref[...])

    @pl.when(step == 0)
    def _():
        back_ref[...] = back

    @pl.when(step > 0)
    def _():
        back_ref[...] += back

    @pl.when(step == pl.num_programs(0) - 1)
    def _():
        for entry, piece in enumerate(pieces):
            piece[...] = pre_rows[:, pl.ds(aligned(scalars[2 + entry]), piece.shape[1])]


def feed_back(scalars, down_in, down, slope, weight, packs):
    count, width = down_in.shape
    hidden = weight.shape[1]
    size = hidden // 3
    window = windows(hidden, packs)[1]
    outs = [array((count, width), F32), array((1, hidden), F32)]
    outs += [array((count, window), BF16)] * packs
    out_specs = [whole(out.shape) for out in outs]
    out_specs[1] = pl.BlockSpec((1, size), lambda i: (0, i))
    result = kernel_call(
        feed_back_body,
        "feed_back",
        outs,
        [scalars, down_in, down, slope, weight],
        4 * count * width * hidden,
        far=(2, 4),
        grid=(hidden // size,),
        in_specs=[
            SMEM,
            whole(down_in.shape),
            pl.BlockSpec((size, width), lambda i: (i, 0)),
            pl.BlockSpec((count, size), lambda i: (0, i)),
            pl.BlockSpec((width, size), lambda i: (0, i)),
        ],
        out_specs=tuple(out_specs),
        scratch=[pltpu.VMEM((count, hidden), BF16)],
    )
    return result[0], result[1], list(result[2:])


def middle_back_body(term_ref, other_ref, branch_ref, kept_ref, up_ref, mod_ref, *rest):
    weight_ref, middle_grad_ref, branch_grad_ref, attended_ref, sums_ref, bias_ref = rest
    hidden_grad = term_ref[...] + other_ref[...]
    branch = branch_ref[...]
    gate = mod_ref[0, 2:3]
    normed, inverse = layer_norm(kept_ref[...].astype(F32) + gate * branch)
    middle_grad = up_ref[...].astype(F32) + norm_back(
        hidden_grad * (1.0 + mod_ref[0, 4:5]), normed, inverse
    )
    middle_grad_ref[...] = middle_grad
    branch_grad = (gate * middle_grad).astype(BF16)
    branch_grad_ref[...] = branch_grad
    attended_ref[...] = dot_by(ROWS_BY_ROWS, branch_grad, weight_ref[...]).astype(BF16)
    bias_ref[0] = jnp.sum(branch_grad.astype(F32), axis=0, keepdims=True)
    sums_ref[0, 0:1] = jnp.sum(middle_grad * branch, axis=0, keepdims=True)
    sums_ref[0, 1:2] = jnp.sum(hidden_grad, axis=0, keepdims=True)
    sums_ref[0, 2:3] = jnp.sum(hidden_grad * normed, axis=0, keepdims=True)


def by_place(body, name, outs, args, flops, far=()):
    places = args[0].shape[0] // SHORT

    def spec(a):
        if a.shape[0] == places * SHORT and len(a.shape) == 2:
            return pl.BlockSpec((SHORT, a.shape[1]), lambda i: (i, 0))
        if a.shape[0] == places and len(a.shape) == 3:
            return pl.BlockSpec((1, *a.shape[1:]), lambda i: (i, 0, 0))
        return pl.BlockSpec(a.shape, lambda i: (0,) * len(a.shape))

    return kernel_call(
        body,
        name,
        outs,
        args,
        flops,
        far=far,
        grid=(places,),
        in_specs=[spec(a) for a in args],
        out_specs=tuple(spec(a) for a in outs),
    )


def middle_back(term, other, branch, kept, upstream, mod_places, weight):
    count, width = kept.shape
    places = count // SHORT
    return by_place(
        middle_back_body,
        "middle_back",
        [
            array((count, width), F32),
            array((count, width), BF16),
            array((count, weight.shape[0]), BF16),
            array((places, 3, width), F32),
            array((places, 1, width), F32),
        ],
        [term, other, branch, kept, upstream, mod_places, weight],
        2 * count * width * weight.shape[0],
        far=(6,),
    )


def input_back_body(term_ref, other_ref, middle_grad_ref, kept_ref, mod_ref, grad_ref, sums_ref):
    hidden_grad = term_ref[...].astype(F32) + other_ref[...].astype(F32)
    normed, inverse = layer_norm(kept_ref[...].astype(F32))
    grad = middle_grad_ref[...] + norm_back(hidden_grad * (1.0 + mod_ref[0, 1:2]), normed, inverse)
    grad_ref[...] = grad.astype(BF16)
    sums_ref[0, 0:1] = jnp.sum(hidden_grad, axis=0, keepdims=True)
    sums_ref[0, 1:2] = jnp.sum(hidden_grad * normed, axis=0, keepdims=True)


def input_back(term, other, middle_grad, kept, mod_places):
    count, width = kept.shape
    return by_place(
        input_back_body,
        "input_back",
        [array((count, width), BF16), array((count // SHORT, 2, width), F32)],
        [term, other, middle_grad, kept, mod_places],
        0,
    )


def result_body(term_ref, other_ref, bias_ref, branch_ref, kept_ref, up_ref, mod_ref, *rest):
    result_ref, sums_ref, bias_grad_ref = rest
    branch_two = term_ref[...].astype(F32) + other_ref[...].astype(F32) + bias_ref[...]
    middle = kept_ref[...].astype(F32) + mod_ref[0, 2:3] * branch_ref[...]
    gate = mod_ref[0, 5:6]
    upstream = up_ref[...].astype(F32)
    result_ref[...] = (middle + gate * branch_two).astype(BF16)
    sums_ref[0, 0:1] = jnp.sum(upstream * branch_two, axis=0, keepdims=True)
    down_in = (gate * upstream).astype(BF16).astype(F32)
    bias_grad_ref[0] = jnp.sum(down_in, axis=0, keepdims=True)


def result(term, other, bias, branch, kept, upstream, mod_places):
    count, width = kept.shape
    places = count // SHORT
    return by_place(
        result_body,
        "result",
        [
            array((count, width), BF16),
            array((places, 1, width), F32),
            array((places, 1, width), F32),
        ],
        [term, other, bias, branch, kept, upstream, mod_places],
        0,
    )


def weight_grad_body(packs, offset, count_shares, scalars, *refs):
    shares, refs = refs[:count_shares], refs[count_shares:]
    columns, refs = refs[:packs], refs[packs:]
    outs, (rows_all, columns_all, total) = refs[:-3], refs[-3:]
    count, wide = columns[0].shape
    width = rows_all.shape[1]
    half = half_width(width)
    for entry in range(packs):
        rows = pl.ds(entry * count, count)
        columns_all[rows] = columns[entry][...]
        if count_shares == 1:
            source = jnp.bitwise_xor(scalars[2 + packs], entry) * (2 * count)
            low = pl.ds(aligned(source, SHORT), count)
            high = pl.ds(aligned(source + count, SHORT), count)
            rows_all[rows, :half] = shares[0][low, offset : offset + half]
            rows_all[rows, half:] = shares[0][high, offset + 2 * half - width : offset + half]
        elif entry == 0:
            rows_all[rows] = shares[0][:count]
        else:
            rows_all[rows] = shares[1][(entry - 1) * count : entry * count]
    if len(outs) == 1:
        outs[0][...] = dot_by(COLUMNS_BY_COLUMNS, rows_all[...], columns_all[...]).astype(BF16)
        return
    total[:, :wide] = dot_by(COLUMNS_BY_COLUMNS, rows_all[...], columns_all[...])
    if total.shape[1] > wide:
        others, outs = outs[:packs], outs[packs:]
        other = others[0][...].astype(F32)
        for entry in range(1, packs):
            other = other + others[entry][...].astype(F32)
        total[:, wide:] = other.T
    cut_by_blk(scalars, total, outs)


def cut_by_blk(scalars, total, outs):
    blocks = len(outs)
    size = total.shape[0] // blocks
    for step in range(blocks):
        target = lax.rem(scalars[1] + step, blocks)
        piece = total[pl.ds(aligned(target * size, 8), size)]
        outs[step][...] = piece.astype(outs[step].dtype)


def cut_shapes(width, wide, blocks):
    size = width // blocks
    return [array((size, wide), F32)] + [array((size, wide), BF16)] * (blocks - 1)


def weight_grad(scalars, width, offset, shares, columns, others=(), blocks=1):
    packs = len(columns)
    count, wide = columns[0].shape
    total = wide + (others[0].shape[0] if others else 0)
    outs = [array((width, wide), BF16)]
    if blocks > 1:
        outs = cut_shapes(width, total, blocks)
    return kernel_call(
        lambda *refs: weight_grad_body(packs, offset, len(shares), *refs),
        "weight_grad",
        outs,
        [scalars, *shares, *columns, *others],
        2 * packs * count * width * wide,
        in_specs=[SMEM] + [VMEM] * (packs + len(shares) + len(others)),
        scratch=[
            pltpu.VMEM((packs * count, width), BF16),
            pltpu.VMEM((packs * count, wide), BF16),
            pltpu.VMEM((width, total), F32),
        ],
    )


def own_weight_grad_body(packs, scalars, rows_ref, columns_ref, *refs):
    pieces, total = refs[:-1], refs[-1]
    total[...] = dot_by(COLUMNS_BY_COLUMNS, rows_ref[...], columns_ref[...])
    size = total.shape[0] // packs
    for entry, piece in enumerate(pieces):
        start = jnp.bitwise_xor(scalars[2 + packs], entry) * size
        piece[...] = total[pl.ds(aligned(start, 8), size)].astype(BF16)


def own_weight_grad(scalars, rows, columns, packs):
    shape = (rows.shape[1], columns.shape[1])
    return kernel_call(
        lambda *refs: own_weight_grad_body(packs, *refs),
        "own_weight_grad",
        [array((shape[0] // packs, shape[1]), BF16)] * packs,
        [scalars, rows, columns],
        2 * rows.shape[0] * math.prod(shape),
        in_specs=[SMEM, VMEM, VMEM],
        scratch=[pltpu.VMEM(shape, F32)],
    )


def join_body(kind, starts, packs, scalars, *refs):
    outs, held = refs[1:-1], refs[-1]
    size = refs[0].shape[0] // packs
    stacked = kind == "hidden"
    if not stacked:
        entries, outs = refs[:packs], refs[packs:-1]
        for entry in range(packs):
            held[entry] = entries[entry][...]
    for number in range(packs):
        if stacked:
            piece = refs[0][number * size : (number + 1) * size].astype(F32)
        else:
            piece = held[jnp.bitwise_xor(scalars[2 + packs], number)].astype(F32)
        if kind == "qkv":
            share = piece.shape[1] // 4
            columns = pl.ds(number * share, share)
            for part in range(3):
                outs[0][part, :, columns] = piece[:, part * share : (part + 1) * share]
            outs[1][:, columns] = piece[:, 3 * share :]
        else:
            end = [*starts[1:], outs[0].shape[1]][number]
            outs[0][:, starts[number] : end] = piece[:, : end - starts[number]]


def join(kind, scalars, entries, packs, shapes, starts=()):
    return kernel_call(
        lambda *refs: join_body(kind, starts, packs, *refs),
        "join_" + kind,
        [array(shape, F32) for shape in shapes],
        [scalars, *entries],
        0,
        in_specs=[SMEM] + [VMEM] * len(entries),
        scratch=[pltpu.VMEM((packs, *entries[0].shape), BF16)],
    )


def collect_body(scalars, input_ref, middle_ref, two_ref, active_ref, *refs):
    qkv_ref, output_ref, hidden_ref, down_ref, out_ref, held = refs
    places, _, width = middle_ref.shape
    half = width // 2
    row = 0

    def put(value):
        nonlocal row
        held[row : row + 1] = value
        row += 1

    def put_twice(value):
        high = value.astype(BF16).astype(F32)
        put(high)
        put(value - high)

    def put_sums(start):
        nonlocal row
        row = 0
        for place in range(places):
            for source in (input_ref, middle_ref, two_ref):
                for number in range(source.shape[1]):
                    put(source[place, number : number + 1, start : start + half])

    held[...] = jnp.zeros_like(held)
    pl.when(scalars[0] == 0)(lambda: put_sums(0))
    pl.when(scalars[0] == 1)(lambda: put_sums(half))
    for place in range(places):
        active = active_ref[place : place + 1].astype(F32)
        put(active[:, :half])
        put(active[:, half:])
    put_twice(qkv_ref[0:1])
    put_twice(qkv_ref[1:2])
    for number in range(hidden_ref.shape[1] // half):
        put_twice(hidden_ref[:, number * half : (number + 1) * half])
    for source in (output_ref, down_ref):
        total = jnp.sum(source[...], axis=0)
        put_twice(total[:, :half])
        put_twice(total[:, half:])
    out_ref[...] = held[...].astype(BF16)


def collect(scalars, *args):
    places, _, width = args[0].shape
    hidden = args[6].shape[1]
    used = places * 8 + 2 * (2 + 2 * hidden // width + 4)
    size = -(-used // 16) * 16
    return kernel_call(
        collect_body,
        "collect",
        [array((size, width // 2), BF16)],
        [scalars, *args],
        0,
        in_specs=[SMEM] + [VMEM] * len(args),
        scratch=[pltpu.VMEM((size, width // 2), F32)],
    )[0]


def spread_body(packs, blocks, places, size, scalars, segments, *refs):
    entries = refs[:packs]
    weight_ref, bias_ref, biases_ref, grad_ref, held, rows_all, active, sums = refs[packs:]
    half = weight_ref.shape[2]
    rows = weight_ref.shape[1]
    pack = scalars[2 + packs]
    for entry in range(packs):
        held[entry] = entries[entry][...].reshape(blocks, size, half)
    for number in range(packs):
        for block in range(blocks):
            piece = held[jnp.bitwise_xor(pack, number), jnp.bitwise_xor(scalars[1], block)]
            rows_all[number * blocks + block] = piece.astype(F32)
    cut = 6 * places
    devices = packs * blocks

    def take_active(block):
        start = block * rows
        for device in range(devices):
            for place in range(places):
                row = cut + 2 * place
                whole_row = jnp.concatenate(
                    [rows_all[device, row : row + 1], rows_all[device, row + 1 : row + 2]], axis=1
                )
                number = device * places + place
                active[number : number + 1] = whole_row[:, start : start + rows]

    for block in range(blocks):
        pl.when(scalars[1] == block)(lambda: take_active(block))
    own_active = active[...].astype(BF16)
    for group in range(6):
        for device in range(devices):
            for place in range(places):
                number = device * places + place
                row = place * 6 + group
                sums[number : number + 1] = rows_all[device, row : row + 1]
        values = sums[...]
        bias_ref[group : group + 1] = jnp.sum(values, axis=0, keepdims=True)
        weight_ref[group] = dot_by(COLUMNS_BY_COLUMNS, own_active, values.astype(BF16))
    first = cut + 2 * places
    total = rows_all[0, first:]
    for device in range(1, devices):
        total = total + rows_all[device, first:]
    biases_ref[...] = total
    grad_ref[...] = jnp.zeros_like(grad_ref)
    for block in range(blocks):
        for place in range(places):
            segment = segments[(block * places + place) * SHORT]
            own = rows_all[pack * blocks + block, place * 6 : place * 6 + 6]
            grad_ref[segment] = grad_ref[segment] + own


def spread(scalars, segments, entries, packs, blocks, places, seg_count, width):
    devices = packs * blocks
    size = entries[0].shape[0] // blocks
    half = entries[0].shape[1]
    return kernel_call(
        lambda *refs: spread_body(packs, blocks, places, size, *refs),
        "spread",
        [
            array((6, width // blocks, half), F32),
            array((6, half), F32),
            array((size - 8 * places, half), F32),
            array((seg_count, 6, half), F32),
        ],
        [scalars, segments, *entries],
        0,
        in_specs=[SMEM, SMEM] + [VMEM] * packs,
        scratch=[
            pltpu.VMEM((packs, blocks, size, half), BF16),
            pltpu.VMEM((devices, size, half), F32),
            pltpu.VMEM((devices * places, width // blocks), F32),
            pltpu.VMEM((devices * places, half), F32),
        ],
    )


def xor_permute(block, axis, bits):
    return lax.ppermute(block, axis, [(i, i ^ bits) for i in range(lax.axis_size(axis))])


def swap(block):
    return xor_permute(block, "head", 1)


def move(block, step):
    count = lax.axis_size("blk")
    pairs = [(i, i + step) for i in range(count) if 0 <= i + step < count]
    return lax.ppermute(block, "blk", pairs)


def gather_xor(block, axis, turned=False):
    bits = [1 << b for b in range((lax.axis_size(axis) - 1).bit_length())]
    held = {0: block}
    for bit in bits[::-1] if turned else bits:
        for entry in list(held):
            held[entry ^ bit] = xor_permute(held[entry], axis, bit)
    return [held[entry] for entry in range(lax.axis_size(axis))]


def gather_each(block, axis):
    return [block] + [xor_permute(block, axis, r) for r in range(1, lax.axis_size(axis))]


def in_order(entries, axis):
    order = jnp.arange(len(entries), dtype=jnp.int32) ^ lax.axis_index(axis)
    return jnp.take(jnp.stack(entries), order, axis=0)


def trade(pieces, axis, entries):
    return {r: xor_permute(pieces[r], axis, r) for r in entries}


def windows(width, parts):
    tiles = width // LANES
    size = -(-tiles // parts)
    return [LANES * (q * (tiles - size) // (parts - 1)) for q in range(parts)], size * LANES


def half_width(width):
    return -(-width // (2 * LANES)) * LANES


def share_of(block):
    half = half_width(block.shape[1])
    first, last = block[:, :half], block[:, block.shape[1] - half :]
    return jnp.where(lax.axis_index("head") == 0, first, last)


def gather_shares(share):
    return lax.all_gather(share, ("pack", "head"), axis=0, tiled=True)


def hold(values, *after):
    flat, tree = jax.tree.flatten(values)
    held = lax.optimization_barrier((*flat, *after))
    return jax.tree.unflatten(tree, held[: len(flat)])


def send_blk(pieces):
    count = len(pieces)
    found = [pieces[0]]
    for step in range(1, count):
        pairs = [(i, (i + step) % count) for i in range(count)]
        found.append(lax.ppermute(pieces[step], "blk", pairs))
    return found


def add_blk(found):
    total = found[0]
    for piece in found[1:]:
        total = total + piece.astype(F32)
    return total.astype(BF16)


def local(
    tokens_full,
    condition,
    kept_index,
    segment_ids,
    cotangent,
    qkv_weight,
    query_value_bias,
    output_weight,
    output_bias,
    hidden_weight,
    hidden_bias,
    down_weight,
    down_bias,
    modulation_weight,
    modulation_bias,
):
    width = tokens_full.shape[2]
    own_width = qkv_weight.shape[2]
    hidden = hidden_weight.shape[1]
    count = kept_index.shape[1]
    seg_count = condition.shape[1]
    places = count // SHORT
    longs = (segment_ids.shape[1] - SHORT * seg_count) // (LONG - SHORT)
    packs = lax.axis_size("pack")
    blocks = lax.axis_size("blk")
    blk = lax.axis_index("blk")
    core = lax.axis_index("head")
    pack = lax.axis_index("pack")

    modulation_turned = jnp.transpose(modulation_weight, (1, 2, 0))
    starts, window = windows(hidden, packs)
    place = jnp.stack([core, blk, pack, jnp.int32(blocks)]).astype(jnp.int32)
    scalars = plan(longs, packs, starts, place, segment_ids[0])
    base = 3 + packs
    own_active, near_active = latents(
        scalars, base + 3 + 2 * places, condition[0], places, places if longs == 1 else 2 * places
    )
    local_index, own_active = hold((kept_index[0] - blk * (2 * count), own_active))
    full_rows = tokens_full[0]
    cot_rows = cotangent[0]
    picker = (
        local_index[:, None] == jnp.arange(full_rows.shape[0], dtype=jnp.int32)[None, :]
    ).astype(BF16)
    kept_rows = bf_dot(picker, full_rows).astype(BF16)
    upstream = bf_dot(picker, cot_rows).astype(BF16)

    reaches_low = scalars[-1] == 1

    def beside(block):
        low, high = move(block, 1), move(block, -1)
        if longs == 1:
            return jnp.where(reaches_low, low, high)
        return jnp.concatenate([low, high], axis=0)

    half = count // 2
    kept_half = lax.dynamic_slice_in_dim(kept_rows, core * half, half, 0)
    near_half = beside(kept_half)
    token_shares = gather_shares(
        jnp.concatenate(
            [kept_half, lax.dynamic_slice_in_dim(upstream, core * half, half, 0)], axis=0
        )
    )
    other_half = swap(near_half)
    first = jnp.where(core == 0, near_half, other_half).reshape(-1, half, width)
    second = jnp.where(core == 0, other_half, near_half).reshape(-1, half, width)
    near_rows = jnp.concatenate([first, second], axis=1).reshape(-1, width)

    near_count = near_rows.shape[0] // SHORT
    other_active = list(trade([own_active] * packs, "pack", range(1, packs)).values())
    mod_own = (
        jnp.einsum(
            "sd,gfd->sgf",
            jnp.concatenate([own_active, near_active, *other_active], axis=0),
            modulation_turned,
            preferred_element_type=F32,
        )
        + modulation_bias.astype(F32)[None]
    )
    mod_all = pick(scalars, mod_own, swap(mod_own))
    mod_places = mod_all[:places]
    wide_bias = query_value_bias.astype(F32)
    qkv_bias = jnp.stack([wide_bias[0], jnp.zeros_like(wide_bias[0]), wide_bias[1]])[:, None]
    hidden_rows, down_in = norm(kept_rows, near_rows, upstream, mod_all)
    qkv_turned = jnp.transpose(qkv_weight, (1, 2, 0))
    projected = jnp.einsum("td,gfd->gtf", hidden_rows, qkv_turned, preferred_element_type=F32)
    qkv_rows = (projected + qkv_bias).astype(BF16)

    attended, branch_term = attend(base, scalars, qkv_rows, output_weight, count)
    branch_one, hidden_two, hidden_two_share, slope, gelu, gelu_pieces = feed_up(
        scalars,
        kept_rows,
        branch_term,
        swap(branch_term),
        output_bias.astype(F32)[None],
        mod_places,
        hidden_weight,
        hidden_bias.astype(F32)[None],
        packs,
    )
    one_step = [r for r in range(1, packs) if r & (r - 1) == 0]
    further = [r for r in range(1, packs) if r & (r - 1)]

    def by_entry(pieces, *parts):
        found = {0: pieces[0]}
        for part in parts:
            found.update(part)
        return [found[r] for r in range(packs)]

    hidden_two_shares = gather_shares(hidden_two_share)
    gelu_first = trade(gelu_pieces, "pack", one_step)
    back_term, hidden_sums, pre_pieces = feed_back(
        scalars, down_in, down_weight, slope, hidden_weight, packs
    )
    back_term, gelu_first, gelu_pieces, pre_pieces = hold(
        (back_term, gelu_first, gelu_pieces, pre_pieces)
    )
    gelu_last = trade(gelu_pieces, "pack", further)
    middle_grad, branch_grad, attended_grad, middle_sums, output_sums = middle_back(
        back_term, swap(back_term), branch_one, kept_rows, upstream, mod_places, output_weight
    )
    attended_grad, token_shares, pre_pieces, gelu, branch_grad = hold(
        (attended_grad, token_shares, pre_pieces, gelu, branch_grad)
    )
    near_grad = beside(attended_grad)
    rows = width // blocks

    pre_first = trade(pre_pieces, "pack", range(1, packs))
    gelu_all = by_entry(gelu_pieces, gelu_first, gelu_last)
    hidden_other_packs, down_other_packs = others(
        scalars, token_shares, mod_all, places + near_count, packs, count
    )
    down_raw = weight_grad(scalars, width, 0, [down_in, down_other_packs], gelu_all)[0]
    output_pieces = own_weight_grad(scalars, attended, branch_grad, packs)
    near_grad, down_raw, output_pieces, pre_first = hold(
        (near_grad, down_raw, output_pieces, pre_first)
    )
    down_term = lax.psum_scatter(down_raw, "blk", scatter_dimension=0, tiled=True)
    output_first = trade(output_pieces, "pack", one_step)
    hidden_term, qkv_sums, qkv_pieces = attend_back(
        base, scalars, qkv_rows, attended_grad, near_grad, qkv_turned, packs
    )
    hidden_term, qkv_pieces, output_first, output_pieces, gelu, pre_first = hold(
        (hidden_term, qkv_pieces, output_first, output_pieces, gelu, pre_first)
    )
    qkv_first = trade(qkv_pieces, "pack", one_step)
    qkv_last = trade(qkv_pieces, "pack", further)
    output_last = trade(output_pieces, "pack", further)

    pre_all = by_entry(pre_pieces, pre_first)
    hidden_raw = weight_grad(scalars, width, 0, [hidden_two_shares], pre_all)[0]
    hidden_reduced = lax.psum_scatter(hidden_raw, "blk", scatter_dimension=0, tiled=True)
    hidden_other, qkv_first, output_last, hidden_raw, gelu = hold(
        (swap(hidden_term), qkv_first, output_last, hidden_raw, gelu)
    )
    input_grad, input_sums = input_back(
        hidden_term, hidden_other, middle_grad, kept_rows, mod_places
    )
    two_term = bf_dot(gelu, down_weight).astype(BF16)
    result_rows, two_sums, down_sums = result(
        two_term,
        swap(two_term),
        down_bias.astype(F32)[None],
        branch_one,
        kept_rows,
        upstream,
        mod_places,
    )
    sent = collect(
        scalars,
        input_sums,
        middle_sums,
        two_sums,
        own_active,
        qkv_sums,
        output_sums,
        hidden_sums,
        down_sums,
    )
    qkv_last, sent = hold((qkv_last, sent))
    by_blk = gather_each(sent, "blk")
    qkv_terms = weight_grad(
        scalars,
        width,
        0,
        [hidden_rows, hidden_other_packs],
        by_entry(qkv_pieces, qkv_first, qkv_last),
        by_entry(output_pieces, output_first, output_last),
        blocks,
    )
    qkv_terms, by_blk, result_rows, input_grad, down_term = hold(
        (qkv_terms, by_blk, result_rows, input_grad, down_term)
    )

    def put_rows(base, rows):
        spread = dot_by(COLUMNS_BY_COLUMNS, picker, rows)
        kept = jnp.max(picker, axis=0)[:, None] > 0
        return jnp.where(kept, spread.astype(BF16), base)[None]

    qkv_found = send_blk(qkv_terms)
    entries = gather_each(jnp.concatenate(by_blk, axis=0), "pack")
    down_entries = gather_each(down_term, "pack")
    block_output = put_rows(full_rows, result_rows)
    tokens_grad = put_rows(cot_rows, input_grad)
    qkv_found, entries, block_output, tokens_grad, down_entries = hold(
        (qkv_found, entries, block_output, tokens_grad, down_entries)
    )
    qkv_entries = gather_each(add_blk(qkv_found), "pack")
    hidden_gathered = lax.all_gather(hidden_reduced, "pack", axis=0, tiled=True)
    modulation_weight_grad, modulation_bias_grad, biases, mod_grad = spread(
        scalars, segment_ids[0], entries, packs, blocks, places, seg_count, width
    )
    qkv_weight_grad, output_weight_grad = join(
        "qkv", scalars, qkv_entries, packs, [(3, rows, own_width), (rows, own_width)]
    )
    down_weight_grad = join(
        "down",
        scalars,
        down_entries,
        packs,
        [(rows, hidden)],
        starts,
    )[0].T
    hidden_weight_grad = join(
        "hidden", scalars, [hidden_gathered], packs, [(rows, hidden)], starts
    )[0]
    output_weight_grad = output_weight_grad.T
    qkv_weight_grad = jnp.swapaxes(qkv_weight_grad, 0, 1)
    modulation_weight_grad = jnp.swapaxes(modulation_weight_grad, 0, 1)
    mod_high = mod_grad.astype(BF16)
    mod_low = (mod_grad - mod_high.astype(F32)).astype(BF16)
    cond_terms = jnp.einsum(
        "sgf,gfd->sd",
        jnp.concatenate([mod_high, mod_low], axis=0),
        modulation_turned,
        preferred_element_type=F32,
    )
    cond_term = cond_terms[:seg_count] + cond_terms[seg_count:]
    cond_total = cond_term + swap(cond_term)
    cond_rows = condition[0].astype(F32)
    squashed = jax.nn.sigmoid(cond_rows)
    condition_grad = (cond_total * squashed * (1.0 + cond_rows * (1.0 - squashed)))[None]

    def bias_rows(first, number):
        pairs = biases[2 * first : 2 * (first + number)].reshape(number, 2, own_width)
        return (pairs[:, 0] + pairs[:, 1]).reshape(-1)

    value_bias = bias_rows(0, 2).reshape(2, own_width)
    hidden_rows_count = hidden // own_width
    return (
        block_output,
        tokens_grad,
        condition_grad,
        qkv_weight_grad,
        value_bias,
        output_weight_grad,
        bias_rows(2 + hidden_rows_count, 2),
        hidden_weight_grad,
        bias_rows(2, hidden_rows_count),
        down_weight_grad,
        bias_rows(4 + hidden_rows_count, 2),
        modulation_weight_grad,
        modulation_bias_grad,
    )


def solution(mesh):
    in_specs = (
        P("pack", "blk", None),
        P("pack", None, None),
        P("pack", "blk"),
        P("pack", None),
        P("pack", "blk", None),
        P(None, None, "head"),
        P(None, "head"),
        P("head", None),
        P(),
        P(None, "head"),
        P("head"),
        P("head", None),
        P(),
        P(None, None, "head"),
        P(None, "head"),
    )
    out_specs = (
        P("pack", "blk", None),
        P("pack", "blk", None),
        P("pack", None, None),
        P("blk", None, "head"),
        P(None, "head"),
        P("head", "blk"),
        P(),
        P("blk", "head"),
        P("head"),
        P("head", "blk"),
        P(),
        P("blk", None, "head"),
        P(None, "head"),
    )
    return jax.shard_map(local, mesh=mesh, in_specs=in_specs, out_specs=out_specs, check_vma=False)
```

```python
import math

import jax
import jax.numpy as jnp
from jax import lax
from jax.experimental import pallas as pl
from jax.experimental.pallas import tpu as pltpu
from jax.sharding import PartitionSpec as P

HEAD_DIM = 72
SHORT = 128
LONG = 4 * SHORT
LANES = 128
EPSILON = 1e-06
FACTOR = 1.0 / math.sqrt(HEAD_DIM)
FACTOR_LOG2 = FACTOR * math.log2(math.e)
GELU_SLOPE = math.sqrt(2.0 / math.pi)
GELU_CUBE = 0.044715
F32 = jnp.float32
BF16 = jnp.bfloat16
ROWS_BY_ROWS = (((1,), (1,)), ((), ()))
COLUMNS_BY_COLUMNS = (((0,), (0,)), ((), ()))
VMEM = pl.BlockSpec(memory_space=pltpu.VMEM)
SMEM = pl.BlockSpec(memory_space=pltpu.SMEM)


def bf_dot(operand_a, operand_b):
    return jnp.dot(operand_a, operand_b, preferred_element_type=F32)


def dot_by(dims, operand_a, operand_b):
    return lax.dot_general(operand_a, operand_b, dims, preferred_element_type=F32)


def array(shape, kind):
    return jax.ShapeDtypeStruct(shape, kind)


SLOW = 1000


def kernel_call(
    body, name, outs, args, flops, grid=(), in_specs=None, out_specs=None, scratch=(), far=(), vmem=48
):
    args = [
        pltpu.with_memory_space_constraint(a, pltpu.HBM) if number in far else a
        for number, a in enumerate(args)
    ]
    moved = sum(math.prod(a.shape) * a.dtype.itemsize for a in (*args, *outs))
    return pl.pallas_call(
        body,
        name=name,
        out_shape=tuple(outs),
        grid=grid,
        in_specs=in_specs or [VMEM] * len(args),
        out_specs=out_specs or (VMEM,) * len(outs),
        scratch_shapes=scratch,
        compiler_params=pltpu.CompilerParams(vmem_limit_bytes=vmem << 20),
        cost_estimate=pl.CostEstimate(
            flops=int(flops) // SLOW, bytes_accessed=int(moved) // SLOW, transcendentals=0
        ),
    )(*args)


def aligned(index, to=LANES):
    return pl.multiple_of(index, to)


def layer_norm(values):
    center = values - jnp.mean(values, axis=-1, keepdims=True)
    spread = jnp.mean(center * center, axis=-1, keepdims=True)
    inverse = lax.rsqrt(spread + EPSILON)
    return (center * inverse, inverse)


def norm_back(upstream, normed, inverse):
    mean_grad = jnp.mean(upstream, axis=-1, keepdims=True)
    mean_cross = jnp.mean(upstream * normed, axis=-1, keepdims=True)
    return inverse * (upstream - mean_grad - normed * mean_cross)


def gelu_pair(value):
    square = value * value
    bent = jnp.tanh(GELU_SLOPE * (value + GELU_CUBE * (value * square)))
    half = 0.5 * (1.0 + bent)
    slope = GELU_SLOPE * (1.0 + (3.0 * GELU_CUBE) * square)
    return value * half, half + 0.5 * value * (1.0 - bent * bent) * slope


def plan_body(longs, packs, starts, place_ref, segments, out_ref):
    core, blk, pack, blocks = (place_ref[number] for number in range(4))
    places = 3
    out_ref[0] = core
    out_ref[1] = blk
    for entry in range(packs):
        window = jnp.bitwise_xor(pack, entry)
        start = jnp.int32(0)
        for number in range(packs):
            start = jnp.where(window == number, starts[number], start)
        out_ref[2 + entry] = start
    out_ref[2 + packs] = pack
    near = []
    for number in range(3 * places):
        index = (blk - 1) * places + number
        inside = jnp.logical_and(index >= 0, index < blocks * places)
        found = segments[jnp.clip(index, 0, blocks * places - 1) * SHORT]
        near.append(jnp.where(inside, found, -1))
    reaches_low = near[places - 1] == near[places]
    reaches_high = near[2 * places - 1] == near[2 * places]
    base = 3 + packs
    firsts, lengths = [], []
    for place in range(places):
        own = near[places + place]
        first = jnp.int32(0)
        length = jnp.int32(0)
        for number in reversed(range(3 * places)):
            same = near[number] == own
            first = jnp.where(same, number, first)
            length = length + same.astype(jnp.int32)
        firsts.append(first)
        lengths.append((length > 1).astype(jnp.int32))
    out_ref[base] = jnp.where(reaches_low, 0, 2 * places * SHORT)
    out_ref[base + 1] = jnp.where(reaches_low, firsts[0], -1)
    out_ref[base + 2] = jnp.where(reaches_high, firsts[-1], -1)
    for place in range(places):
        out_ref[base + 3 + place] = firsts[place]
        out_ref[base + 3 + places + place] = lengths[place]
        out_ref[base + 3 + 2 * places + place] = near[places + place]
    beside = near[:places] + near[2 * places :]
    if longs == 1:
        beside = [
            jnp.where(reaches_low, low, high)
            for low, high in zip(near[:places], near[2 * places :])
        ]
    for number, segment in enumerate(beside):
        out_ref[base + 3 + 3 * places + number] = jnp.maximum(segment, 0)
    out_ref[base + 3 + 3 * places + len(beside)] = reaches_low.astype(jnp.int32)


def plan(longs, packs, starts, place, segments):
    beside = 3 if longs == 1 else 6
    size = 3 + packs + 3 + 9 + beside + 1
    return kernel_call(
        lambda *refs: plan_body(longs, packs, starts, *refs),
        "plan",
        [array((size,), jnp.int32)],
        [place, segments],
        0,
        in_specs=[SMEM, SMEM],
        out_specs=(SMEM,),
    )[0]


def latents_body(first, scalars, condition_ref, own_ref, near_ref):
    wide = condition_ref[...].astype(F32)
    active = (wide / (1.0 + jnp.exp(-wide))).astype(BF16).astype(F32)
    segments = lax.broadcasted_iota(jnp.int32, active.shape, 0)
    number = 0
    for out in (own_ref, near_ref):
        rows = []
        for _ in range(out.shape[0]):
            chosen = jnp.where(segments == scalars[first + number], active, 0.0)
            rows.append(jnp.sum(chosen, axis=0, keepdims=True))
            number += 1
        out[...] = jnp.concatenate(rows, axis=0).astype(BF16)


def latents(scalars, first, condition, own, near):
    width = condition.shape[1]
    return kernel_call(
        lambda *refs: latents_body(first, *refs),
        "latents",
        [array((own, width), BF16), array((near, width), BF16)],
        [scalars, condition],
        0,
        in_specs=[SMEM, VMEM],
    )


def pick_body(scalars, own_ref, other_ref, out_ref):
    half = own_ref.shape[2]

    def write(low, high):
        out_ref[:, :, :half] = low[...]
        out_ref[:, :, half:] = high[...]

    pl.when(scalars[0] == 0)(lambda: write(own_ref, other_ref))
    pl.when(scalars[0] == 1)(lambda: write(other_ref, own_ref))


def pick(scalars, own, other):
    return kernel_call(
        pick_body,
        "pick",
        [array((*own.shape[:2], 2 * own.shape[2]), F32)],
        [scalars, own, other],
        0,
        in_specs=[SMEM, VMEM, VMEM],
    )[0]


def others_body(first, places, scalars, shares_ref, mod_ref, hidden_ref, down_in_ref):
    entry, core = pl.program_id(0), pl.program_id(1)
    half = hidden_ref.shape[0]
    size = SHORT // 2
    for block in range(half // size):
        rows = pl.ds(block * size, size)
        place = first + entry * places + (core * (half // size) + block) // 2
        normed, _ = layer_norm(shares_ref[rows].astype(F32))
        shift, scale, gate = (mod_ref[place, group : group + 1] for group in (0, 1, 5))
        hidden_ref[rows] = (normed * (1.0 + scale) + shift).astype(BF16)
        upstream = shares_ref[pl.ds(half + block * size, size)].astype(F32)
        down_in_ref[rows] = (gate * upstream).astype(BF16)


def others(scalars, shares, mod_all, first, packs, count):
    width = shares.shape[1]
    shape = ((packs - 1) * count, width)

    def source(r, c, scalars_ref):
        return (jnp.bitwise_xor(scalars_ref[2 + packs], r + 1) * 2 + c, 0)

    half_rows = pl.BlockSpec((count // 2, width), lambda r, c, _: (2 * r + c, 0))
    return pl.pallas_call(
        lambda *refs: others_body(first, count // SHORT, *refs),
        name="others",
        out_shape=(array(shape, BF16), array(shape, BF16)),
        grid_spec=pltpu.PrefetchScalarGridSpec(
            num_scalar_prefetch=1,
            grid=(packs - 1, 2),
            in_specs=[
                pl.BlockSpec((count, width), source),
                pl.BlockSpec(mod_all.shape, lambda r, c, _: (0, 0, 0)),
            ],
            out_specs=(half_rows, half_rows),
        ),
        compiler_params=pltpu.CompilerParams(vmem_limit_bytes=56 << 20),
        cost_estimate=pl.CostEstimate(flops=0, bytes_accessed=0, transcendentals=0),
    )(scalars, shares, mod_all)


def norm_body(own_ref, near_ref, up_ref, mod_ref, hidden_ref, down_in_ref):
    step = pl.program_id(0)
    places = 3
    shift, scale = mod_ref[0, 0:1], mod_ref[0, 1:2]

    def write(rows):
        normed, _ = layer_norm(rows.astype(F32))
        hidden_ref[...] = (normed * (1.0 + scale) + shift).astype(BF16)

    @pl.when(step < places)
    def _():
        write(own_ref[...])
        down_in_ref[...] = (mod_ref[0, 5:6] * up_ref[...].astype(F32)).astype(BF16)

    pl.when(step >= places)(lambda: write(near_ref[...]))


def norm(own, near, upstream, mod_places):
    count, width = own.shape
    places = count // SHORT
    total = count + near.shape[0]

    def own_place(i):
        return (jnp.minimum(i, places - 1), 0)

    return kernel_call(
        norm_body,
        "norm",
        [array((total, width), BF16), array((count, width), BF16)],
        [own, near, upstream, mod_places],
        0,
        grid=(total // SHORT,),
        in_specs=[
            pl.BlockSpec((SHORT, width), own_place),
            pl.BlockSpec((SHORT, width), lambda i: (jnp.maximum(i - places, 0), 0)),
            pl.BlockSpec((SHORT, width), own_place),
            pl.BlockSpec((1, *mod_places.shape[1:]), lambda i: (i, 0, 0)),
        ],
        out_specs=(
            pl.BlockSpec((SHORT, width), lambda i: (i, 0)),
            pl.BlockSpec((SHORT, width), own_place),
        ),
    )


def lay_beside(buffer, own, beside, table):
    count = own.shape[0]
    buffer[count : 2 * count] = own
    if beside.shape[0] == count:
        buffer[pl.ds(aligned(table[0], SHORT), count)] = beside
    else:
        buffer[:count] = beside[:count]
        buffer[2 * count :] = beside[count:]


def attend_body(base, scalars, rows_ref, weight_ref, attended_ref, branch_ref, keys, values, turned):
    count, own_width = attended_ref.shape
    places = count // SHORT
    table = [scalars[base + number] for number in range(3)]
    lay_beside(keys, rows_ref[1, :count], rows_ref[1, count:], table)
    lay_beside(values, rows_ref[2, :count], rows_ref[2, count:], table)

    def attend(place, size):
        near = pl.ds(aligned(scalars[base + 3 + place] * SHORT, SHORT), size)
        rows = pl.ds(aligned(place * SHORT, SHORT), SHORT)
        for head in range(own_width // HEAD_DIM):
            columns = pl.ds(head * HEAD_DIM, HEAD_DIM)
            scores = dot_by(ROWS_BY_ROWS, keys[near, columns], rows_ref[0, rows, columns])
            peak = jnp.max(scores, axis=0, keepdims=True)
            exponent = jnp.exp2((scores - peak) * FACTOR_LOG2)
            total = jnp.sum(exponent, axis=0, keepdims=True)
            probs = (exponent * (1.0 / total)).astype(BF16)
            turned[columns] = dot_by(COLUMNS_BY_COLUMNS, values[near, columns], probs)
        attended_ref[rows] = turned[...].T.astype(BF16)

    def one_place(place, carry):
        is_long = scalars[base + 3 + places + place]
        pl.when(is_long == 1)(lambda: attend(place, LONG))
        pl.when(is_long == 0)(lambda: attend(place, SHORT))
        return carry

    lax.fori_loop(0, places, one_place, 0)
    branch_ref[...] = bf_dot(attended_ref[...], weight_ref[...])


def attend(base, scalars, rows, weight, count):
    own_width, width = weight.shape
    return kernel_call(
        lambda *refs: attend_body(base, *refs),
        "attend",
        [array((count, own_width), BF16), array((count, width), F32)],
        [scalars, rows, weight],
        2 * count * own_width * (width + 2 * LONG),
        far=(2,),
        in_specs=[SMEM, VMEM, VMEM],
        scratch=[
            pltpu.VMEM((3 * count, own_width), BF16),
            pltpu.VMEM((3 * count, own_width), BF16),
            pltpu.VMEM((own_width, SHORT), F32),
        ],
    )


def attend_back_body(base, scalars, rows_ref, grad_ref, near_grad_ref, weight_ref, *rest):
    hidden_grad_ref, bias_ref, pieces = rest[0], rest[1], rest[2:-3]
    held, grads, split = rest[-3:]
    count, own_width = grad_ref.shape
    places = count // SHORT
    table = [scalars[base + number] for number in range(3)]
    for number in range(3):
        lay_beside(held.at[number], rows_ref[number, :count], rows_ref[number, count:], table)
    lay_beside(held.at[3], grad_ref[...], near_grad_ref[...], table)

    def attend_back(first, size):
        rows = pl.ds(aligned(first * SHORT, SHORT), size)
        for head in range(own_width // HEAD_DIM):
            columns = pl.ds(head * HEAD_DIM, HEAD_DIM)
            query, key, value, grad = (held[number, rows, columns] for number in range(4))
            scores = dot_by(ROWS_BY_ROWS, key, query)
            peak = jnp.max(scores, axis=0, keepdims=True)
            exponent = jnp.exp2((scores - peak) * FACTOR_LOG2)
            probs = exponent * (1.0 / jnp.sum(exponent, axis=0, keepdims=True))
            probs_grad = dot_by(ROWS_BY_ROWS, value, grad)
            row_dot = jnp.sum(probs * probs_grad, axis=0, keepdims=True)
            score_grad = (probs * (probs_grad - row_dot)).astype(BF16)
            query_grad = dot_by(COLUMNS_BY_COLUMNS, score_grad, key) * FACTOR
            grads[0, rows, columns] = query_grad.astype(BF16)
            grads[1, rows, columns] = (bf_dot(score_grad, query) * FACTOR).astype(BF16)
            grads[2, rows, columns] = bf_dot(probs.astype(BF16), grad).astype(BF16)

    def short_latent(place, carry):
        is_long = scalars[base + 3 + places + place]
        pl.when(is_long == 0)(lambda: attend_back(places + place, SHORT))
        return carry

    lax.fori_loop(0, places, short_latent, 0)

    def long_latent(number, carry):
        first = scalars[base + 1 + number]
        pl.when(first >= 0)(lambda: attend_back(first, LONG))
        return carry

    lax.fori_loop(0, 2, long_latent, 0)
    own_grads = [grads[number, count : 2 * count] for number in range(3)]
    total = bf_dot(own_grads[0], weight_ref[0])
    for number in range(1, 3):
        total = total + bf_dot(own_grads[number], weight_ref[number])
    hidden_grad_ref[...] = total.astype(BF16)
    for number, grad in enumerate((own_grads[0], own_grads[2])):
        bias_ref[number : number + 1] = jnp.sum(grad.astype(F32), axis=0, keepdims=True)
    share = own_width // len(pieces)
    for number in range(len(pieces)):
        for part in range(3):
            split[number, :, part * share : (part + 1) * share] = own_grads[part][
                :, number * share : (number + 1) * share
            ]
    for entry, piece in enumerate(pieces):
        piece[...] = split[jnp.bitwise_xor(scalars[base - 1], entry)]


def attend_back(base, scalars, rows, grad, near_grad, weight, packs):
    count, own_width = grad.shape
    width = weight.shape[2]
    share = 3 * own_width // packs
    outs = kernel_call(
        lambda *refs: attend_back_body(base, *refs),
        "attend_back",
        [array((count, width), BF16), array((2, own_width), F32)]
        + [array((count, share), BF16)] * packs,
        [scalars, rows, grad, near_grad, weight],
        6 * count * own_width * width + 10 * own_width * LONG * LONG,
        far=(4,),
        in_specs=[SMEM] + [VMEM] * 4,
        scratch=[
            pltpu.VMEM((4, 3 * count, own_width), BF16),
            pltpu.VMEM((3, 3 * count, own_width), BF16),
            pltpu.VMEM((packs, count, share), BF16),
        ],
    )
    return outs[0], outs[1], list(outs[2:])


def whole(shape):
    return pl.BlockSpec(shape, lambda i: (0,) * len(shape))


def feed_up_body(scalars, kept_ref, term_ref, other_ref, bias_ref, mod_ref, *rest):
    weight_ref, hidden_bias_ref, branch_ref, hidden_ref, share_ref, slope_ref = rest[:6]
    gelu_ref, pieces = rest[6], rest[7:]
    step = pl.program_id(0)
    size = weight_ref.shape[1]

    @pl.when(step == 0)
    def _():
        def place(number, carry):
            rows = pl.ds(aligned(number * SHORT, SHORT), SHORT)
            branch = (term_ref[rows] + other_ref[rows]) + bias_ref[...]
            branch_ref[rows] = branch
            middle = kept_ref[rows].astype(F32) + mod_ref[number, 2:3] * branch
            normed, _ = layer_norm(middle)
            shift, scale = mod_ref[number, 3:4], mod_ref[number, 4:5]
            hidden_ref[rows] = (normed * (1.0 + scale) + shift).astype(BF16)
            return carry

        lax.fori_loop(0, kept_ref.shape[0] // SHORT, place, 0)
        start = aligned(scalars[0] * (hidden_ref.shape[1] - share_ref.shape[1]))
        share_ref[...] = hidden_ref[:, pl.ds(start, share_ref.shape[1])]

    gelu, slope = gelu_pair(bf_dot(hidden_ref[...], weight_ref[...]) + hidden_bias_ref[...])
    slope_ref[...] = slope
    gelu_ref[:, pl.ds(aligned(step * size), size)] = gelu.astype(BF16)

    @pl.when(step == pl.num_programs(0) - 1)
    def _():
        for entry, piece in enumerate(pieces):
            piece[...] = gelu_ref[:, pl.ds(aligned(scalars[2 + entry]), piece.shape[1])]


def feed_up(scalars, kept, term, other, bias, mod_places, weight, hidden_bias, packs):
    count, width = kept.shape
    hidden = weight.shape[1]
    size = hidden // 3
    window = windows(hidden, packs)[1]
    outs = [
        array((count, width), F32),
        array((count, width), BF16),
        array((count, half_width(width)), BF16),
        array((count, hidden), F32),
        array((count, hidden), BF16),
    ] + [array((count, window), BF16)] * packs
    out_specs = [whole(out.shape) for out in outs]
    out_specs[3] = pl.BlockSpec((count, size), lambda i: (0, i))
    result = kernel_call(
        feed_up_body,
        "feed_up",
        outs,
        [scalars, kept, term, other, bias, mod_places, weight, hidden_bias],
        2 * count * width * hidden,
        far=(6,),
        grid=(hidden // size,),
        in_specs=[
            SMEM,
            *[whole(a.shape) for a in (kept, term, other, bias, mod_places)],
            pl.BlockSpec((width, size), lambda i: (0, i)),
            pl.BlockSpec((1, size), lambda i: (0, i)),
        ],
        out_specs=tuple(out_specs),
    )
    return *result[:5], list(result[5:])


def feed_back_body(scalars, down_in_ref, down_ref, slope_ref, weight_ref, *rest):
    back_ref, sums_ref, pieces, pre_rows = rest[0], rest[1], rest[2:-1], rest[-1]
    step = pl.program_id(0)
    size = weight_ref.shape[1]
    pre_grad = dot_by(ROWS_BY_ROWS, down_in_ref[...], down_ref[...]) * slope_ref[...]
    pre_grad = pre_grad.astype(BF16)
    pre_rows[:, pl.ds(aligned(step * size), size)] = pre_grad
    sums_ref[...] = jnp.sum(pre_grad.astype(F32), axis=0, keepdims=True)
    back = dot_by(ROWS_BY_ROWS, pre_grad, weight_ref[...])

    @pl.when(step == 0)
    def _():
        back_ref[...] = back

    @pl.when(step > 0)
    def _():
        back_ref[...] += back

    @pl.when(step == pl.num_programs(0) - 1)
    def _():
        for entry, piece in enumerate(pieces):
            piece[...] = pre_rows[:, pl.ds(aligned(scalars[2 + entry]), piece.shape[1])]


def feed_back(scalars, down_in, down, slope, weight, packs):
    count, width = down_in.shape
    hidden = weight.shape[1]
    size = hidden // 3
    window = windows(hidden, packs)[1]
    outs = [array((count, width), F32), array((1, hidden), F32)]
    outs += [array((count, window), BF16)] * packs
    out_specs = [whole(out.shape) for out in outs]
    out_specs[1] = pl.BlockSpec((1, size), lambda i: (0, i))
    result = kernel_call(
        feed_back_body,
        "feed_back",
        outs,
        [scalars, down_in, down, slope, weight],
        4 * count * width * hidden,
        far=(2, 4),
        grid=(hidden // size,),
        in_specs=[
            SMEM,
            whole(down_in.shape),
            pl.BlockSpec((size, width), lambda i: (i, 0)),
            pl.BlockSpec((count, size), lambda i: (0, i)),
            pl.BlockSpec((width, size), lambda i: (0, i)),
        ],
        out_specs=tuple(out_specs),
        scratch=[pltpu.VMEM((count, hidden), BF16)],
    )
    return result[0], result[1], list(result[2:])


def middle_back_body(term_ref, other_ref, branch_ref, kept_ref, up_ref, mod_ref, *rest):
    weight_ref, middle_grad_ref, branch_grad_ref, attended_ref, sums_ref, bias_ref = rest
    hidden_grad = term_ref[...] + other_ref[...]
    branch = branch_ref[...]
    gate = mod_ref[0, 2:3]
    normed, inverse = layer_norm(kept_ref[...].astype(F32) + gate * branch)
    middle_grad = up_ref[...].astype(F32) + norm_back(
        hidden_grad * (1.0 + mod_ref[0, 4:5]), normed, inverse
    )
    middle_grad_ref[...] = middle_grad
    branch_grad = (gate * middle_grad).astype(BF16)
    branch_grad_ref[...] = branch_grad
    attended_ref[...] = dot_by(ROWS_BY_ROWS, branch_grad, weight_ref[...]).astype(BF16)
    bias_ref[0] = jnp.sum(branch_grad.astype(F32), axis=0, keepdims=True)
    sums_ref[0, 0:1] = jnp.sum(middle_grad * branch, axis=0, keepdims=True)
    sums_ref[0, 1:2] = jnp.sum(hidden_grad, axis=0, keepdims=True)
    sums_ref[0, 2:3] = jnp.sum(hidden_grad * normed, axis=0, keepdims=True)


def by_place(body, name, outs, args, flops, far=()):
    places = args[0].shape[0] // SHORT

    def spec(a):
        if a.shape[0] == places * SHORT and len(a.shape) == 2:
            return pl.BlockSpec((SHORT, a.shape[1]), lambda i: (i, 0))
        if a.shape[0] == places and len(a.shape) == 3:
            return pl.BlockSpec((1, *a.shape[1:]), lambda i: (i, 0, 0))
        return pl.BlockSpec(a.shape, lambda i: (0,) * len(a.shape))

    return kernel_call(
        body,
        name,
        outs,
        args,
        flops,
        far=far,
        grid=(places,),
        in_specs=[spec(a) for a in args],
        out_specs=tuple(spec(a) for a in outs),
    )


def middle_back(term, other, branch, kept, upstream, mod_places, weight):
    count, width = kept.shape
    places = count // SHORT
    return by_place(
        middle_back_body,
        "middle_back",
        [
            array((count, width), F32),
            array((count, width), BF16),
            array((count, weight.shape[0]), BF16),
            array((places, 3, width), F32),
            array((places, 1, width), F32),
        ],
        [term, other, branch, kept, upstream, mod_places, weight],
        2 * count * width * weight.shape[0],
        far=(6,),
    )


def input_back_body(term_ref, other_ref, middle_grad_ref, kept_ref, mod_ref, grad_ref, sums_ref):
    hidden_grad = term_ref[...].astype(F32) + other_ref[...].astype(F32)
    normed, inverse = layer_norm(kept_ref[...].astype(F32))
    grad = middle_grad_ref[...] + norm_back(hidden_grad * (1.0 + mod_ref[0, 1:2]), normed, inverse)
    grad_ref[...] = grad.astype(BF16)
    sums_ref[0, 0:1] = jnp.sum(hidden_grad, axis=0, keepdims=True)
    sums_ref[0, 1:2] = jnp.sum(hidden_grad * normed, axis=0, keepdims=True)


def input_back(term, other, middle_grad, kept, mod_places):
    count, width = kept.shape
    return by_place(
        input_back_body,
        "input_back",
        [array((count, width), BF16), array((count // SHORT, 2, width), F32)],
        [term, other, middle_grad, kept, mod_places],
        0,
    )


def result_body(term_ref, other_ref, bias_ref, branch_ref, kept_ref, up_ref, mod_ref, *rest):
    result_ref, sums_ref, bias_grad_ref = rest
    branch_two = term_ref[...].astype(F32) + other_ref[...].astype(F32) + bias_ref[...]
    middle = kept_ref[...].astype(F32) + mod_ref[0, 2:3] * branch_ref[...]
    gate = mod_ref[0, 5:6]
    upstream = up_ref[...].astype(F32)
    result_ref[...] = (middle + gate * branch_two).astype(BF16)
    sums_ref[0, 0:1] = jnp.sum(upstream * branch_two, axis=0, keepdims=True)
    down_in = (gate * upstream).astype(BF16).astype(F32)
    bias_grad_ref[0] = jnp.sum(down_in, axis=0, keepdims=True)


def result(term, other, bias, branch, kept, upstream, mod_places):
    count, width = kept.shape
    places = count // SHORT
    return by_place(
        result_body,
        "result",
        [
            array((count, width), BF16),
            array((places, 1, width), F32),
            array((places, 1, width), F32),
        ],
        [term, other, bias, branch, kept, upstream, mod_places],
        0,
    )


def weight_grad_body(packs, offset, count_shares, scalars, *refs):
    shares, refs = refs[:count_shares], refs[count_shares:]
    columns, refs = refs[:packs], refs[packs:]
    outs, (rows_all, columns_all, total) = refs[:-3], refs[-3:]
    count, wide = columns[0].shape
    width = rows_all.shape[1]
    half = half_width(width)
    for entry in range(packs):
        rows = pl.ds(entry * count, count)
        columns_all[rows] = columns[entry][...]
        if count_shares == 1:
            source = jnp.bitwise_xor(scalars[2 + packs], entry) * (2 * count)
            low = pl.ds(aligned(source, SHORT), count)
            high = pl.ds(aligned(source + count, SHORT), count)
            rows_all[rows, :half] = shares[0][low, offset : offset + half]
            rows_all[rows, half:] = shares[0][high, offset + 2 * half - width : offset + half]
        elif entry == 0:
            rows_all[rows] = shares[0][:count]
        else:
            rows_all[rows] = shares[1][(entry - 1) * count : entry * count]
    if len(outs) == 1:
        outs[0][...] = dot_by(COLUMNS_BY_COLUMNS, rows_all[...], columns_all[...]).astype(BF16)
        return
    total[:, :wide] = dot_by(COLUMNS_BY_COLUMNS, rows_all[...], columns_all[...])
    if total.shape[1] > wide:
        others, outs = outs[:packs], outs[packs:]
        other = others[0][...].astype(F32)
        for entry in range(1, packs):
            other = other + others[entry][...].astype(F32)
        total[:, wide:] = other.T
    cut_by_blk(scalars, total, outs)


def cut_by_blk(scalars, total, outs):
    blocks = len(outs)
    size = total.shape[0] // blocks
    for step in range(blocks):
        target = lax.rem(scalars[1] + step, blocks)
        piece = total[pl.ds(aligned(target * size, 8), size)]
        outs[step][...] = piece.astype(outs[step].dtype)


def cut_shapes(width, wide, blocks):
    size = width // blocks
    return [array((size, wide), F32)] + [array((size, wide), BF16)] * (blocks - 1)


def weight_grad(scalars, width, offset, shares, columns, others=(), blocks=1):
    packs = len(columns)
    count, wide = columns[0].shape
    total = wide + (others[0].shape[0] if others else 0)
    outs = [array((width, wide), BF16)]
    if blocks > 1:
        outs = cut_shapes(width, total, blocks)
    return kernel_call(
        lambda *refs: weight_grad_body(packs, offset, len(shares), *refs),
        "weight_grad",
        outs,
        [scalars, *shares, *columns, *others],
        2 * packs * count * width * wide,
        in_specs=[SMEM] + [VMEM] * (packs + len(shares) + len(others)),
        scratch=[
            pltpu.VMEM((packs * count, width), BF16),
            pltpu.VMEM((packs * count, wide), BF16),
            pltpu.VMEM((width, total), F32),
        ],
    )


def own_weight_grad_body(packs, scalars, rows_ref, columns_ref, *refs):
    pieces, total = refs[:-1], refs[-1]
    total[...] = dot_by(COLUMNS_BY_COLUMNS, rows_ref[...], columns_ref[...])
    size = total.shape[0] // packs
    for entry, piece in enumerate(pieces):
        start = jnp.bitwise_xor(scalars[2 + packs], entry) * size
        piece[...] = total[pl.ds(aligned(start, 8), size)].astype(BF16)


def own_weight_grad(scalars, rows, columns, packs):
    shape = (rows.shape[1], columns.shape[1])
    return kernel_call(
        lambda *refs: own_weight_grad_body(packs, *refs),
        "own_weight_grad",
        [array((shape[0] // packs, shape[1]), BF16)] * packs,
        [scalars, rows, columns],
        2 * rows.shape[0] * math.prod(shape),
        in_specs=[SMEM, VMEM, VMEM],
        scratch=[pltpu.VMEM(shape, F32)],
    )


def join_body(kind, starts, packs, scalars, *refs):
    outs, held = refs[1:-1], refs[-1]
    size = refs[0].shape[0] // packs
    stacked = kind == "hidden"
    if not stacked:
        entries, outs = refs[:packs], refs[packs:-1]
        for entry in range(packs):
            held[entry] = entries[entry][...]
    for number in range(packs):
        if stacked:
            piece = refs[0][number * size : (number + 1) * size].astype(F32)
        else:
            piece = held[jnp.bitwise_xor(scalars[2 + packs], number)].astype(F32)
        if kind == "qkv":
            share = piece.shape[1] // 4
            columns = pl.ds(number * share, share)
            for part in range(3):
                outs[0][part, :, columns] = piece[:, part * share : (part + 1) * share]
            outs[1][:, columns] = piece[:, 3 * share :]
        else:
            end = [*starts[1:], outs[0].shape[1]][number]
            outs[0][:, starts[number] : end] = piece[:, : end - starts[number]]


def join(kind, scalars, entries, packs, shapes, starts=()):
    return kernel_call(
        lambda *refs: join_body(kind, starts, packs, *refs),
        "join_" + kind,
        [array(shape, F32) for shape in shapes],
        [scalars, *entries],
        0,
        in_specs=[SMEM] + [VMEM] * len(entries),
        scratch=[pltpu.VMEM((packs, *entries[0].shape), BF16)],
    )


def collect_body(scalars, input_ref, middle_ref, two_ref, active_ref, *refs):
    qkv_ref, output_ref, hidden_ref, down_ref, out_ref, held = refs
    places, _, width = middle_ref.shape
    half = width // 2
    row = 0

    def put(value):
        nonlocal row
        held[row : row + 1] = value
        row += 1

    def put_twice(value):
        high = value.astype(BF16).astype(F32)
        put(high)
        put(value - high)

    def put_sums(start):
        nonlocal row
        row = 0
        for place in range(places):
            for source in (input_ref, middle_ref, two_ref):
                for number in range(source.shape[1]):
                    put(source[place, number : number + 1, start : start + half])

    held[...] = jnp.zeros_like(held)
    pl.when(scalars[0] == 0)(lambda: put_sums(0))
    pl.when(scalars[0] == 1)(lambda: put_sums(half))
    for place in range(places):
        active = active_ref[place : place + 1].astype(F32)
        put(active[:, :half])
        put(active[:, half:])
    put_twice(qkv_ref[0:1])
    put_twice(qkv_ref[1:2])
    for number in range(hidden_ref.shape[1] // half):
        put_twice(hidden_ref[:, number * half : (number + 1) * half])
    for source in (output_ref, down_ref):
        total = jnp.sum(source[...], axis=0)
        put_twice(total[:, :half])
        put_twice(total[:, half:])
    out_ref[...] = held[...].astype(BF16)


def collect(scalars, *args):
    places, _, width = args[0].shape
    hidden = args[6].shape[1]
    used = places * 8 + 2 * (2 + 2 * hidden // width + 4)
    size = -(-used // 16) * 16
    return kernel_call(
        collect_body,
        "collect",
        [array((size, width // 2), BF16)],
        [scalars, *args],
        0,
        in_specs=[SMEM] + [VMEM] * len(args),
        scratch=[pltpu.VMEM((size, width // 2), F32)],
    )[0]


def spread_body(packs, blocks, places, size, scalars, segments, *refs):
    entries = refs[:packs]
    weight_ref, bias_ref, biases_ref, grad_ref, held, rows_all, active, sums = refs[packs:]
    half = weight_ref.shape[2]
    rows = weight_ref.shape[1]
    pack = scalars[2 + packs]
    for entry in range(packs):
        held[entry] = entries[entry][...].reshape(blocks, size, half)
    for number in range(packs):
        for block in range(blocks):
            piece = held[jnp.bitwise_xor(pack, number), jnp.bitwise_xor(scalars[1], block)]
            rows_all[number * blocks + block] = piece.astype(F32)
    cut = 6 * places
    devices = packs * blocks

    def take_active(block):
        start = block * rows
        for device in range(devices):
            for place in range(places):
                row = cut + 2 * place
                whole_row = jnp.concatenate(
                    [rows_all[device, row : row + 1], rows_all[device, row + 1 : row + 2]], axis=1
                )
                number = device * places + place
                active[number : number + 1] = whole_row[:, start : start + rows]

    for block in range(blocks):
        pl.when(scalars[1] == block)(lambda: take_active(block))
    own_active = active[...].astype(BF16)
    for group in range(6):
        for device in range(devices):
            for place in range(places):
                number = device * places + place
                row = place * 6 + group
                sums[number : number + 1] = rows_all[device, row : row + 1]
        values = sums[...]
        bias_ref[group : group + 1] = jnp.sum(values, axis=0, keepdims=True)
        weight_ref[group] = dot_by(COLUMNS_BY_COLUMNS, own_active, values.astype(BF16))
    first = cut + 2 * places
    total = rows_all[0, first:]
    for device in range(1, devices):
        total = total + rows_all[device, first:]
    biases_ref[...] = total
    grad_ref[...] = jnp.zeros_like(grad_ref)
    for block in range(blocks):
        for place in range(places):
            segment = segments[(block * places + place) * SHORT]
            own = rows_all[pack * blocks + block, place * 6 : place * 6 + 6]
            grad_ref[segment] = grad_ref[segment] + own


def spread(scalars, segments, entries, packs, blocks, places, seg_count, width):
    devices = packs * blocks
    size = entries[0].shape[0] // blocks
    half = entries[0].shape[1]
    return kernel_call(
        lambda *refs: spread_body(packs, blocks, places, size, *refs),
        "spread",
        [
            array((6, width // blocks, half), F32),
            array((6, half), F32),
            array((size - 8 * places, half), F32),
            array((seg_count, 6, half), F32),
        ],
        [scalars, segments, *entries],
        0,
        in_specs=[SMEM, SMEM] + [VMEM] * packs,
        scratch=[
            pltpu.VMEM((packs, blocks, size, half), BF16),
            pltpu.VMEM((devices, size, half), F32),
            pltpu.VMEM((devices * places, width // blocks), F32),
            pltpu.VMEM((devices * places, half), F32),
        ],
    )


def xor_permute(block, axis, bits):
    return lax.ppermute(block, axis, [(i, i ^ bits) for i in range(lax.axis_size(axis))])


def swap(block):
    return xor_permute(block, "head", 1)


def move(block, step):
    count = lax.axis_size("blk")
    pairs = [(i, i + step) for i in range(count) if 0 <= i + step < count]
    return lax.ppermute(block, "blk", pairs)


def gather_xor(block, axis, turned=False):
    bits = [1 << b for b in range((lax.axis_size(axis) - 1).bit_length())]
    held = {0: block}
    for bit in bits[::-1] if turned else bits:
        for entry in list(held):
            held[entry ^ bit] = xor_permute(held[entry], axis, bit)
    return [held[entry] for entry in range(lax.axis_size(axis))]


def gather_each(block, axis):
    return [block] + [xor_permute(block, axis, r) for r in range(1, lax.axis_size(axis))]


def trade(pieces, axis, entries):
    return {r: xor_permute(pieces[r], axis, r) for r in entries}


def windows(width, parts):
    tiles = width // LANES
    size = -(-tiles // parts)
    return [LANES * (q * (tiles - size) // (parts - 1)) for q in range(parts)], size * LANES


def half_width(width):
    return -(-width // (2 * LANES)) * LANES


def gather_shares(share):
    return lax.all_gather(share, ("pack", "head"), axis=0, tiled=True)


def hold(values, *after):
    flat, tree = jax.tree.flatten(values)
    held = lax.optimization_barrier((*flat, *after))
    return jax.tree.unflatten(tree, held[: len(flat)])


def send_blk(pieces):
    count = len(pieces)
    found = [pieces[0]]
    for step in range(1, count):
        pairs = [(i, (i + step) % count) for i in range(count)]
        found.append(lax.ppermute(pieces[step], "blk", pairs))
    return found


def add_blk(found):
    total = found[0]
    for piece in found[1:]:
        total = total + piece.astype(F32)
    return total.astype(BF16)


def local(
    tokens_full,
    condition,
    kept_index,
    segment_ids,
    cotangent,
    qkv_weight,
    query_value_bias,
    output_weight,
    output_bias,
    hidden_weight,
    hidden_bias,
    down_weight,
    down_bias,
    modulation_weight,
    modulation_bias,
):
    width = tokens_full.shape[2]
    own_width = qkv_weight.shape[2]
    hidden = hidden_weight.shape[1]
    count = kept_index.shape[1]
    seg_count = condition.shape[1]
    places = count // SHORT
    longs = (segment_ids.shape[1] - SHORT * seg_count) // (LONG - SHORT)
    packs = lax.axis_size("pack")
    blocks = lax.axis_size("blk")
    blk = lax.axis_index("blk")
    core = lax.axis_index("head")
    pack = lax.axis_index("pack")

    modulation_turned = jnp.transpose(modulation_weight, (1, 2, 0))
    starts, window = windows(hidden, packs)
    place = jnp.stack([core, blk, pack, jnp.int32(blocks)]).astype(jnp.int32)
    scalars = plan(longs, packs, starts, place, segment_ids[0])
    base = 3 + packs
    own_active, near_active = latents(
        scalars, base + 3 + 2 * places, condition[0], places, places if longs == 1 else 2 * places
    )
    local_index, own_active = hold((kept_index[0] - blk * (2 * count), own_active))
    full_rows = tokens_full[0]
    cot_rows = cotangent[0]
    picker = (
        local_index[:, None] == jnp.arange(full_rows.shape[0], dtype=jnp.int32)[None, :]
    ).astype(BF16)
    kept_rows = bf_dot(picker, full_rows).astype(BF16)
    upstream = bf_dot(picker, cot_rows).astype(BF16)

    reaches_low = scalars[-1] == 1

    def beside(block):
        low, high = move(block, 1), move(block, -1)
        if longs == 1:
            return jnp.where(reaches_low, low, high)
        return jnp.concatenate([low, high], axis=0)

    half = count // 2
    kept_half = lax.dynamic_slice_in_dim(kept_rows, core * half, half, 0)
    near_half = beside(kept_half)
    token_shares = gather_shares(
        jnp.concatenate(
            [kept_half, lax.dynamic_slice_in_dim(upstream, core * half, half, 0)], axis=0
        )
    )
    other_half = swap(near_half)
    first = jnp.where(core == 0, near_half, other_half).reshape(-1, half, width)
    second = jnp.where(core == 0, other_half, near_half).reshape(-1, half, width)
    near_rows = jnp.concatenate([first, second], axis=1).reshape(-1, width)

    near_count = near_rows.shape[0] // SHORT
    other_active = list(trade([own_active] * packs, "pack", range(1, packs)).values())
    mod_own = (
        jnp.einsum(
            "sd,gfd->sgf",
            jnp.concatenate([own_active, near_active, *other_active], axis=0),
            modulation_turned,
            preferred_element_type=F32,
        )
        + modulation_bias.astype(F32)[None]
    )
    mod_all = pick(scalars, mod_own, swap(mod_own))
    mod_places = mod_all[:places]
    wide_bias = query_value_bias.astype(F32)
    qkv_bias = jnp.stack([wide_bias[0], jnp.zeros_like(wide_bias[0]), wide_bias[1]])[:, None]
    hidden_rows, down_in = norm(kept_rows, near_rows, upstream, mod_all)
    qkv_turned = jnp.transpose(qkv_weight, (1, 2, 0))
    projected = jnp.einsum("td,gfd->gtf", hidden_rows, qkv_turned, preferred_element_type=F32)
    qkv_rows = (projected + qkv_bias).astype(BF16)

    attended, branch_term = attend(base, scalars, qkv_rows, output_weight, count)
    branch_one, hidden_two, hidden_two_share, slope, gelu, gelu_pieces = feed_up(
        scalars,
        kept_rows,
        branch_term,
        swap(branch_term),
        output_bias.astype(F32)[None],
        mod_places,
        hidden_weight,
        hidden_bias.astype(F32)[None],
        packs,
    )
    one_step = [r for r in range(1, packs) if r & (r - 1) == 0]
    further = [r for r in range(1, packs) if r & (r - 1)]

    def by_entry(pieces, *parts):
        found = {0: pieces[0]}
        for part in parts:
            found.update(part)
        return [found[r] for r in range(packs)]

    hidden_two_shares = gather_shares(hidden_two_share)
    gelu_first = trade(gelu_pieces, "pack", one_step)
    back_term, hidden_sums, pre_pieces = feed_back(
        scalars, down_in, down_weight, slope, hidden_weight, packs
    )
    back_term, gelu_first, gelu_pieces, pre_pieces = hold(
        (back_term, gelu_first, gelu_pieces, pre_pieces)
    )
    gelu_last = trade(gelu_pieces, "pack", further)
    hidden_other_packs, down_other_packs = others(
        scalars, token_shares, mod_all, places + near_count, packs, count
    )
    back_other, hidden_other_packs, down_other_packs = hold(
        (swap(back_term), hidden_other_packs, down_other_packs)
    )
    middle_grad, branch_grad, attended_grad, middle_sums, output_sums = middle_back(
        back_term, back_other, branch_one, kept_rows, upstream, mod_places, output_weight
    )
    attended_grad, pre_pieces, gelu, branch_grad = hold(
        (attended_grad, pre_pieces, gelu, branch_grad)
    )
    near_grad = beside(attended_grad)
    rows = width // blocks

    pre_first = trade(pre_pieces, "pack", one_step)
    gelu_all = by_entry(gelu_pieces, gelu_first, gelu_last)
    down_raw = weight_grad(scalars, width, 0, [down_in, down_other_packs], gelu_all)[0]
    output_pieces = own_weight_grad(scalars, attended, branch_grad, packs)
    pre_last = trade(pre_pieces, "pack", further)
    near_grad, down_raw, output_pieces, pre_first = hold(
        (near_grad, down_raw, output_pieces, pre_first)
    )
    down_term = lax.psum_scatter(down_raw, "blk", scatter_dimension=0, tiled=True)
    output_first = trade(output_pieces, "pack", one_step)
    hidden_term, qkv_sums, qkv_pieces = attend_back(
        base, scalars, qkv_rows, attended_grad, near_grad, qkv_turned, packs
    )
    hidden_term, qkv_pieces, output_first, output_pieces, gelu, pre_last = hold(
        (hidden_term, qkv_pieces, output_first, output_pieces, gelu, pre_last)
    )
    qkv_first = trade(qkv_pieces, "pack", one_step)
    qkv_last = trade(qkv_pieces, "pack", further)
    output_last = trade(output_pieces, "pack", further)

    pre_all = by_entry(pre_pieces, pre_first, pre_last)
    hidden_raw = weight_grad(scalars, width, 0, [hidden_two_shares], pre_all)[0]
    hidden_reduced = lax.psum_scatter(hidden_raw, "blk", scatter_dimension=0, tiled=True)
    hidden_other, qkv_first, output_last, hidden_raw, gelu = hold(
        (swap(hidden_term), qkv_first, output_last, hidden_raw, gelu)
    )
    input_grad, input_sums = input_back(
        hidden_term, hidden_other, middle_grad, kept_rows, mod_places
    )
    two_term = bf_dot(gelu, down_weight).astype(BF16)
    result_rows, two_sums, down_sums = result(
        two_term,
        swap(two_term),
        down_bias.astype(F32)[None],
        branch_one,
        kept_rows,
        upstream,
        mod_places,
    )
    sent = collect(
        scalars,
        input_sums,
        middle_sums,
        two_sums,
        own_active,
        qkv_sums,
        output_sums,
        hidden_sums,
        down_sums,
    )
    qkv_last, sent = hold((qkv_last, sent))
    by_blk = gather_each(sent, "blk")
    qkv_terms = weight_grad(
        scalars,
        width,
        0,
        [hidden_rows, hidden_other_packs],
        by_entry(qkv_pieces, qkv_first, qkv_last),
        by_entry(output_pieces, output_first, output_last),
        blocks,
    )
    qkv_terms, by_blk, result_rows, input_grad, down_term = hold(
        (qkv_terms, by_blk, result_rows, input_grad, down_term)
    )

    def put_rows(base, rows):
        spread = dot_by(COLUMNS_BY_COLUMNS, picker, rows)
        kept = jnp.max(picker, axis=0)[:, None] > 0
        return jnp.where(kept, spread.astype(BF16), base)[None]

    qkv_found = send_blk(qkv_terms)
    entries = gather_each(jnp.concatenate(by_blk, axis=0), "pack")
    down_entries = gather_each(down_term, "pack")
    block_output = put_rows(full_rows, result_rows)
    tokens_grad = put_rows(cot_rows, input_grad)
    qkv_found, entries, block_output, tokens_grad, down_entries = hold(
        (qkv_found, entries, block_output, tokens_grad, down_entries)
    )
    qkv_entries = gather_each(add_blk(qkv_found), "pack")
    hidden_gathered = lax.all_gather(hidden_reduced, "pack", axis=0, tiled=True)
    modulation_weight_grad, modulation_bias_grad, biases, mod_grad = spread(
        scalars, segment_ids[0], entries, packs, blocks, places, seg_count, width
    )
    qkv_weight_grad, output_weight_grad = join(
        "qkv", scalars, qkv_entries, packs, [(3, rows, own_width), (rows, own_width)]
    )
    down_weight_grad = join(
        "down",
        scalars,
        down_entries,
        packs,
        [(rows, hidden)],
        starts,
    )[0].T
    hidden_weight_grad = join(
        "hidden", scalars, [hidden_gathered], packs, [(rows, hidden)], starts
    )[0]
    output_weight_grad = output_weight_grad.T
    qkv_weight_grad = jnp.swapaxes(qkv_weight_grad, 0, 1)
    modulation_weight_grad = jnp.swapaxes(modulation_weight_grad, 0, 1)
    mod_high = mod_grad.astype(BF16)
    mod_low = (mod_grad - mod_high.astype(F32)).astype(BF16)
    cond_terms = jnp.einsum(
        "sgf,gfd->sd",
        jnp.concatenate([mod_high, mod_low], axis=0),
        modulation_turned,
        preferred_element_type=F32,
    )
    cond_term = cond_terms[:seg_count] + cond_terms[seg_count:]
    cond_total = cond_term + swap(cond_term)
    cond_rows = condition[0].astype(F32)
    squashed = jax.nn.sigmoid(cond_rows)
    condition_grad = (cond_total * squashed * (1.0 + cond_rows * (1.0 - squashed)))[None]

    def bias_rows(first, number):
        pairs = biases[2 * first : 2 * (first + number)].reshape(number, 2, own_width)
        return (pairs[:, 0] + pairs[:, 1]).reshape(-1)

    value_bias = bias_rows(0, 2).reshape(2, own_width)
    hidden_rows_count = hidden // own_width
    return (
        block_output,
        tokens_grad,
        condition_grad,
        qkv_weight_grad,
        value_bias,
        output_weight_grad,
        bias_rows(2 + hidden_rows_count, 2),
        hidden_weight_grad,
        bias_rows(2, hidden_rows_count),
        down_weight_grad,
        bias_rows(4 + hidden_rows_count, 2),
        modulation_weight_grad,
        modulation_bias_grad,
    )


def solution(mesh):
    in_specs = (
        P("pack", "blk", None),
        P("pack", None, None),
        P("pack", "blk"),
        P("pack", None),
        P("pack", "blk", None),
        P(None, None, "head"),
        P(None, "head"),
        P("head", None),
        P(),
        P(None, "head"),
        P("head"),
        P("head", None),
        P(),
        P(None, None, "head"),
        P(None, "head"),
    )
    out_specs = (
        P("pack", "blk", None),
        P("pack", "blk", None),
        P("pack", None, None),
        P("blk", None, "head"),
        P(None, "head"),
        P("head", "blk"),
        P(),
        P("blk", "head"),
        P("head"),
        P("head", "blk"),
        P(),
        P("blk", None, "head"),
        P(None, "head"),
    )
    return jax.shard_map(local, mesh=mesh, in_specs=in_specs, out_specs=out_specs, check_vma=False)
```

```python
import math

import jax
import jax.numpy as jnp
from jax import lax
from jax.experimental import pallas as pl
from jax.experimental.pallas import tpu as pltpu
from jax.sharding import PartitionSpec as P

HEAD_DIM = 72
SHORT = 128
LONG = 4 * SHORT
LANES = 128
EPSILON = 1e-06
FACTOR = 1.0 / math.sqrt(HEAD_DIM)
FACTOR_LOG2 = FACTOR * math.log2(math.e)
GELU_SLOPE = math.sqrt(2.0 / math.pi)
GELU_CUBE = 0.044715
F32 = jnp.float32
BF16 = jnp.bfloat16
ROWS_BY_ROWS = (((1,), (1,)), ((), ()))
COLUMNS_BY_COLUMNS = (((0,), (0,)), ((), ()))
VMEM = pl.BlockSpec(memory_space=pltpu.VMEM)
SMEM = pl.BlockSpec(memory_space=pltpu.SMEM)


def bf_dot(operand_a, operand_b):
    return jnp.dot(operand_a, operand_b, preferred_element_type=F32)


def dot_by(dims, operand_a, operand_b):
    return lax.dot_general(operand_a, operand_b, dims, preferred_element_type=F32)


def array(shape, kind):
    return jax.ShapeDtypeStruct(shape, kind)


SLOW = 1000


def kernel_call(
    body, name, outs, args, flops, grid=(), in_specs=None, out_specs=None, scratch=(), far=(), vmem=48
):
    args = [
        pltpu.with_memory_space_constraint(a, pltpu.HBM) if number in far else a
        for number, a in enumerate(args)
    ]
    moved = sum(math.prod(a.shape) * a.dtype.itemsize for a in (*args, *outs))
    return pl.pallas_call(
        body,
        name=name,
        out_shape=tuple(outs),
        grid=grid,
        in_specs=in_specs or [VMEM] * len(args),
        out_specs=out_specs or (VMEM,) * len(outs),
        scratch_shapes=scratch,
        compiler_params=pltpu.CompilerParams(vmem_limit_bytes=vmem << 20),
        cost_estimate=pl.CostEstimate(
            flops=int(flops) // SLOW, bytes_accessed=int(moved) // SLOW, transcendentals=0
        ),
    )(*args)


def aligned(index, to=LANES):
    return pl.multiple_of(index, to)


def layer_norm(values):
    center = values - jnp.mean(values, axis=-1, keepdims=True)
    spread = jnp.mean(center * center, axis=-1, keepdims=True)
    inverse = lax.rsqrt(spread + EPSILON)
    return (center * inverse, inverse)


def norm_back(upstream, normed, inverse):
    mean_grad = jnp.mean(upstream, axis=-1, keepdims=True)
    mean_cross = jnp.mean(upstream * normed, axis=-1, keepdims=True)
    return inverse * (upstream - mean_grad - normed * mean_cross)


def gelu_pair(value):
    square = value * value
    bent = jnp.tanh(GELU_SLOPE * (value + GELU_CUBE * (value * square)))
    half = 0.5 * (1.0 + bent)
    slope = GELU_SLOPE * (1.0 + (3.0 * GELU_CUBE) * square)
    return value * half, half + 0.5 * value * (1.0 - bent * bent) * slope


def plan_body(longs, packs, starts, place_ref, segments, out_ref):
    core, blk, pack, blocks = (place_ref[number] for number in range(4))
    places = 3
    out_ref[0] = core
    out_ref[1] = blk
    for entry in range(packs):
        window = jnp.bitwise_xor(pack, entry)
        start = jnp.int32(0)
        for number in range(packs):
            start = jnp.where(window == number, starts[number], start)
        out_ref[2 + entry] = start
    out_ref[2 + packs] = pack
    near = []
    for number in range(3 * places):
        index = (blk - 1) * places + number
        inside = jnp.logical_and(index >= 0, index < blocks * places)
        found = segments[jnp.clip(index, 0, blocks * places - 1) * SHORT]
        near.append(jnp.where(inside, found, -1))
    reaches_low = near[places - 1] == near[places]
    reaches_high = near[2 * places - 1] == near[2 * places]
    base = 3 + packs
    firsts, lengths = [], []
    for place in range(places):
        own = near[places + place]
        first = jnp.int32(0)
        length = jnp.int32(0)
        for number in reversed(range(3 * places)):
            same = near[number] == own
            first = jnp.where(same, number, first)
            length = length + same.astype(jnp.int32)
        firsts.append(first)
        lengths.append((length > 1).astype(jnp.int32))
    out_ref[base] = jnp.where(reaches_low, 0, 2 * places * SHORT)
    out_ref[base + 1] = jnp.where(reaches_low, firsts[0], -1)
    out_ref[base + 2] = jnp.where(reaches_high, firsts[-1], -1)
    for place in range(places):
        out_ref[base + 3 + place] = firsts[place]
        out_ref[base + 3 + places + place] = lengths[place]
        out_ref[base + 3 + 2 * places + place] = near[places + place]
    beside = near[:places] + near[2 * places :]
    if longs == 1:
        beside = [
            jnp.where(reaches_low, low, high)
            for low, high in zip(near[:places], near[2 * places :])
        ]
    for number, segment in enumerate(beside):
        out_ref[base + 3 + 3 * places + number] = jnp.maximum(segment, 0)
    out_ref[base + 3 + 3 * places + len(beside)] = reaches_low.astype(jnp.int32)


def plan(longs, packs, starts, place, segments):
    beside = 3 if longs == 1 else 6
    size = 3 + packs + 3 + 9 + beside + 1
    return kernel_call(
        lambda *refs: plan_body(longs, packs, starts, *refs),
        "plan",
        [array((size,), jnp.int32)],
        [place, segments],
        0,
        in_specs=[SMEM, SMEM],
        out_specs=(SMEM,),
    )[0]


def latents_body(first, scalars, condition_ref, own_ref, near_ref):
    wide = condition_ref[...].astype(F32)
    active = (wide / (1.0 + jnp.exp(-wide))).astype(BF16).astype(F32)
    segments = lax.broadcasted_iota(jnp.int32, active.shape, 0)
    number = 0
    for out in (own_ref, near_ref):
        rows = []
        for _ in range(out.shape[0]):
            chosen = jnp.where(segments == scalars[first + number], active, 0.0)
            rows.append(jnp.sum(chosen, axis=0, keepdims=True))
            number += 1
        out[...] = jnp.concatenate(rows, axis=0).astype(BF16)


def latents(scalars, first, condition, own, near):
    width = condition.shape[1]
    return kernel_call(
        lambda *refs: latents_body(first, *refs),
        "latents",
        [array((own, width), BF16), array((near, width), BF16)],
        [scalars, condition],
        0,
        in_specs=[SMEM, VMEM],
    )


def pick_body(scalars, own_ref, other_ref, out_ref):
    half = own_ref.shape[2]

    def write(low, high):
        out_ref[:, :, :half] = low[...]
        out_ref[:, :, half:] = high[...]

    pl.when(scalars[0] == 0)(lambda: write(own_ref, other_ref))
    pl.when(scalars[0] == 1)(lambda: write(other_ref, own_ref))


def pick(scalars, own, other):
    return kernel_call(
        pick_body,
        "pick",
        [array((*own.shape[:2], 2 * own.shape[2]), F32)],
        [scalars, own, other],
        0,
        in_specs=[SMEM, VMEM, VMEM],
    )[0]


def others_body(first, places, scalars, shares_ref, mod_ref, hidden_ref, down_in_ref):
    entry, core = pl.program_id(0), pl.program_id(1)
    half = hidden_ref.shape[0]
    size = SHORT // 2
    for block in range(half // size):
        rows = pl.ds(block * size, size)
        place = first + entry * places + (core * (half // size) + block) // 2
        normed, _ = layer_norm(shares_ref[rows].astype(F32))
        shift, scale, gate = (mod_ref[place, group : group + 1] for group in (0, 1, 5))
        hidden_ref[rows] = (normed * (1.0 + scale) + shift).astype(BF16)
        upstream = shares_ref[pl.ds(half + block * size, size)].astype(F32)
        down_in_ref[rows] = (gate * upstream).astype(BF16)


def others(scalars, shares, mod_all, first, packs, count):
    width = shares.shape[1]
    shape = ((packs - 1) * count, width)

    def source(r, c, scalars_ref):
        return (jnp.bitwise_xor(scalars_ref[2 + packs], r + 1) * 2 + c, 0)

    half_rows = pl.BlockSpec((count // 2, width), lambda r, c, _: (2 * r + c, 0))
    return pl.pallas_call(
        lambda *refs: others_body(first, count // SHORT, *refs),
        name="others",
        out_shape=(array(shape, BF16), array(shape, BF16)),
        grid_spec=pltpu.PrefetchScalarGridSpec(
            num_scalar_prefetch=1,
            grid=(packs - 1, 2),
            in_specs=[
                pl.BlockSpec((count, width), source),
                pl.BlockSpec(mod_all.shape, lambda r, c, _: (0, 0, 0)),
            ],
            out_specs=(half_rows, half_rows),
        ),
        compiler_params=pltpu.CompilerParams(vmem_limit_bytes=56 << 20),
        cost_estimate=pl.CostEstimate(flops=0, bytes_accessed=0, transcendentals=0),
    )(scalars, shares, mod_all)


def norm_body(own_ref, near_ref, up_ref, mod_ref, hidden_ref, down_in_ref):
    step = pl.program_id(0)
    places = 3
    shift, scale = mod_ref[0, 0:1], mod_ref[0, 1:2]

    def write(rows):
        normed, _ = layer_norm(rows.astype(F32))
        hidden_ref[...] = (normed * (1.0 + scale) + shift).astype(BF16)

    @pl.when(step < places)
    def _():
        write(own_ref[...])
        down_in_ref[...] = (mod_ref[0, 5:6] * up_ref[...].astype(F32)).astype(BF16)

    pl.when(step >= places)(lambda: write(near_ref[...]))


def norm(own, near, upstream, mod_places):
    count, width = own.shape
    places = count // SHORT
    total = count + near.shape[0]

    def own_place(i):
        return (jnp.minimum(i, places - 1), 0)

    return kernel_call(
        norm_body,
        "norm",
        [array((total, width), BF16), array((count, width), BF16)],
        [own, near, upstream, mod_places],
        0,
        grid=(total // SHORT,),
        in_specs=[
            pl.BlockSpec((SHORT, width), own_place),
            pl.BlockSpec((SHORT, width), lambda i: (jnp.maximum(i - places, 0), 0)),
            pl.BlockSpec((SHORT, width), own_place),
            pl.BlockSpec((1, *mod_places.shape[1:]), lambda i: (i, 0, 0)),
        ],
        out_specs=(
            pl.BlockSpec((SHORT, width), lambda i: (i, 0)),
            pl.BlockSpec((SHORT, width), own_place),
        ),
    )


def lay_beside(buffer, own, beside, table):
    count = own.shape[0]
    buffer[count : 2 * count] = own
    if beside.shape[0] == count:
        buffer[pl.ds(aligned(table[0], SHORT), count)] = beside
    else:
        buffer[:count] = beside[:count]
        buffer[2 * count :] = beside[count:]


def attend_body(base, scalars, rows_ref, weight_ref, attended_ref, branch_ref, keys, values, turned):
    count, own_width = attended_ref.shape
    places = count // SHORT
    table = [scalars[base + number] for number in range(3)]
    lay_beside(keys, rows_ref[1, :count], rows_ref[1, count:], table)
    lay_beside(values, rows_ref[2, :count], rows_ref[2, count:], table)

    def attend(place, size):
        near = pl.ds(aligned(scalars[base + 3 + place] * SHORT, SHORT), size)
        rows = pl.ds(aligned(place * SHORT, SHORT), SHORT)
        for head in range(own_width // HEAD_DIM):
            columns = pl.ds(head * HEAD_DIM, HEAD_DIM)
            scores = dot_by(ROWS_BY_ROWS, keys[near, columns], rows_ref[0, rows, columns])
            peak = jnp.max(scores, axis=0, keepdims=True)
            exponent = jnp.exp2((scores - peak) * FACTOR_LOG2)
            total = jnp.sum(exponent, axis=0, keepdims=True)
            probs = (exponent * (1.0 / total)).astype(BF16)
            turned[columns] = dot_by(COLUMNS_BY_COLUMNS, values[near, columns], probs)
        attended_ref[rows] = turned[...].T.astype(BF16)

    def one_place(place, carry):
        is_long = scalars[base + 3 + places + place]
        pl.when(is_long == 1)(lambda: attend(place, LONG))
        pl.when(is_long == 0)(lambda: attend(place, SHORT))
        return carry

    lax.fori_loop(0, places, one_place, 0)
    branch_ref[...] = bf_dot(attended_ref[...], weight_ref[...])


def attend(base, scalars, rows, weight, count):
    own_width, width = weight.shape
    return kernel_call(
        lambda *refs: attend_body(base, *refs),
        "attend",
        [array((count, own_width), BF16), array((count, width), F32)],
        [scalars, rows, weight],
        2 * count * own_width * (width + 2 * LONG),
        far=(2,),
        in_specs=[SMEM, VMEM, VMEM],
        scratch=[
            pltpu.VMEM((3 * count, own_width), BF16),
            pltpu.VMEM((3 * count, own_width), BF16),
            pltpu.VMEM((own_width, SHORT), F32),
        ],
    )


def attend_back_body(base, scalars, rows_ref, grad_ref, near_grad_ref, weight_ref, *rest):
    hidden_grad_ref, bias_ref, pieces = rest[0], rest[1], rest[2:-3]
    held, grads, split = rest[-3:]
    count, own_width = grad_ref.shape
    places = count // SHORT
    table = [scalars[base + number] for number in range(3)]
    for number in range(3):
        lay_beside(held.at[number], rows_ref[number, :count], rows_ref[number, count:], table)
    lay_beside(held.at[3], grad_ref[...], near_grad_ref[...], table)

    def attend_back(first, size):
        rows = pl.ds(aligned(first * SHORT, SHORT), size)
        for head in range(own_width // HEAD_DIM):
            columns = pl.ds(head * HEAD_DIM, HEAD_DIM)
            query, key, value, grad = (held[number, rows, columns] for number in range(4))
            scores = dot_by(ROWS_BY_ROWS, key, query)
            peak = jnp.max(scores, axis=0, keepdims=True)
            exponent = jnp.exp2((scores - peak) * FACTOR_LOG2)
            probs = exponent * (1.0 / jnp.sum(exponent, axis=0, keepdims=True))
            probs_grad = dot_by(ROWS_BY_ROWS, value, grad)
            row_dot = jnp.sum(probs * probs_grad, axis=0, keepdims=True)
            score_grad = (probs * (probs_grad - row_dot)).astype(BF16)
            query_grad = dot_by(COLUMNS_BY_COLUMNS, score_grad, key) * FACTOR
            grads[0, rows, columns] = query_grad.astype(BF16)
            grads[1, rows, columns] = (bf_dot(score_grad, query) * FACTOR).astype(BF16)
            grads[2, rows, columns] = bf_dot(probs.astype(BF16), grad).astype(BF16)

    def short_latent(place, carry):
        is_long = scalars[base + 3 + places + place]
        pl.when(is_long == 0)(lambda: attend_back(places + place, SHORT))
        return carry

    lax.fori_loop(0, places, short_latent, 0)

    def long_latent(number, carry):
        first = scalars[base + 1 + number]
        pl.when(first >= 0)(lambda: attend_back(first, LONG))
        return carry

    lax.fori_loop(0, 2, long_latent, 0)
    own_grads = [grads[number, count : 2 * count] for number in range(3)]
    total = bf_dot(own_grads[0], weight_ref[0])
    for number in range(1, 3):
        total = total + bf_dot(own_grads[number], weight_ref[number])
    hidden_grad_ref[...] = total.astype(BF16)
    for number, grad in enumerate((own_grads[0], own_grads[2])):
        bias_ref[number : number + 1] = jnp.sum(grad.astype(F32), axis=0, keepdims=True)
    share = own_width // len(pieces)
    for number in range(len(pieces)):
        for part in range(3):
            split[number, :, part * share : (part + 1) * share] = own_grads[part][
                :, number * share : (number + 1) * share
            ]
    for entry, piece in enumerate(pieces):
        piece[...] = split[jnp.bitwise_xor(scalars[base - 1], entry)]


def attend_back(base, scalars, rows, grad, near_grad, weight, packs):
    count, own_width = grad.shape
    width = weight.shape[2]
    share = 3 * own_width // packs
    outs = kernel_call(
        lambda *refs: attend_back_body(base, *refs),
        "attend_back",
        [array((count, width), BF16), array((2, own_width), F32)]
        + [array((count, share), BF16)] * packs,
        [scalars, rows, grad, near_grad, weight],
        6 * count * own_width * width + 10 * own_width * LONG * LONG,
        far=(4,),
        in_specs=[SMEM] + [VMEM] * 4,
        scratch=[
            pltpu.VMEM((4, 3 * count, own_width), BF16),
            pltpu.VMEM((3, 3 * count, own_width), BF16),
            pltpu.VMEM((packs, count, share), BF16),
        ],
    )
    return outs[0], outs[1], list(outs[2:])


def whole(shape):
    return pl.BlockSpec(shape, lambda i: (0,) * len(shape))


def feed_up_body(scalars, kept_ref, term_ref, other_ref, bias_ref, mod_ref, *rest):
    weight_ref, hidden_bias_ref, branch_ref, hidden_ref, share_ref, slope_ref = rest[:6]
    gelu_ref, pieces = rest[6], rest[7:]
    step = pl.program_id(0)
    size = weight_ref.shape[1]

    @pl.when(step == 0)
    def _():
        def place(number, carry):
            rows = pl.ds(aligned(number * SHORT, SHORT), SHORT)
            branch = (term_ref[rows] + other_ref[rows]) + bias_ref[...]
            branch_ref[rows] = branch
            middle = kept_ref[rows].astype(F32) + mod_ref[number, 2:3] * branch
            normed, _ = layer_norm(middle)
            shift, scale = mod_ref[number, 3:4], mod_ref[number, 4:5]
            hidden_ref[rows] = (normed * (1.0 + scale) + shift).astype(BF16)
            return carry

        lax.fori_loop(0, kept_ref.shape[0] // SHORT, place, 0)
        start = aligned(scalars[0] * (hidden_ref.shape[1] - share_ref.shape[1]))
        share_ref[...] = hidden_ref[:, pl.ds(start, share_ref.shape[1])]

    gelu, slope = gelu_pair(bf_dot(hidden_ref[...], weight_ref[...]) + hidden_bias_ref[...])
    slope_ref[...] = slope
    gelu_ref[:, pl.ds(aligned(step * size), size)] = gelu.astype(BF16)

    @pl.when(step == pl.num_programs(0) - 1)
    def _():
        for entry, piece in enumerate(pieces):
            piece[...] = gelu_ref[:, pl.ds(aligned(scalars[2 + entry]), piece.shape[1])]


def feed_up(scalars, kept, term, other, bias, mod_places, weight, hidden_bias, packs):
    count, width = kept.shape
    hidden = weight.shape[1]
    size = hidden // 3
    window = windows(hidden, packs)[1]
    outs = [
        array((count, width), F32),
        array((count, width), BF16),
        array((count, half_width(width)), BF16),
        array((count, hidden), F32),
        array((count, hidden), BF16),
    ] + [array((count, window), BF16)] * packs
    out_specs = [whole(out.shape) for out in outs]
    out_specs[3] = pl.BlockSpec((count, size), lambda i: (0, i))
    result = kernel_call(
        feed_up_body,
        "feed_up",
        outs,
        [scalars, kept, term, other, bias, mod_places, weight, hidden_bias],
        2 * count * width * hidden,
        far=(6,),
        grid=(hidden // size,),
        in_specs=[
            SMEM,
            *[whole(a.shape) for a in (kept, term, other, bias, mod_places)],
            pl.BlockSpec((width, size), lambda i: (0, i)),
            pl.BlockSpec((1, size), lambda i: (0, i)),
        ],
        out_specs=tuple(out_specs),
    )
    return *result[:5], list(result[5:])


def feed_back_body(scalars, down_in_ref, down_ref, slope_ref, weight_ref, *rest):
    back_ref, sums_ref, pieces, pre_rows = rest[0], rest[1], rest[2:-1], rest[-1]
    step = pl.program_id(0)
    size = weight_ref.shape[1]
    pre_grad = dot_by(ROWS_BY_ROWS, down_in_ref[...], down_ref[...]) * slope_ref[...]
    pre_grad = pre_grad.astype(BF16)
    pre_rows[:, pl.ds(aligned(step * size), size)] = pre_grad
    sums_ref[...] = jnp.sum(pre_grad.astype(F32), axis=0, keepdims=True)
    back = dot_by(ROWS_BY_ROWS, pre_grad, weight_ref[...])

    @pl.when(step == 0)
    def _():
        back_ref[...] = back

    @pl.when(step > 0)
    def _():
        back_ref[...] += back

    @pl.when(step == pl.num_programs(0) - 1)
    def _():
        for entry, piece in enumerate(pieces):
            piece[...] = pre_rows[:, pl.ds(aligned(scalars[2 + entry]), piece.shape[1])]


def feed_back(scalars, down_in, down, slope, weight, packs):
    count, width = down_in.shape
    hidden = weight.shape[1]
    size = hidden // 3
    window = windows(hidden, packs)[1]
    outs = [array((count, width), F32), array((1, hidden), F32)]
    outs += [array((count, window), BF16)] * packs
    out_specs = [whole(out.shape) for out in outs]
    out_specs[1] = pl.BlockSpec((1, size), lambda i: (0, i))
    result = kernel_call(
        feed_back_body,
        "feed_back",
        outs,
        [scalars, down_in, down, slope, weight],
        4 * count * width * hidden,
        far=(2, 4),
        grid=(hidden // size,),
        in_specs=[
            SMEM,
            whole(down_in.shape),
            pl.BlockSpec((size, width), lambda i: (i, 0)),
            pl.BlockSpec((count, size), lambda i: (0, i)),
            pl.BlockSpec((width, size), lambda i: (0, i)),
        ],
        out_specs=tuple(out_specs),
        scratch=[pltpu.VMEM((count, hidden), BF16)],
    )
    return result[0], result[1], list(result[2:])


def middle_back_body(term_ref, other_ref, branch_ref, kept_ref, up_ref, mod_ref, *rest):
    weight_ref, middle_grad_ref, branch_grad_ref, attended_ref, sums_ref, bias_ref = rest
    hidden_grad = term_ref[...] + other_ref[...]
    branch = branch_ref[...]
    gate = mod_ref[0, 2:3]
    normed, inverse = layer_norm(kept_ref[...].astype(F32) + gate * branch)
    middle_grad = up_ref[...].astype(F32) + norm_back(
        hidden_grad * (1.0 + mod_ref[0, 4:5]), normed, inverse
    )
    middle_grad_ref[...] = middle_grad
    branch_grad = (gate * middle_grad).astype(BF16)
    branch_grad_ref[...] = branch_grad
    attended_ref[...] = dot_by(ROWS_BY_ROWS, branch_grad, weight_ref[...]).astype(BF16)
    bias_ref[0] = jnp.sum(branch_grad.astype(F32), axis=0, keepdims=True)
    sums_ref[0, 0:1] = jnp.sum(middle_grad * branch, axis=0, keepdims=True)
    sums_ref[0, 1:2] = jnp.sum(hidden_grad, axis=0, keepdims=True)
    sums_ref[0, 2:3] = jnp.sum(hidden_grad * normed, axis=0, keepdims=True)


def by_place(body, name, outs, args, flops, far=()):
    places = args[0].shape[0] // SHORT

    def spec(a):
        if a.shape[0] == places * SHORT and len(a.shape) == 2:
            return pl.BlockSpec((SHORT, a.shape[1]), lambda i: (i, 0))
        if a.shape[0] == places and len(a.shape) == 3:
            return pl.BlockSpec((1, *a.shape[1:]), lambda i: (i, 0, 0))
        return pl.BlockSpec(a.shape, lambda i: (0,) * len(a.shape))

    return kernel_call(
        body,
        name,
        outs,
        args,
        flops,
        far=far,
        grid=(places,),
        in_specs=[spec(a) for a in args],
        out_specs=tuple(spec(a) for a in outs),
    )


def middle_back(term, other, branch, kept, upstream, mod_places, weight):
    count, width = kept.shape
    places = count // SHORT
    return by_place(
        middle_back_body,
        "middle_back",
        [
            array((count, width), F32),
            array((count, width), BF16),
            array((count, weight.shape[0]), BF16),
            array((places, 3, width), F32),
            array((places, 1, width), F32),
        ],
        [term, other, branch, kept, upstream, mod_places, weight],
        2 * count * width * weight.shape[0],
        far=(6,),
    )


def input_back_body(term_ref, other_ref, middle_grad_ref, kept_ref, mod_ref, grad_ref, sums_ref):
    hidden_grad = term_ref[...].astype(F32) + other_ref[...].astype(F32)
    normed, inverse = layer_norm(kept_ref[...].astype(F32))
    grad = middle_grad_ref[...] + norm_back(hidden_grad * (1.0 + mod_ref[0, 1:2]), normed, inverse)
    grad_ref[...] = grad.astype(BF16)
    sums_ref[0, 0:1] = jnp.sum(hidden_grad, axis=0, keepdims=True)
    sums_ref[0, 1:2] = jnp.sum(hidden_grad * normed, axis=0, keepdims=True)


def input_back(term, other, middle_grad, kept, mod_places):
    count, width = kept.shape
    return by_place(
        input_back_body,
        "input_back",
        [array((count, width), BF16), array((count // SHORT, 2, width), F32)],
        [term, other, middle_grad, kept, mod_places],
        0,
    )


def result_body(term_ref, other_ref, bias_ref, branch_ref, kept_ref, up_ref, mod_ref, *rest):
    result_ref, sums_ref, bias_grad_ref = rest
    branch_two = term_ref[...].astype(F32) + other_ref[...].astype(F32) + bias_ref[...]
    middle = kept_ref[...].astype(F32) + mod_ref[0, 2:3] * branch_ref[...]
    gate = mod_ref[0, 5:6]
    upstream = up_ref[...].astype(F32)
    result_ref[...] = (middle + gate * branch_two).astype(BF16)
    sums_ref[0, 0:1] = jnp.sum(upstream * branch_two, axis=0, keepdims=True)
    down_in = (gate * upstream).astype(BF16).astype(F32)
    bias_grad_ref[0] = jnp.sum(down_in, axis=0, keepdims=True)


def result(term, other, bias, branch, kept, upstream, mod_places):
    count, width = kept.shape
    places = count // SHORT
    return by_place(
        result_body,
        "result",
        [
            array((count, width), BF16),
            array((places, 1, width), F32),
            array((places, 1, width), F32),
        ],
        [term, other, bias, branch, kept, upstream, mod_places],
        0,
    )


def weight_grad_body(packs, offset, count_shares, scalars, *refs):
    shares, refs = refs[:count_shares], refs[count_shares:]
    columns, refs = refs[:packs], refs[packs:]
    outs, (rows_all, columns_all, total) = refs[:-3], refs[-3:]
    count, wide = columns[0].shape
    width = rows_all.shape[1]
    half = half_width(width)
    for entry in range(packs):
        rows = pl.ds(entry * count, count)
        columns_all[rows] = columns[entry][...]
        if count_shares == 1:
            source = jnp.bitwise_xor(scalars[2 + packs], entry) * (2 * count)
            low = pl.ds(aligned(source, SHORT), count)
            high = pl.ds(aligned(source + count, SHORT), count)
            rows_all[rows, :half] = shares[0][low, offset : offset + half]
            rows_all[rows, half:] = shares[0][high, offset + 2 * half - width : offset + half]
        elif entry == 0:
            rows_all[rows] = shares[0][:count]
        else:
            rows_all[rows] = shares[1][(entry - 1) * count : entry * count]
    if len(outs) == 1:
        outs[0][...] = dot_by(COLUMNS_BY_COLUMNS, rows_all[...], columns_all[...]).astype(BF16)
        return
    total[:, :wide] = dot_by(COLUMNS_BY_COLUMNS, rows_all[...], columns_all[...])
    if total.shape[1] > wide:
        others, outs = outs[:packs], outs[packs:]
        other = others[0][...].astype(F32)
        for entry in range(1, packs):
            other = other + others[entry][...].astype(F32)
        total[:, wide:] = other.T
    cut_by_blk(scalars, total, outs)


def cut_by_blk(scalars, total, outs):
    blocks = len(outs)
    size = total.shape[0] // blocks
    for step in range(blocks):
        target = lax.rem(scalars[1] + step, blocks)
        piece = total[pl.ds(aligned(target * size, 8), size)]
        outs[step][...] = piece.astype(outs[step].dtype)


def cut_shapes(width, wide, blocks):
    size = width // blocks
    return [array((size, wide), F32)] + [array((size, wide), BF16)] * (blocks - 1)


def weight_grad(scalars, width, offset, shares, columns, others=(), blocks=1):
    packs = len(columns)
    count, wide = columns[0].shape
    total = wide + (others[0].shape[0] if others else 0)
    outs = [array((width, wide), BF16)]
    if blocks > 1:
        outs = cut_shapes(width, total, blocks)
    return kernel_call(
        lambda *refs: weight_grad_body(packs, offset, len(shares), *refs),
        "weight_grad",
        outs,
        [scalars, *shares, *columns, *others],
        2 * packs * count * width * wide,
        in_specs=[SMEM] + [VMEM] * (packs + len(shares) + len(others)),
        scratch=[
            pltpu.VMEM((packs * count, width), BF16),
            pltpu.VMEM((packs * count, wide), BF16),
            pltpu.VMEM((width, total), F32),
        ],
    )


def own_weight_grad_body(packs, scalars, rows_ref, columns_ref, *refs):
    pieces, total = refs[:-1], refs[-1]
    total[...] = dot_by(COLUMNS_BY_COLUMNS, rows_ref[...], columns_ref[...])
    size = total.shape[0] // packs
    for entry, piece in enumerate(pieces):
        start = jnp.bitwise_xor(scalars[2 + packs], entry) * size
        piece[...] = total[pl.ds(aligned(start, 8), size)].astype(BF16)


def own_weight_grad(scalars, rows, columns, packs):
    shape = (rows.shape[1], columns.shape[1])
    return kernel_call(
        lambda *refs: own_weight_grad_body(packs, *refs),
        "own_weight_grad",
        [array((shape[0] // packs, shape[1]), BF16)] * packs,
        [scalars, rows, columns],
        2 * rows.shape[0] * math.prod(shape),
        in_specs=[SMEM, VMEM, VMEM],
        scratch=[pltpu.VMEM(shape, F32)],
    )


def join_body(kind, starts, packs, scalars, *refs):
    outs, held = refs[1:-1], refs[-1]
    size = refs[0].shape[0] // packs
    stacked = kind == "hidden"
    if not stacked:
        entries, outs = refs[:packs], refs[packs:-1]
        for entry in range(packs):
            held[entry] = entries[entry][...]
    for number in range(packs):
        if stacked:
            piece = refs[0][number * size : (number + 1) * size].astype(F32)
        else:
            piece = held[jnp.bitwise_xor(scalars[2 + packs], number)].astype(F32)
        if kind == "qkv":
            share = piece.shape[1] // 4
            columns = pl.ds(number * share, share)
            for part in range(3):
                outs[0][part, :, columns] = piece[:, part * share : (part + 1) * share]
            outs[1][:, columns] = piece[:, 3 * share :]
        else:
            end = [*starts[1:], outs[0].shape[1]][number]
            outs[0][:, starts[number] : end] = piece[:, : end - starts[number]]


def join(kind, scalars, entries, packs, shapes, starts=()):
    return kernel_call(
        lambda *refs: join_body(kind, starts, packs, *refs),
        "join_" + kind,
        [array(shape, F32) for shape in shapes],
        [scalars, *entries],
        0,
        in_specs=[SMEM] + [VMEM] * len(entries),
        scratch=[pltpu.VMEM((packs, *entries[0].shape), BF16)],
    )


def collect_body(scalars, input_ref, middle_ref, two_ref, active_ref, *refs):
    qkv_ref, output_ref, hidden_ref, down_ref, out_ref, held = refs
    places, _, width = middle_ref.shape
    half = width // 2
    row = 0

    def put(value):
        nonlocal row
        held[row : row + 1] = value
        row += 1

    def put_twice(value):
        high = value.astype(BF16).astype(F32)
        put(high)
        put(value - high)

    def put_sums(start):
        nonlocal row
        row = 0
        for place in range(places):
            for source in (input_ref, middle_ref, two_ref):
                for number in range(source.shape[1]):
                    put(source[place, number : number + 1, start : start + half])

    held[...] = jnp.zeros_like(held)
    pl.when(scalars[0] == 0)(lambda: put_sums(0))
    pl.when(scalars[0] == 1)(lambda: put_sums(half))
    for place in range(places):
        active = active_ref[place : place + 1].astype(F32)
        put(active[:, :half])
        put(active[:, half:])
    put_twice(qkv_ref[0:1])
    put_twice(qkv_ref[1:2])
    for number in range(hidden_ref.shape[1] // half):
        put_twice(hidden_ref[:, number * half : (number + 1) * half])
    for source in (output_ref, down_ref):
        total = jnp.sum(source[...], axis=0)
        put_twice(total[:, :half])
        put_twice(total[:, half:])
    out_ref[...] = held[...].astype(BF16)


def collect(scalars, *args):
    places, _, width = args[0].shape
    hidden = args[6].shape[1]
    used = places * 8 + 2 * (2 + 2 * hidden // width + 4)
    size = -(-used // 16) * 16
    return kernel_call(
        collect_body,
        "collect",
        [array((size, width // 2), BF16)],
        [scalars, *args],
        0,
        in_specs=[SMEM] + [VMEM] * len(args),
        scratch=[pltpu.VMEM((size, width // 2), F32)],
    )[0]


def spread_body(packs, blocks, places, size, scalars, segments, *refs):
    entries = refs[:packs]
    weight_ref, bias_ref, biases_ref, grad_ref, held, rows_all, active, sums = refs[packs:]
    half = weight_ref.shape[2]
    rows = weight_ref.shape[1]
    pack = scalars[2 + packs]
    for entry in range(packs):
        held[entry] = entries[entry][...].reshape(blocks, size, half)
    for number in range(packs):
        for block in range(blocks):
            piece = held[jnp.bitwise_xor(pack, number), jnp.bitwise_xor(scalars[1], block)]
            rows_all[number * blocks + block] = piece.astype(F32)
    cut = 6 * places
    devices = packs * blocks

    def take_active(block):
        start = block * rows
        for device in range(devices):
            for place in range(places):
                row = cut + 2 * place
                whole_row = jnp.concatenate(
                    [rows_all[device, row : row + 1], rows_all[device, row + 1 : row + 2]], axis=1
                )
                number = device * places + place
                active[number : number + 1] = whole_row[:, start : start + rows]

    for block in range(blocks):
        pl.when(scalars[1] == block)(lambda: take_active(block))
    own_active = active[...].astype(BF16)
    for group in range(6):
        for device in range(devices):
            for place in range(places):
                number = device * places + place
                row = place * 6 + group
                sums[number : number + 1] = rows_all[device, row : row + 1]
        values = sums[...]
        bias_ref[group : group + 1] = jnp.sum(values, axis=0, keepdims=True)
        weight_ref[group] = dot_by(COLUMNS_BY_COLUMNS, own_active, values.astype(BF16))
    first = cut + 2 * places
    total = rows_all[0, first:]
    for device in range(1, devices):
        total = total + rows_all[device, first:]
    biases_ref[...] = total
    grad_ref[...] = jnp.zeros_like(grad_ref)
    for block in range(blocks):
        for place in range(places):
            segment = segments[(block * places + place) * SHORT]
            own = rows_all[pack * blocks + block, place * 6 : place * 6 + 6]
            grad_ref[segment] = grad_ref[segment] + own


def spread(scalars, segments, entries, packs, blocks, places, seg_count, width):
    devices = packs * blocks
    size = entries[0].shape[0] // blocks
    half = entries[0].shape[1]
    return kernel_call(
        lambda *refs: spread_body(packs, blocks, places, size, *refs),
        "spread",
        [
            array((6, width // blocks, half), F32),
            array((6, half), F32),
            array((size - 8 * places, half), F32),
            array((seg_count, 6, half), F32),
        ],
        [scalars, segments, *entries],
        0,
        in_specs=[SMEM, SMEM] + [VMEM] * packs,
        scratch=[
            pltpu.VMEM((packs, blocks, size, half), BF16),
            pltpu.VMEM((devices, size, half), F32),
            pltpu.VMEM((devices * places, width // blocks), F32),
            pltpu.VMEM((devices * places, half), F32),
        ],
    )


def xor_permute(block, axis, bits):
    return lax.ppermute(block, axis, [(i, i ^ bits) for i in range(lax.axis_size(axis))])


def swap(block):
    return xor_permute(block, "head", 1)


def move(block, step):
    count = lax.axis_size("blk")
    pairs = [(i, i + step) for i in range(count) if 0 <= i + step < count]
    return lax.ppermute(block, "blk", pairs)


def gather_xor(block, axis, turned=False):
    bits = [1 << b for b in range((lax.axis_size(axis) - 1).bit_length())]
    held = {0: block}
    for bit in bits[::-1] if turned else bits:
        for entry in list(held):
            held[entry ^ bit] = xor_permute(held[entry], axis, bit)
    return [held[entry] for entry in range(lax.axis_size(axis))]


def gather_each(block, axis):
    return [block] + [xor_permute(block, axis, r) for r in range(1, lax.axis_size(axis))]


def trade(pieces, axis, entries):
    return {r: xor_permute(pieces[r], axis, r) for r in entries}


def windows(width, parts):
    tiles = width // LANES
    size = -(-tiles // parts)
    return [LANES * (q * (tiles - size) // (parts - 1)) for q in range(parts)], size * LANES


def half_width(width):
    return -(-width // (2 * LANES)) * LANES


def gather_shares(share):
    return lax.all_gather(share, ("pack", "head"), axis=0, tiled=True)


def hold(values, *after):
    flat, tree = jax.tree.flatten(values)
    held = lax.optimization_barrier((*flat, *after))
    return jax.tree.unflatten(tree, held[: len(flat)])


def send_blk(pieces):
    count = len(pieces)
    found = [pieces[0]]
    for step in range(1, count):
        pairs = [(i, (i + step) % count) for i in range(count)]
        found.append(lax.ppermute(pieces[step], "blk", pairs))
    return found


def add_blk(found):
    total = found[0]
    for piece in found[1:]:
        total = total + piece.astype(F32)
    return total.astype(BF16)


def local(
    tokens_full,
    condition,
    kept_index,
    segment_ids,
    cotangent,
    qkv_weight,
    query_value_bias,
    output_weight,
    output_bias,
    hidden_weight,
    hidden_bias,
    down_weight,
    down_bias,
    modulation_weight,
    modulation_bias,
):
    width = tokens_full.shape[2]
    own_width = qkv_weight.shape[2]
    hidden = hidden_weight.shape[1]
    count = kept_index.shape[1]
    seg_count = condition.shape[1]
    places = count // SHORT
    longs = (segment_ids.shape[1] - SHORT * seg_count) // (LONG - SHORT)
    packs = lax.axis_size("pack")
    blocks = lax.axis_size("blk")
    blk = lax.axis_index("blk")
    core = lax.axis_index("head")
    pack = lax.axis_index("pack")

    modulation_turned = jnp.transpose(modulation_weight, (1, 2, 0))
    starts, window = windows(hidden, packs)
    place = jnp.stack([core, blk, pack, jnp.int32(blocks)]).astype(jnp.int32)
    scalars = plan(longs, packs, starts, place, segment_ids[0])
    base = 3 + packs
    own_active, near_active = latents(
        scalars, base + 3 + 2 * places, condition[0], places, places if longs == 1 else 2 * places
    )
    local_index, own_active = hold((kept_index[0] - blk * (2 * count), own_active))
    full_rows = tokens_full[0]
    cot_rows = cotangent[0]
    picker = (
        local_index[:, None] == jnp.arange(full_rows.shape[0], dtype=jnp.int32)[None, :]
    ).astype(BF16)
    kept_rows = bf_dot(picker, full_rows).astype(BF16)
    upstream = bf_dot(picker, cot_rows).astype(BF16)

    reaches_low = scalars[-1] == 1

    def beside(block):
        low, high = move(block, 1), move(block, -1)
        if longs == 1:
            return jnp.where(reaches_low, low, high)
        return jnp.concatenate([low, high], axis=0)

    half = count // 2
    kept_half = lax.dynamic_slice_in_dim(kept_rows, core * half, half, 0)
    near_half = beside(kept_half)
    token_shares = gather_shares(
        jnp.concatenate(
            [kept_half, lax.dynamic_slice_in_dim(upstream, core * half, half, 0)], axis=0
        )
    )
    other_half = swap(near_half)
    first = jnp.where(core == 0, near_half, other_half).reshape(-1, half, width)
    second = jnp.where(core == 0, other_half, near_half).reshape(-1, half, width)
    near_rows = jnp.concatenate([first, second], axis=1).reshape(-1, width)

    near_count = near_rows.shape[0] // SHORT
    other_active = list(trade([own_active] * packs, "pack", range(1, packs)).values())
    mod_own = (
        jnp.einsum(
            "sd,gfd->sgf",
            jnp.concatenate([own_active, near_active, *other_active], axis=0),
            modulation_turned,
            preferred_element_type=F32,
        )
        + modulation_bias.astype(F32)[None]
    )
    mod_all = pick(scalars, mod_own, swap(mod_own))
    mod_places = mod_all[:places]
    wide_bias = query_value_bias.astype(F32)
    qkv_bias = jnp.stack([wide_bias[0], jnp.zeros_like(wide_bias[0]), wide_bias[1]])[:, None]
    hidden_rows, down_in = norm(kept_rows, near_rows, upstream, mod_all)
    qkv_turned = jnp.transpose(qkv_weight, (1, 2, 0))
    projected = jnp.einsum("td,gfd->gtf", hidden_rows, qkv_turned, preferred_element_type=F32)
    qkv_rows = (projected + qkv_bias).astype(BF16)

    attended, branch_term = attend(base, scalars, qkv_rows, output_weight, count)
    branch_one, hidden_two, hidden_two_share, slope, gelu, gelu_pieces = feed_up(
        scalars,
        kept_rows,
        branch_term,
        swap(branch_term),
        output_bias.astype(F32)[None],
        mod_places,
        hidden_weight,
        hidden_bias.astype(F32)[None],
        packs,
    )
    one_step = [r for r in range(1, packs) if r & (r - 1) == 0]
    further = [r for r in range(1, packs) if r & (r - 1)]

    def by_entry(pieces, *parts):
        found = {0: pieces[0]}
        for part in parts:
            found.update(part)
        return [found[r] for r in range(packs)]

    hidden_two_shares = gather_shares(hidden_two_share)
    gelu_first = trade(gelu_pieces, "pack", one_step)
    back_term, hidden_sums, pre_pieces = feed_back(
        scalars, down_in, down_weight, slope, hidden_weight, packs
    )
    back_term, gelu_first, gelu_pieces, pre_pieces = hold(
        (back_term, gelu_first, gelu_pieces, pre_pieces)
    )
    gelu_last = trade(gelu_pieces, "pack", further)
    hidden_other_packs, down_other_packs = others(
        scalars, token_shares, mod_all, places + near_count, packs, count
    )
    back_other, hidden_other_packs, down_other_packs = hold(
        (swap(back_term), hidden_other_packs, down_other_packs)
    )
    middle_grad, branch_grad, attended_grad, middle_sums, output_sums = middle_back(
        back_term, back_other, branch_one, kept_rows, upstream, mod_places, output_weight
    )
    attended_grad, pre_pieces, gelu, branch_grad = hold(
        (attended_grad, pre_pieces, gelu, branch_grad)
    )
    near_grad = beside(attended_grad)
    rows = width // blocks

    pre_first = trade(pre_pieces, "pack", one_step)
    gelu_all = by_entry(gelu_pieces, gelu_first, gelu_last)
    down_raw = weight_grad(scalars, width, 0, [down_in, down_other_packs], gelu_all)[0]
    output_pieces = own_weight_grad(scalars, attended, branch_grad, packs)
    pre_last = trade(pre_pieces, "pack", further)
    near_grad, down_raw, output_pieces, pre_first = hold(
        (near_grad, down_raw, output_pieces, pre_first)
    )
    down_term = lax.psum_scatter(down_raw, "blk", scatter_dimension=0, tiled=True)
    output_first = trade(output_pieces, "pack", one_step)
    hidden_term, qkv_sums, qkv_pieces = attend_back(
        base, scalars, qkv_rows, attended_grad, near_grad, qkv_turned, packs
    )
    hidden_term, qkv_pieces, output_first, output_pieces, gelu, pre_last = hold(
        (hidden_term, qkv_pieces, output_first, output_pieces, gelu, pre_last)
    )
    qkv_first = trade(qkv_pieces, "pack", one_step)
    qkv_last = trade(qkv_pieces, "pack", further)
    output_last = trade(output_pieces, "pack", further)

    pre_all = by_entry(pre_pieces, pre_first, pre_last)
    hidden_raw = weight_grad(scalars, width, 0, [hidden_two_shares], pre_all)[0]
    hidden_reduced = lax.psum_scatter(hidden_raw, "blk", scatter_dimension=0, tiled=True)
    hidden_other, qkv_first, output_last, hidden_raw = hold(
        (swap(hidden_term), qkv_first, output_last, hidden_raw)
    )
    input_grad, input_sums = input_back(
        hidden_term, hidden_other, middle_grad, kept_rows, mod_places
    )
    two_term = bf_dot(gelu, down_weight).astype(BF16)
    result_rows, two_sums, down_sums = result(
        two_term,
        swap(two_term),
        down_bias.astype(F32)[None],
        branch_one,
        kept_rows,
        upstream,
        mod_places,
    )
    sent = collect(
        scalars,
        input_sums,
        middle_sums,
        two_sums,
        own_active,
        qkv_sums,
        output_sums,
        hidden_sums,
        down_sums,
    )
    qkv_last, sent = hold((qkv_last, sent))
    by_blk = gather_each(sent, "blk")
    qkv_terms = weight_grad(
        scalars,
        width,
        0,
        [hidden_rows, hidden_other_packs],
        by_entry(qkv_pieces, qkv_first, qkv_last),
        by_entry(output_pieces, output_first, output_last),
        blocks,
    )
    qkv_terms, by_blk, result_rows, input_grad, down_term = hold(
        (qkv_terms, by_blk, result_rows, input_grad, down_term)
    )

    def put_rows(base, rows):
        spread = dot_by(COLUMNS_BY_COLUMNS, picker, rows)
        kept = jnp.max(picker, axis=0)[:, None] > 0
        return jnp.where(kept, spread.astype(BF16), base)[None]

    qkv_found = send_blk(qkv_terms)
    entries = gather_each(jnp.concatenate(by_blk, axis=0), "pack")
    down_entries = gather_each(down_term, "pack")
    block_output = put_rows(full_rows, result_rows)
    tokens_grad = put_rows(cot_rows, input_grad)
    qkv_found, entries, block_output, tokens_grad, down_entries = hold(
        (qkv_found, entries, block_output, tokens_grad, down_entries)
    )
    qkv_entries = gather_each(add_blk(qkv_found), "pack")
    hidden_gathered = lax.all_gather(hidden_reduced, "pack", axis=0, tiled=True)
    modulation_weight_grad, modulation_bias_grad, biases, mod_grad = spread(
        scalars, segment_ids[0], entries, packs, blocks, places, seg_count, width
    )
    qkv_weight_grad, output_weight_grad = join(
        "qkv", scalars, qkv_entries, packs, [(3, rows, own_width), (rows, own_width)]
    )
    down_weight_grad = join(
        "down",
        scalars,
        down_entries,
        packs,
        [(rows, hidden)],
        starts,
    )[0].T
    hidden_weight_grad = join(
        "hidden", scalars, [hidden_gathered], packs, [(rows, hidden)], starts
    )[0]
    output_weight_grad = output_weight_grad.T
    qkv_weight_grad = jnp.swapaxes(qkv_weight_grad, 0, 1)
    modulation_weight_grad = jnp.swapaxes(modulation_weight_grad, 0, 1)
    mod_high = mod_grad.astype(BF16)
    mod_low = (mod_grad - mod_high.astype(F32)).astype(BF16)
    cond_terms = jnp.einsum(
        "sgf,gfd->sd",
        jnp.concatenate([mod_high, mod_low], axis=0),
        modulation_turned,
        preferred_element_type=F32,
    )
    cond_term = cond_terms[:seg_count] + cond_terms[seg_count:]
    cond_total = cond_term + swap(cond_term)
    cond_rows = condition[0].astype(F32)
    squashed = jax.nn.sigmoid(cond_rows)
    condition_grad = (cond_total * squashed * (1.0 + cond_rows * (1.0 - squashed)))[None]

    def bias_rows(first, number):
        pairs = biases[2 * first : 2 * (first + number)].reshape(number, 2, own_width)
        return (pairs[:, 0] + pairs[:, 1]).reshape(-1)

    value_bias = bias_rows(0, 2).reshape(2, own_width)
    hidden_rows_count = hidden // own_width
    return (
        block_output,
        tokens_grad,
        condition_grad,
        qkv_weight_grad,
        value_bias,
        output_weight_grad,
        bias_rows(2 + hidden_rows_count, 2),
        hidden_weight_grad,
        bias_rows(2, hidden_rows_count),
        down_weight_grad,
        bias_rows(4 + hidden_rows_count, 2),
        modulation_weight_grad,
        modulation_bias_grad,
    )


def solution(mesh):
    in_specs = (
        P("pack", "blk", None),
        P("pack", None, None),
        P("pack", "blk"),
        P("pack", None),
        P("pack", "blk", None),
        P(None, None, "head"),
        P(None, "head"),
        P("head", None),
        P(),
        P(None, "head"),
        P("head"),
        P("head", None),
        P(),
        P(None, None, "head"),
        P(None, "head"),
    )
    out_specs = (
        P("pack", "blk", None),
        P("pack", "blk", None),
        P("pack", None, None),
        P("blk", None, "head"),
        P(None, "head"),
        P("head", "blk"),
        P(),
        P("blk", "head"),
        P("head"),
        P("head", "blk"),
        P(),
        P("blk", None, "head"),
        P(None, "head"),
    )
    return jax.shard_map(local, mesh=mesh, in_specs=in_specs, out_specs=out_specs, check_vma=False)
```
